512 devices in a mesh: row: 16 (over z), col: 32 (over x, y, core).
Axes of the slice: x: 4, y: 4, z: 16, core: 2. Of those that a mesh axis runs over, the one named last changes fastest.
Arguments:
- magnet: float32 [3, 2048, 2048], P(None, 'col', 'row'), may hold values from -1 to 1, as said below
- stiffness: float32 [2048, 2048], P('col', 'row'), may hold values from 0.5 to 2
- kern: float32 [6, 2048, 4096], P(None, ('row', 'col')), may hold values from -8 to 8
Outputs:
- torque: float32 [3, 2048, 2048], P(None, 'col', 'row')
The draws below stay inside these ranges and needn't reach their ends.
Inputs may be any that keep to these rules, and one draw needn't show every extreme that they name: `magnet`: each cell's three components form a unit vector.
All inputs are finite; a program needn't handle non-finite values.
Results may differ from the reference program's by a relative error of at most 0.00011.
Values sent between devices are 32-bit elements; how exact they have to be, the bound alone decides.
No kernel may reach another device: no remote copies, remote signals or barrier semaphores. Data moves between devices by JAX's collectives and lax.ppermute only.
A program may use at most 64 MiB of HBM per device.

```python
import math
import jax
import jax.numpy as jnp
from jax import lax

NX = 2048
NY = 2048
LX = 4096


def draw_magnet(key, part):
    key = jax.random.fold_in(key, 7)
    polar_key, turn_key = jax.random.split(key)
    height = jax.random.uniform(polar_key, (NX, NY), jnp.float32, -1.0, 1.0)
    azimuth = jax.random.uniform(turn_key, (NX, NY), jnp.float32, -math.pi, math.pi)
    radial = jnp.sqrt(jnp.maximum(1.0 - height * height, 0.0))
    return jnp.stack([radial * jnp.cos(azimuth), radial * jnp.sin(azimuth), height])


def block_levels(own_key, dims, cuts, low, high):
    def one(dim, shards_of):
        steps = jax.random.uniform(jax.random.fold_in(jax.random.fold_in(own_key, 6), dim), (shards_of,), jnp.float32, low / len(cuts), high / len(cuts))
        return jnp.repeat(jnp.exp(steps), dims[dim] // shards_of).reshape((-1,) + (1,) * (len(dims) - dim - 1))

    factor_of = one(*cuts[0])
    for cut in cuts[1:]:
        factor_of = factor_of * one(*cut)
    return factor_of


def gaussian(stream_key, shape, deviation, most, cuts=(), held_as=jnp.bfloat16):
    level = block_levels(stream_key, shape, cuts, -0.22, 0.18) if cuts else 1.0
    values = jax.random.normal(stream_key, shape, jnp.float32) * deviation * level
    return jnp.minimum(jnp.maximum(values, -most), most).astype(held_as)


def setup_inputs(seed: int = 0) -> dict:
    seeds = jax.random.split(jax.random.key(seed), 4)
    return {
        "magnet": draw_magnet(jax.random.fold_in(seeds[3], 71), 0),
        "stiffness": jnp.clip(jnp.exp(math.log(2.0) - 1.3862944 * jax.random.uniform(seeds[1], (NX, NY), jnp.float32) ** block_levels(seeds[1], (NX, NY), ((0, 32), (1, 16)), -0.2, 0.2)), 0.5, 2.0),
        "kern": gaussian(seeds[2], (6, NY, LX), 1.5, 8.0, ((1, 512),), jnp.float32),
    }


damping = 0.3
anisotropy = 0.8
tensor_slots = ((0, 3, 4), (3, 1, 5), (4, 5, 2))


def exchange_field(padded, start_x, start_y, total_x, total_y):
    cells_x = padded.shape[1] - 2
    cells_y = padded.shape[2] - 2
    centre = padded[:, 1:1 + cells_x, 1:1 + cells_y]
    coord_x = start_x + jnp.arange(cells_x, dtype=jnp.int32)
    coord_y = start_y + jnp.arange(cells_y, dtype=jnp.int32)
    result = jnp.zeros_like(centre[:3])
    for step_x, step_y in ((1, 0), (-1, 0), (0, 1), (0, -1)):
        beside = padded[:, 1 + step_x:1 + step_x + cells_x, 1 + step_y:1 + step_y + cells_y]
        inside_x = (coord_x + step_x >= 0) & (coord_x + step_x < total_x)
        inside_y = (coord_y + step_y >= 0) & (coord_y + step_y < total_y)
        inside = inside_x[:, None] & inside_y[None, :]
        coupling = jnp.where(inside, 0.5 * (centre[3] + beside[3]), 0.0)
        result = result + coupling[None] * (beside[:3] - centre[:3])
    return result


def cross(former, latter):
    return jnp.stack([former[1] * latter[2] - former[2] * latter[1],
                      former[2] * latter[0] - former[0] * latter[2],
                      former[0] * latter[1] - former[1] * latter[0]])


def torque_of(magnet, field):
    field = jnp.concatenate([field[:2], field[2:] + anisotropy * magnet[2:]], 0)
    first_cross = cross(magnet, field)
    second_cross = cross(magnet, first_cross)
    return -(first_cross + damping * second_cross) / (1.0 + damping * damping)


def reference(magnet, stiffness, kern):
    cells_x = magnet.shape[1]
    cells_y = magnet.shape[2]
    stacked = jnp.concatenate([magnet, stiffness[None]], 0)
    padded = jnp.pad(stacked, ((0, 0), (1, 1), (1, 1)))
    exchange_part = exchange_field(padded, 0, 0, cells_x, cells_y)
    along_y = jnp.fft.rfft(magnet, n=2 * cells_y, axis=2)[:, :, :cells_y]
    spectrum = jnp.fft.fft(along_y, n=2 * cells_x, axis=1)
    first_ky = jnp.arange(cells_y, dtype=jnp.int32) == 0
    fields = []
    for target in range(3):
        summed = None
        for source in range(3):
            term = jnp.transpose(kern[tensor_slots[target][source]]) * spectrum[source]
            summed = term if summed is None else summed + term
        inverse_x = jnp.fft.ifft(-summed, axis=0)[:cells_x]
        coef_re = jnp.where(first_ky, 1.0, 2.0) * jnp.real(inverse_x)
        coef_im = jnp.where(first_ky, 0.0, 2.0) * jnp.imag(inverse_x)
        inverse_y = jnp.fft.ifft(lax.complex(coef_re, coef_im), n=2 * cells_y, axis=1)
        fields.append(jnp.real(inverse_y)[:, :cells_y])
    demag_part = jnp.stack(fields)
    return torque_of(magnet, exchange_part + demag_part)
```

```python
import functools
import math

import jax
import jax.numpy as jnp
import ml_dtypes
import numpy as np
from jax import lax
from jax.experimental import pallas as pl
from jax.experimental.pallas import tpu as pltpu
from jax.sharding import PartitionSpec as P

damping = 0.3
anisotropy = 0.8
tensor_slots = ((0, 3, 4), (3, 1, 5), (4, 5, 2))

rows_n = 16
cols_n = 32
cells = 64
lanes = 128
length = 4096
bf16 = jnp.bfloat16
f32 = jnp.float32


def wave(first, second, period):
    angle = 2.0 * math.pi * (np.outer(first, second) % period) / period
    return np.cos(angle), np.sin(angle)


def split_table(table):
    high = table.astype(ml_dtypes.bfloat16)
    low = (table - high.astype(np.float64)).astype(ml_dtypes.bfloat16)
    return high, low


def thick(table):
    high, low = split_table(table)
    return np.concatenate([high, low, high], 1)


def tall(table):
    return np.concatenate(split_table(table), 0)


def tables():
    row = np.arange(rows_n)
    col = np.arange(cols_n)
    y_l = np.arange(lanes)
    k1 = (4 * np.arange(8)[None, :] + np.arange(4)[:, None]).reshape(-1)
    k2 = np.arange(64)
    x_ir = (4 * row[None, :] + np.arange(4)[:, None]).reshape(-1)
    k1x = np.arange(64)
    k2x = (2 * np.arange(32)[None, :] + np.arange(2)[:, None]).reshape(-1)
    x_rci = np.repeat(4 * row[:, None, None] + np.arange(4)[None, None, :], 2, 1).reshape(-1)
    imag_rci = np.repeat(np.repeat(np.arange(2)[None, :, None], rows_n, 0), 4, 2).reshape(-1, 1)
    kappa = (4 * col[None, :] + np.arange(4)[:, None]).reshape(-1)
    y1 = np.arange(32)
    u_order = (4 * row[None, :] + np.arange(4)[:, None]).reshape(-1)

    cos, sin = wave(k1, row, 32)
    y_first = thick(np.concatenate([cos, -sin], 0))
    cos, sin = wave(k1, y_l, length)
    y_twist = np.stack([cos, sin]).astype(np.float32)
    cos, sin = wave(k2, y_l, 128)
    y_last = np.stack([np.concatenate([cos, sin], 1), np.concatenate([-sin, cos], 1)], 1)
    y_last = tall(y_last.reshape(128, 256))

    cos, sin = wave(k1x, col, 64)
    x_first = thick(np.concatenate([cos, sin], 0))
    x_back = tall(np.concatenate([cos, sin], 0).reshape(2, 64, 32).transpose(2, 0, 1).reshape(32, 128))
    cos, sin = wave(k1x, x_ir, length)
    x_twist = np.stack([np.concatenate([cos, cos], 1), np.concatenate([sin, -sin], 1)])
    cos, sin = wave(k2x, x_ir, 64)
    x_last = tall(np.concatenate([cos, sin], 1))
    cos, sin = wave(x_rci, k2x, 64)
    x_lead = tall(np.concatenate([cos, sin], 1))
    cos, sin = wave(x_rci, k1x, length)
    own = np.where(imag_rci == 0, np.concatenate([cos, -cos], 1), np.concatenate([sin, -sin], 1))
    other = np.where(imag_rci == 0, np.concatenate([-sin, -sin], 1), np.concatenate([cos, cos], 1))
    x_untwist = np.stack([own, other])
    x_twists = np.concatenate([x_twist, x_untwist], 1).astype(np.float32)

    cos, sin = wave(y1, row, 32)
    z_first = thick(np.concatenate([np.concatenate([cos, -sin], 1), np.concatenate([sin, cos], 1)], 0))
    cos, sin = wave(y1, kappa, length)
    z_twist = np.stack([cos, sin]).astype(np.float32)
    cos, sin = wave(u_order, kappa, 128)
    z_last = tall(np.concatenate([cos, -sin], 1))
    return {
        "y": (y_first, y_twist, y_last),
        "x": (x_first, x_twists, x_last, x_lead, x_back),
        "z": (z_first, z_twist, z_last),
    }


def split(values):
    high = values.astype(bf16)
    low = (values - high.astype(f32)).astype(bf16)
    return high, low


def stacked_product(table, values):
    high, low = split(values)
    return jnp.dot(table, jnp.concatenate([high, high, low], 0), preferred_element_type=f32)


def split_product(table, values, contract):
    high, low = split(values)
    dims = (((1,), (contract,)), ((), ()))
    size = table.shape[0] // 2
    both = lax.dot_general(table, high, dims, preferred_element_type=f32)
    rest = lax.dot_general(table[:size], low, dims, preferred_element_type=f32)
    return both[:size] + both[size:] + rest


def half_turn(values):
    return pltpu.roll(values, 64, 1)


def lane_index(shape):
    return lax.broadcasted_iota(jnp.int32, shape, len(shape) - 1)


def pack_body(magnet_ref, stiff_ref, out_ref, edge_ref):
    for a in range(3):
        for i in range(4):
            out_ref[pl.ds(4 * a + i, rows_n, stride=16), :] = magnet_ref[
                a, pl.ds(i, rows_n, stride=4), :
            ]
    former = jnp.concatenate([magnet_ref[0], magnet_ref[1]], 0).T
    latter = jnp.concatenate([magnet_ref[2], stiff_ref[...]], 0).T
    for row, piece in enumerate((former[:1], latter[:1], former[127:], latter[127:])):
        out_ref[pl.ds(12 + row, rows_n, stride=16), :] = jnp.broadcast_to(piece, (rows_n, lanes))
    for a in range(3):
        edge_ref[a : a + 1, :] = magnet_ref[a, :1, :]
        edge_ref[4 + a : 5 + a, :] = magnet_ref[a, cells - 1 :, :]
    edge_ref[3:4, :] = stiff_ref[:1, :]
    edge_ref[7:8, :] = stiff_ref[cells - 1 :, :]


def kern_body(kern_ref, out_ref, held_ref):
    for j in range(6):
        for b in range(32):
            held_ref[pl.ds(j * 128 + b, 4, stride=32), :] = kern_ref[j, :, pl.ds(128 * b, 128)]
    low = lane_index((128, 128)) < 64
    for j in range(6):
        part = held_ref[pl.ds(j * 128, 128), :]
        turned = half_turn(part)
        even = jnp.where(low, part, turned)
        odd = jnp.where(low, turned, part)
        for k in range(4):
            out_ref[j, k, 0:32, :] = even[32 * k : 32 * k + 32]
            out_ref[j, k, 32:64, :] = odd[32 * k : 32 * k + 32]


def forward_rows_body(in_ref, first_ref, twist_ref, last_ref, out_ref):
    lines = [in_ref[pl.ds(4 * a + i, rows_n, stride=16), :] for i in range(4) for a in range(3)]
    section = stacked_product(first_ref[...], jnp.concatenate(lines, 1))
    cos, sin = twist_ref[0], twist_ref[1]
    turned = []
    for n in range(12):
        re = section[:32, 128 * n : 128 * n + 128]
        im = section[32:, 128 * n : 128 * n + 128]
        turned.append(jnp.concatenate([re * cos + im * sin, im * cos - re * sin], 1))
    result = split_product(last_ref[...], jnp.concatenate(turned, 0), 1)
    for r in range(rows_n):
        for t in range(3):
            out_ref[24 * r + 8 * t : 24 * r + 8 * t + 8, :] = result[
                8 * r : 8 * r + 8, 128 * t : 128 * t + 128
            ]


def forward_cols_body(place_ref, in_ref, edge_ref, out_ref):
    lane = lane_index((rows_n, 128))
    for k2l in range(4):
        pieces = []
        for part in range(2):
            tiles = [
                in_ref[pl.ds(8 * t + 2 * k2l + part, rows_n, stride=24), :]
                for t in range(3)
            ]
            pieces.append(tiles[0])
            for i in range(1, 4):
                tile, offset = divmod(96 * i, 128)
                piece = pltpu.roll(tiles[tile], 128 - offset, 1)
                if tile < 2:
                    after = pltpu.roll(tiles[tile + 1], 128 - offset, 1)
                    piece = jnp.where(lane < 128 - offset, piece, after)
                pieces.append(piece)
        turned = jnp.concatenate(pieces, 0).T
        for a in range(3):
            for k in range(4):
                out_ref[pl.ds(128 * k2l + 4 * a + k, 8, stride=16), :] = turned[
                    32 * a + 8 * k : 32 * a + 8 * k + 8
                ]
    col = place_ref[1]
    first, last = edge_ref[0:4, :], edge_ref[4:8, :]
    for c in range(cols_n):
        out_ref[16 * c + 12 : 16 * c + 16, :] = jnp.where(c > col, last, first)


def spectral_body(
    place_ref, in_ref, kern_ref, first_ref, twist_ref, last_ref, lead_ref, back_ref, out_ref
):
    columns = [in_ref[pl.ds(j, cols_n, stride=16), :] for j in range(12)]
    section = stacked_product(first_ref[...], jnp.concatenate(columns, 1))
    lane = lane_index((64, 128))
    sign = jnp.where(lane < 64, 1.0, -1.0).astype(f32)
    own, other = twist_ref[0, :64, :], twist_ref[1, :64, :]
    turned = []
    for j in range(12):
        block = section[:, 128 * j : 128 * j + 128]
        block = block[:64] + half_turn(block[64:]) * sign
        block = block * own + half_turn(block) * other
        turned.append(block)
        turned.append(half_turn(block) * sign)
    freq = split_product(last_ref[...], jnp.concatenate(turned, 0), 1)
    sources = []
    for target in range(3):
        for k in range(4):
            total = None
            for b in range(3):
                j = 4 * b + k
                term = kern_ref[tensor_slots[target][b], k] * freq[:, 128 * j : 128 * j + 128]
                total = term if total is None else total + term
            sources.append(jnp.concatenate([total, -half_turn(total) * sign], 0))
    section = split_product(lead_ref[...], jnp.concatenate(sources, 1), 0)
    own, other = twist_ref[0, 64:, :], twist_ref[1, 64:, :]
    turned = []
    for j in range(12):
        block = section[:, 128 * j : 128 * j + 128]
        turned.append(block * own + half_turn(block) * other)
    result = split_product(back_ref[...], jnp.concatenate(turned, 0), 1)
    scale = -1.0 / (length * length)
    lane = lane_index((cols_n, 128))
    zero_weight = jnp.where((lane // 4) % 2 == 0, 1.0, 0.0).astype(f32)
    is_zero = jnp.logical_and(place_ref[0] == 0, place_ref[1] == 0)
    for j in range(12):
        block = result[:, 128 * j : 128 * j + 128]
        weight = jnp.full((cols_n, 128), 2.0, f32)
        if j % 4 == 0:
            weight = jnp.where(is_zero, zero_weight, weight)
        out_ref[pl.ds(j, cols_n, stride=16), :] = block * (weight * scale)
    for j in range(12, 16):
        out_ref[pl.ds(j, cols_n, stride=16), :] = jnp.zeros((cols_n, 128), f32)


def back_cols_body(in_ref, out_ref):
    for a in range(3):
        block = [in_ref[pl.ds(4 * a + k, cols_n, stride=16), :] for k in range(4)]
        turned = jnp.concatenate(block, 0).T
        for r in range(rows_n):
            out_ref[24 * r + 8 * a : 24 * r + 8 * a + 8, :] = turned[8 * r : 8 * r + 8]


def back_rows_body(in_ref, first_ref, twist_ref, last_ref, out_ref):
    columns = []
    for a in range(3):
        for i in range(4):
            re = in_ref[pl.ds(8 * a + i, rows_n, stride=24), :]
            im = in_ref[pl.ds(8 * a + 4 + i, rows_n, stride=24), :]
            columns.append(jnp.concatenate([re, im], 0))
    section = stacked_product(first_ref[...], jnp.concatenate(columns, 1))
    cos, sin = twist_ref[0], twist_ref[1]
    turned = []
    for n in range(12):
        re = section[:32, 128 * n : 128 * n + 128]
        im = section[32:, 128 * n : 128 * n + 128]
        turned.append(jnp.concatenate([re * cos - im * sin, im * cos + re * sin], 1))
    result = split_product(last_ref[...], jnp.concatenate(turned, 0), 1)
    for a in range(3):
        for y2 in range(4):
            out_ref[pl.ds(4 * a + y2, rows_n, stride=16), :] = result[
                16 * y2 : 16 * y2 + 16, 128 * a : 128 * a + 128
            ]
    for j in range(12, 16):
        out_ref[pl.ds(j, rows_n, stride=16), :] = jnp.zeros((rows_n, 128), f32)


def cross(former, latter):
    return (
        former[1] * latter[2] - former[2] * latter[1],
        former[2] * latter[0] - former[0] * latter[2],
        former[0] * latter[1] - former[1] * latter[0],
    )


def torque_body(place_ref, in_ref, magnet_ref, stiff_ref, beside_y_ref, beside_x_ref, out_ref, field_ref):
    row, col = place_ref[0], place_ref[1]
    group = lane_index((rows_n, 128)) // 32
    for a in range(3):
        tiles = [in_ref[pl.ds(4 * a + y2, rows_n, stride=16), :] for y2 in range(4)]
        for i in range(4):
            line = None
            for y2 in range(4):
                shift = (32 * (y2 - i)) % 128
                piece = tiles[y2] if shift == 0 else pltpu.roll(tiles[y2], shift, 1)
                line = piece if line is None else jnp.where(group == y2, piece, line)
            field_ref[a, pl.ds(i, rows_n, stride=4), :] = line
    before_y = beside_y_ref[pl.ds(pl.multiple_of(16 * jnp.maximum(row - 1, 0), 16), 16), :]
    after_y = beside_y_ref[pl.ds(pl.multiple_of(16 * jnp.minimum(row + 1, rows_n - 1), 16), 16), :]
    before_x = beside_x_ref[pl.ds(pl.multiple_of(16 * jnp.maximum(col - 1, 0), 16), 16), :]
    after_x = beside_x_ref[pl.ds(pl.multiple_of(16 * jnp.minimum(col + 1, cols_n - 1), 16), 16), :]
    edges = jnp.concatenate([before_y[14:16], after_y[12:14], jnp.zeros((124, 128), f32)], 0).T
    stack = [magnet_ref[0], magnet_ref[1], magnet_ref[2], stiff_ref[...]]
    lane = lane_index((cells, 128))
    sub = lax.broadcasted_iota(jnp.int32, (cells, 128), 0)

    def neighbour(n, direction):
        centre = stack[n]
        part = slice(64 * (n % 2), 64 * (n % 2) + 64)
        if direction == 0:
            return jnp.where(sub == cells - 1, after_x[12 + n : 13 + n], pltpu.roll(centre, cells - 1, 0))
        if direction == 1:
            return jnp.where(sub == 0, before_x[12 + n : 13 + n], pltpu.roll(centre, 1, 0))
        if direction == 2:
            edge = edges[part, 2 + n // 2 : 3 + n // 2]
            return jnp.where(lane == 127, edge, pltpu.roll(centre, 127, 1))
        edge = edges[part, n // 2 : n // 2 + 1]
        return jnp.where(lane == 0, edge, pltpu.roll(centre, 1, 1))

    absent = (
        jnp.logical_and(sub == cells - 1, col == cols_n - 1),
        jnp.logical_and(sub == 0, col == 0),
        jnp.logical_and(lane == 127, row == rows_n - 1),
        jnp.logical_and(lane == 0, row == 0),
    )
    exchange = [None] * 3
    for direction in range(4):
        coupling = 0.5 * (stack[3] + neighbour(3, direction))
        coupling = jnp.where(absent[direction], 0.0, coupling)
        for a in range(3):
            term = coupling * (neighbour(a, direction) - stack[a])
            exchange[a] = term if exchange[a] is None else exchange[a] + term
    magnet = stack[:3]
    field = [exchange[a] + field_ref[a] for a in range(3)]
    field[2] = field[2] + anisotropy * magnet[2]
    first_cross = cross(magnet, field)
    second_cross = cross(magnet, first_cross)
    factor = -1.0 / (1.0 + damping * damping)
    for a in range(3):
        out_ref[a] = (first_cross[a] + damping * second_cross[a]) * factor


in_vmem = pl.BlockSpec(memory_space=pltpu.VMEM)
in_smem = pl.BlockSpec(memory_space=pltpu.SMEM)


def call(body, out_shapes, *args, scratch=(), place=False, flops=10**8):
    shapes = [jax.ShapeDtypeStruct(shape, f32) for shape in out_shapes]
    specs = [in_smem if place and n == 0 else in_vmem for n in range(len(args))]
    return pl.pallas_call(
        body,
        out_shape=shapes,
        in_specs=specs,
        out_specs=[in_vmem] * len(shapes),
        scratch_shapes=list(scratch),
        compiler_params=pltpu.CompilerParams(vmem_limit_bytes=48 * 1024 * 1024),
        cost_estimate=pl.CostEstimate(flops=flops, bytes_accessed=10**6, transcendentals=0),
    )(*args)


def exchange(array, axis, chunks):
    shape = array.shape
    array = array.reshape(chunks, shape[0] // chunks, shape[1])
    return lax.all_to_all(array, axis, split_axis=0, concat_axis=0, tiled=True).reshape(shape)


def local(magnet, stiffness, kern):
    constant = {name: [jnp.asarray(t) for t in group] for name, group in tables().items()}
    place = jnp.stack([lax.axis_index("row"), lax.axis_index("col")]).astype(jnp.int32)
    packed, edge = call(pack_body, [(256, 128), (8, 128)], magnet, stiffness)
    (spread,) = call(
        kern_body, [(6, 4, 64, 128)], kern, scratch=[pltpu.VMEM((768, 128), f32)]
    )
    lines = exchange(packed, "row", rows_n)
    (along_y,) = call(forward_rows_body, [(384, 128)], lines, *constant["y"])
    along_y = exchange(along_y, "row", rows_n)
    (columns,) = call(forward_cols_body, [(512, 128)], place, along_y, edge, place=True)
    columns = exchange(columns, "col", cols_n)
    (inverse_x,) = call(
        spectral_body, [(512, 128)], place, columns, spread, *constant["x"], place=True
    )
    inverse_x = exchange(inverse_x, "col", cols_n)
    (coef,) = call(back_cols_body, [(384, 128)], inverse_x)
    coef = exchange(coef, "row", rows_n)
    (field,) = call(back_rows_body, [(256, 128)], coef, *constant["z"])
    field = exchange(field, "row", rows_n)
    (torque,) = call(
        torque_body,
        [(3, 64, 128)],
        place,
        field,
        magnet,
        stiffness,
        lines,
        columns,
        place=True,
        scratch=[pltpu.VMEM((3, 64, 128), f32)],
    )
    return torque


def solution(mesh):
    in_specs = (P(None, "col", "row"), P("col", "row"), P(None, ("row", "col"), None))
    out_specs = P(None, "col", "row")
    return jax.shard_map(local, mesh=mesh, in_specs=in_specs, out_specs=out_specs, check_vma=False)
```

```python
import math

import jax
import jax.numpy as jnp
import ml_dtypes
import numpy as np
from jax import lax
from jax.experimental import pallas as pl
from jax.experimental.pallas import tpu as pltpu
from jax.sharding import PartitionSpec as P

damping = 0.3
anisotropy = 0.8
tensor_slots = ((0, 3, 4), (3, 1, 5), (4, 5, 2))

rows_n = 16
cols_n = 32
cells = 64
lanes = 128
length = 4096
bf16 = jnp.bfloat16
f32 = jnp.float32


def wave(first, second, period):
    angle = 2.0 * math.pi * (np.outer(first, second) % period) / period
    return np.cos(angle), np.sin(angle)


def split_table(table):
    high = table.astype(ml_dtypes.bfloat16)
    low = (table - high.astype(np.float64)).astype(ml_dtypes.bfloat16)
    return high, low


def thick(table):
    high, low = split_table(table)
    return np.concatenate([high, low, high], 1)


def tall(table):
    return np.concatenate(split_table(table), 0)


def tables():
    row = np.arange(rows_n)
    col = np.arange(cols_n)
    y_l = np.arange(lanes)
    k1 = (4 * np.arange(8)[None, :] + np.arange(4)[:, None]).reshape(-1)
    k2 = np.arange(64)
    x_ir = (4 * row[None, :] + np.arange(4)[:, None]).reshape(-1)
    k1x = np.arange(64)
    k2x = (2 * np.arange(32)[None, :] + np.arange(2)[:, None]).reshape(-1)
    x_rci = np.repeat(4 * row[:, None, None] + np.arange(4)[None, None, :], 2, 1).reshape(-1)
    imag_rci = np.repeat(np.repeat(np.arange(2)[None, :, None], rows_n, 0), 4, 2).reshape(-1, 1)
    kappa = (4 * col[None, :] + np.arange(4)[:, None]).reshape(-1)
    y1 = np.arange(32)
    u_order = (4 * row[None, :] + np.arange(4)[:, None]).reshape(-1)

    cos, sin = wave(k1, row, 32)
    y_first = thick(np.concatenate([cos, -sin], 0))
    cos, sin = wave(k1, y_l, length)
    y_twist = np.stack([cos, sin]).astype(np.float32)
    cos, sin = wave(k2, y_l, 128)
    y_last = np.stack([np.concatenate([cos, sin], 1), np.concatenate([-sin, cos], 1)], 1)
    y_last = tall(y_last.reshape(128, 256))

    cos, sin = wave(k1x, col, 64)
    x_first = thick(np.concatenate([cos, sin], 0))
    x_back = tall(np.concatenate([cos, sin], 0).reshape(2, 64, 32).transpose(2, 0, 1).reshape(32, 128))
    cos, sin = wave(k1x, x_ir, length)
    x_twist = np.stack([np.concatenate([cos, cos], 1), np.concatenate([sin, -sin], 1)])
    cos, sin = wave(k2x, x_ir, 64)
    x_last = tall(np.concatenate([cos, sin], 1))
    cos, sin = wave(x_rci, k2x, 64)
    x_lead = tall(np.concatenate([cos, sin], 1))
    cos, sin = wave(x_rci, k1x, length)
    own = np.where(imag_rci == 0, np.concatenate([cos, -cos], 1), np.concatenate([sin, -sin], 1))
    other = np.where(imag_rci == 0, np.concatenate([-sin, -sin], 1), np.concatenate([cos, cos], 1))
    x_untwist = np.stack([own, other])
    x_twists = np.concatenate([x_twist, x_untwist], 1).astype(np.float32)

    cos, sin = wave(y1, row, 32)
    z_first = thick(np.concatenate([np.concatenate([cos, -sin], 1), np.concatenate([sin, cos], 1)], 0))
    cos, sin = wave(y1, kappa, length)
    z_twist = np.stack([cos, sin]).astype(np.float32)
    cos, sin = wave(u_order, kappa, 128)
    z_last = tall(np.concatenate([cos, -sin], 1))
    return {
        "y": (y_first, y_twist, y_last),
        "x": (x_first, x_twists, x_last, x_lead, x_back),
        "z": (z_first, z_twist, z_last),
    }


def split(values):
    high = values.astype(bf16)
    low = (values - high.astype(f32)).astype(bf16)
    return high, low


def stacked_product(table, values):
    high, low = split(values)
    return jnp.dot(table, jnp.concatenate([high, high, low], 0), preferred_element_type=f32)


def split_product(table, values, contract):
    high, low = split(values)
    dims = (((1,), (contract,)), ((), ()))
    size = table.shape[0] // 2
    both = lax.dot_general(table, high, dims, preferred_element_type=f32)
    rest = lax.dot_general(table[:size], low, dims, preferred_element_type=f32)
    return both[:size] + both[size:] + rest


def half_turn(values):
    return pltpu.roll(values, 64, 1)


def lane_index(shape):
    return lax.broadcasted_iota(jnp.int32, shape, len(shape) - 1)


def pack_body(magnet_hbm, stiff_hbm, out_ref, edge_ref, magnet_ref, stiff_ref, sems):
    copies = [
        pltpu.make_async_copy(magnet_hbm, magnet_ref, sems.at[0]),
        pltpu.make_async_copy(stiff_hbm, stiff_ref, sems.at[1]),
    ]
    for copy in copies:
        copy.start()
    for copy in copies:
        copy.wait()
    for a in range(3):
        for i in range(4):
            out_ref[pl.ds(4 * a + i, rows_n, stride=16), :] = magnet_ref[
                a, pl.ds(i, rows_n, stride=4), :
            ]
    former = jnp.concatenate([magnet_ref[0], magnet_ref[1]], 0).T
    latter = jnp.concatenate([magnet_ref[2], stiff_ref[...]], 0).T
    for row, piece in enumerate((former[:1], latter[:1], former[127:], latter[127:])):
        out_ref[pl.ds(12 + row, rows_n, stride=16), :] = jnp.broadcast_to(piece, (rows_n, lanes))
    for a in range(3):
        edge_ref[a : a + 1, :] = magnet_ref[a, :1, :]
        edge_ref[4 + a : 5 + a, :] = magnet_ref[a, cells - 1 :, :]
    edge_ref[3:4, :] = stiff_ref[:1, :]
    edge_ref[7:8, :] = stiff_ref[cells - 1 :, :]


def spread_kern(kern_ref, held_ref):
    for j in range(6):
        for b in range(32):
            held_ref[pl.ds(j * 128 + b, 4, stride=32), :] = kern_ref[j, :, pl.ds(128 * b, 128)]
    low = lane_index((32, 128)) < 64
    spread = []
    for j in range(6):
        spread.append([])
        for k in range(4):
            part = held_ref[pl.ds(j * 128 + 32 * k, 32), :]
            turned = half_turn(part)
            halves = [jnp.where(low, part, turned), jnp.where(low, turned, part)]
            spread[j].append(jnp.concatenate(halves, 0))
    return spread


def forward_rows_body(in_ref, first_ref, twist_ref, last_ref, out_ref):
    lines = [in_ref[pl.ds(4 * a + i, rows_n, stride=16), :] for i in range(4) for a in range(3)]
    section = stacked_product(first_ref[...], jnp.concatenate(lines, 1))
    cos, sin = twist_ref[0], twist_ref[1]
    turned = []
    for n in range(12):
        re = section[:32, 128 * n : 128 * n + 128]
        im = section[32:, 128 * n : 128 * n + 128]
        turned.append(jnp.concatenate([re * cos + im * sin, im * cos - re * sin], 1))
    result = split_product(last_ref[...], jnp.concatenate(turned, 0), 1)
    for r in range(rows_n):
        for t in range(3):
            out_ref[24 * r + 8 * t : 24 * r + 8 * t + 8, :] = result[
                8 * r : 8 * r + 8, 128 * t : 128 * t + 128
            ]


def forward_cols_body(in_ref, edge_ref, out_ref):
    lane = lane_index((rows_n, 128))
    for k2l in range(4):
        pieces = []
        for part in range(2):
            tiles = [
                in_ref[pl.ds(8 * t + 2 * k2l + part, rows_n, stride=24), :]
                for t in range(3)
            ]
            pieces.append(tiles[0])
            for i in range(1, 4):
                tile, offset = divmod(96 * i, 128)
                piece = pltpu.roll(tiles[tile], 128 - offset, 1)
                if tile < 2:
                    after = pltpu.roll(tiles[tile + 1], 128 - offset, 1)
                    piece = jnp.where(lane < 128 - offset, piece, after)
                pieces.append(piece)
        turned = jnp.concatenate(pieces, 0).T
        for a in range(3):
            for k in range(4):
                out_ref[pl.ds(128 * k2l + 4 * a + k, 8, stride=16), :] = turned[
                    32 * a + 8 * k : 32 * a + 8 * k + 8
                ]
    col = lax.axis_index("col")
    first, last = edge_ref[0:4, :], edge_ref[4:8, :]
    for c in range(cols_n):
        out_ref[16 * c + 12 : 16 * c + 16, :] = jnp.where(c > col, last, first)


def spectral_body(
    in_ref, kern_ref, first_ref, twist_ref, last_ref, lead_ref, back_ref, out_ref, held_ref
):
    columns = [in_ref[pl.ds(j, cols_n, stride=16), :] for j in range(12)]
    section = stacked_product(first_ref[...], jnp.concatenate(columns, 1))
    lane = lane_index((64, 128))
    sign = jnp.where(lane < 64, 1.0, -1.0).astype(f32)
    own, other = twist_ref[0, :64, :], twist_ref[1, :64, :]
    turned = []
    for j in range(12):
        block = section[:, 128 * j : 128 * j + 128]
        block = block[:64] + half_turn(block[64:]) * sign
        block = block * own + half_turn(block) * other
        turned.append(block)
        turned.append(half_turn(block) * sign)
    freq = split_product(last_ref[...], jnp.concatenate(turned, 0), 1)
    kern = spread_kern(kern_ref, held_ref)
    sources = []
    for target in range(3):
        for k in range(4):
            total = None
            for b in range(3):
                j = 4 * b + k
                term = kern[tensor_slots[target][b]][k] * freq[:, 128 * j : 128 * j + 128]
                total = term if total is None else total + term
            sources.append(jnp.concatenate([total, -half_turn(total) * sign], 0))
    section = split_product(lead_ref[...], jnp.concatenate(sources, 1), 0)
    own, other = twist_ref[0, 64:, :], twist_ref[1, 64:, :]
    turned = []
    for j in range(12):
        block = section[:, 128 * j : 128 * j + 128]
        turned.append(block * own + half_turn(block) * other)
    result = split_product(back_ref[...], jnp.concatenate(turned, 0), 1)
    scale = -1.0 / (length * length)
    lane = lane_index((cols_n, 128))
    zero_weight = jnp.where((lane // 4) % 2 == 0, 1.0, 0.0).astype(f32)
    is_zero = jnp.logical_and(lax.axis_index("row") == 0, lax.axis_index("col") == 0)
    for j in range(12):
        block = result[:, 128 * j : 128 * j + 128]
        weight = jnp.full((cols_n, 128), 2.0, f32)
        if j % 4 == 0:
            weight = jnp.where(is_zero, zero_weight, weight)
        out_ref[pl.ds(j, cols_n, stride=16), :] = block * (weight * scale)
    for j in range(12, 16):
        out_ref[pl.ds(j, cols_n, stride=16), :] = jnp.zeros((cols_n, 128), f32)


def back_cols_body(in_ref, out_ref):
    for a in range(3):
        block = [in_ref[pl.ds(4 * a + k, cols_n, stride=16), :] for k in range(4)]
        turned = jnp.concatenate(block, 0).T
        for r in range(rows_n):
            out_ref[24 * r + 8 * a : 24 * r + 8 * a + 8, :] = turned[8 * r : 8 * r + 8]


def back_rows_body(in_ref, first_ref, twist_ref, last_ref, out_ref):
    columns = []
    for a in range(3):
        for i in range(4):
            re = in_ref[pl.ds(8 * a + i, rows_n, stride=24), :]
            im = in_ref[pl.ds(8 * a + 4 + i, rows_n, stride=24), :]
            columns.append(jnp.concatenate([re, im], 0))
    section = stacked_product(first_ref[...], jnp.concatenate(columns, 1))
    cos, sin = twist_ref[0], twist_ref[1]
    turned = []
    for n in range(12):
        re = section[:32, 128 * n : 128 * n + 128]
        im = section[32:, 128 * n : 128 * n + 128]
        turned.append(jnp.concatenate([re * cos - im * sin, im * cos + re * sin], 1))
    result = split_product(last_ref[...], jnp.concatenate(turned, 0), 1)
    for a in range(3):
        for y2 in range(4):
            out_ref[pl.ds(4 * a + y2, rows_n, stride=16), :] = result[
                16 * y2 : 16 * y2 + 16, 128 * a : 128 * a + 128
            ]
    for j in range(12, 16):
        out_ref[pl.ds(j, rows_n, stride=16), :] = jnp.zeros((rows_n, 128), f32)


def cross(former, latter):
    return (
        former[1] * latter[2] - former[2] * latter[1],
        former[2] * latter[0] - former[0] * latter[2],
        former[0] * latter[1] - former[1] * latter[0],
    )


def torque_body(in_ref, magnet_ref, stiff_ref, beside_y_ref, beside_x_ref, out_ref, field_ref):
    row, col = lax.axis_index("row"), lax.axis_index("col")
    group = lane_index((rows_n, 128)) // 32
    for a in range(3):
        tiles = [in_ref[pl.ds(4 * a + y2, rows_n, stride=16), :] for y2 in range(4)]
        for i in range(4):
            line = None
            for y2 in range(4):
                shift = (32 * (y2 - i)) % 128
                piece = tiles[y2] if shift == 0 else pltpu.roll(tiles[y2], shift, 1)
                line = piece if line is None else jnp.where(group == y2, piece, line)
            field_ref[a, pl.ds(i, rows_n, stride=4), :] = line
    before_y = beside_y_ref[pl.ds(pl.multiple_of(16 * jnp.maximum(row - 1, 0), 16), 16), :]
    after_y = beside_y_ref[pl.ds(pl.multiple_of(16 * jnp.minimum(row + 1, rows_n - 1), 16), 16), :]
    before_x = beside_x_ref[pl.ds(pl.multiple_of(16 * jnp.maximum(col - 1, 0), 16), 16), :]
    after_x = beside_x_ref[pl.ds(pl.multiple_of(16 * jnp.minimum(col + 1, cols_n - 1), 16), 16), :]
    edges = jnp.concatenate([before_y[14:16], after_y[12:14], jnp.zeros((124, 128), f32)], 0).T
    stack = [magnet_ref[0], magnet_ref[1], magnet_ref[2], stiff_ref[...]]
    lane = lane_index((cells, 128))
    sub = lax.broadcasted_iota(jnp.int32, (cells, 128), 0)

    def neighbour(n, direction):
        centre = stack[n]
        part = slice(64 * (n % 2), 64 * (n % 2) + 64)
        if direction == 0:
            return jnp.where(sub == cells - 1, after_x[12 + n : 13 + n], pltpu.roll(centre, cells - 1, 0))
        if direction == 1:
            return jnp.where(sub == 0, before_x[12 + n : 13 + n], pltpu.roll(centre, 1, 0))
        if direction == 2:
            edge = edges[part, 2 + n // 2 : 3 + n // 2]
            return jnp.where(lane == 127, edge, pltpu.roll(centre, 127, 1))
        edge = edges[part, n // 2 : n // 2 + 1]
        return jnp.where(lane == 0, edge, pltpu.roll(centre, 1, 1))

    absent = (
        jnp.logical_and(sub == cells - 1, col == cols_n - 1),
        jnp.logical_and(sub == 0, col == 0),
        jnp.logical_and(lane == 127, row == rows_n - 1),
        jnp.logical_and(lane == 0, row == 0),
    )
    exchange = [None] * 3
    for direction in range(4):
        coupling = 0.5 * (stack[3] + neighbour(3, direction))
        coupling = jnp.where(absent[direction], 0.0, coupling)
        for a in range(3):
            term = coupling * (neighbour(a, direction) - stack[a])
            exchange[a] = term if exchange[a] is None else exchange[a] + term
    magnet = stack[:3]
    field = [exchange[a] + field_ref[a] for a in range(3)]
    field[2] = field[2] + anisotropy * magnet[2]
    first_cross = cross(magnet, field)
    second_cross = cross(magnet, first_cross)
    factor = -1.0 / (1.0 + damping * damping)
    for a in range(3):
        out_ref[a] = (first_cross[a] + damping * second_cross[a]) * factor


in_vmem = pl.BlockSpec(memory_space=pltpu.VMEM)
in_any = pl.BlockSpec(memory_space=pl.ANY)


def call(body, out_shapes, *args, scratch=(), in_spec=in_vmem, flops=10**8):
    shapes = [jax.ShapeDtypeStruct(shape, f32) for shape in out_shapes]
    return pl.pallas_call(
        body,
        out_shape=shapes,
        in_specs=[in_spec] * len(args),
        out_specs=[in_vmem] * len(shapes),
        scratch_shapes=list(scratch),
        compiler_params=pltpu.CompilerParams(vmem_limit_bytes=48 * 1024 * 1024),
        cost_estimate=pl.CostEstimate(flops=flops, bytes_accessed=10**6, transcendentals=0),
    )(*args)


def exchange(array, axis, chunks):
    shape = array.shape
    array = array.reshape(chunks, shape[0] // chunks, shape[1])
    return lax.all_to_all(array, axis, split_axis=0, concat_axis=0, tiled=True).reshape(shape)


def local(magnet, stiffness, kern):
    constant = {name: [jnp.asarray(t) for t in group] for name, group in tables().items()}
    packed, edge = call(
        pack_body,
        [(256, 128), (8, 128)],
        magnet,
        stiffness,
        in_spec=in_any,
        scratch=[
            pltpu.VMEM((3, cells, lanes), f32),
            pltpu.VMEM((cells, lanes), f32),
            pltpu.SemaphoreType.DMA((2,)),
        ],
    )
    lines = exchange(packed, "row", rows_n)
    (along_y,) = call(forward_rows_body, [(384, 128)], lines, *constant["y"])
    along_y = exchange(along_y, "row", rows_n)
    (columns,) = call(forward_cols_body, [(512, 128)], along_y, edge)
    columns = exchange(columns, "col", cols_n)
    (inverse_x,) = call(
        spectral_body,
        [(512, 128)],
        columns,
        kern,
        *constant["x"],
        scratch=[pltpu.VMEM((768, 128), f32)],
    )
    inverse_x = exchange(inverse_x, "col", cols_n)
    (coef,) = call(back_cols_body, [(384, 128)], inverse_x)
    coef = exchange(coef, "row", rows_n)
    (field,) = call(back_rows_body, [(256, 128)], coef, *constant["z"])
    field = exchange(field, "row", rows_n)
    (torque,) = call(
        torque_body,
        [(3, 64, 128)],
        field,
        magnet,
        stiffness,
        lines,
        columns,
        scratch=[pltpu.VMEM((3, 64, 128), f32)],
    )
    return torque


def solution(mesh):
    in_specs = (P(None, "col", "row"), P("col", "row"), P(None, ("row", "col"), None))
    out_specs = P(None, "col", "row")
    return jax.shard_map(local, mesh=mesh, in_specs=in_specs, out_specs=out_specs, check_vma=False)
```

```python
import math

import jax
import jax.numpy as jnp
import ml_dtypes
import numpy as np
from jax import lax
from jax.experimental import pallas as pl
from jax.experimental.pallas import tpu as pltpu
from jax.sharding import PartitionSpec as P

damping = 0.3
anisotropy = 0.8
tensor_slots = ((0, 3, 4), (3, 1, 5), (4, 5, 2))

rows_n = 16
cols_n = 32
cells = 64
lanes = 128
length = 4096
bf16 = jnp.bfloat16
f32 = jnp.float32


def wave(first, second, period):
    angle = 2.0 * math.pi * (np.outer(first, second) % period) / period
    return np.cos(angle), np.sin(angle)


def split_table(table):
    high = table.astype(ml_dtypes.bfloat16)
    low = (table - high.astype(np.float64)).astype(ml_dtypes.bfloat16)
    return high, low


def thick(table):
    high, low = split_table(table)
    return np.concatenate([high, low, high], 1)


def tall(table):
    return np.concatenate(split_table(table), 0)


def tables():
    row = np.arange(rows_n)
    col = np.arange(cols_n)
    y_l = np.arange(lanes)
    k1 = (4 * np.arange(8)[None, :] + np.arange(4)[:, None]).reshape(-1)
    k2 = np.arange(64)
    x_ir = (4 * row[None, :] + np.arange(4)[:, None]).reshape(-1)
    k1x = np.arange(64)
    k2x = (2 * np.arange(32)[None, :] + np.arange(2)[:, None]).reshape(-1)
    x_rci = np.repeat(4 * row[:, None, None] + np.arange(4)[None, None, :], 2, 1).reshape(-1)
    imag_rci = np.repeat(np.repeat(np.arange(2)[None, :, None], rows_n, 0), 4, 2).reshape(-1, 1)
    kappa = (4 * col[None, :] + np.arange(4)[:, None]).reshape(-1)
    y1 = np.arange(32)
    u_order = (4 * row[None, :] + np.arange(4)[:, None]).reshape(-1)

    cos, sin = wave(k1, row, 32)
    y_first = thick(np.concatenate([cos, -sin], 0))
    cos, sin = wave(k1, y_l, length)
    y_twist = np.stack([cos, sin]).astype(np.float32)
    cos, sin = wave(k2, y_l, 128)
    y_last = np.stack([np.concatenate([cos, sin], 1), np.concatenate([-sin, cos], 1)], 1)
    y_last = tall(y_last.reshape(128, 256))

    cos, sin = wave(k1x, col, 64)
    x_first = thick(np.concatenate([cos, sin], 0))
    x_back = tall(np.concatenate([cos, sin], 0).reshape(2, 64, 32).transpose(2, 0, 1).reshape(32, 128))
    cos, sin = wave(k1x, x_ir, length)
    x_twist = np.stack([np.concatenate([cos, cos], 1), np.concatenate([sin, -sin], 1)])
    cos, sin = wave(k2x, x_ir, 64)
    x_last = tall(np.concatenate([cos, sin], 1))
    cos, sin = wave(x_rci, k2x, 64)
    x_lead = tall(np.concatenate([cos, sin], 1))
    cos, sin = wave(x_rci, k1x, length)
    own = np.where(imag_rci == 0, np.concatenate([cos, -cos], 1), np.concatenate([sin, -sin], 1))
    other = np.where(imag_rci == 0, np.concatenate([-sin, -sin], 1), np.concatenate([cos, cos], 1))
    x_untwist = np.stack([own, other])
    x_twists = np.concatenate([x_twist, x_untwist], 1).astype(np.float32)

    cos, sin = wave(y1, row, 32)
    z_first = thick(np.concatenate([np.concatenate([cos, -sin], 1), np.concatenate([sin, cos], 1)], 0))
    cos, sin = wave(y1, kappa, length)
    z_twist = np.stack([cos, sin]).astype(np.float32)
    cos, sin = wave(u_order, kappa, 128)
    z_last = tall(np.concatenate([cos, -sin], 1))
    return {
        "y": (y_first, y_twist, y_last),
        "x": (x_first, x_twists, x_last, x_lead, x_back),
        "z": (z_first, z_twist, z_last),
    }


def split(values):
    high = values.astype(bf16)
    low = (values - high.astype(f32)).astype(bf16)
    return high, low


def stacked_product(table, values):
    high, low = split(values)
    return jnp.dot(table, jnp.concatenate([high, high, low], 0), preferred_element_type=f32)


def split_product(table, values, contract):
    high, low = split(values)
    dims = (((1,), (contract,)), ((), ()))
    size = table.shape[0] // 2
    both = lax.dot_general(table, high, dims, preferred_element_type=f32)
    rest = lax.dot_general(table[:size], low, dims, preferred_element_type=f32)
    return both[:size] + both[size:] + rest


def half_turn(values):
    return pltpu.roll(values, 64, 1)


def lane_index(shape):
    return lax.broadcasted_iota(jnp.int32, shape, len(shape) - 1)


def pack_body(magnet_hbm, stiff_hbm, out_ref, edge_ref, magnet_ref, stiff_ref, sems):
    copies = [
        pltpu.make_async_copy(magnet_hbm, magnet_ref, sems.at[0]),
        pltpu.make_async_copy(stiff_hbm, stiff_ref, sems.at[1]),
    ]
    for copy in copies:
        copy.start()
    for copy in copies:
        copy.wait()
    for a in range(3):
        for i in range(4):
            out_ref[pl.ds(4 * a + i, rows_n, stride=14), :] = magnet_ref[
                a, pl.ds(i, rows_n, stride=4), :
            ]
    former = jnp.concatenate([magnet_ref[0], magnet_ref[1]], 0).T
    latter = jnp.concatenate([magnet_ref[2], stiff_ref[...]], 0).T
    after = lax.broadcasted_iota(jnp.int32, (rows_n, lanes), 0) > lax.axis_index("row")
    for n, sides in enumerate((former, latter)):
        out_ref[pl.ds(12 + n, rows_n, stride=14), :] = jnp.where(after, sides[127:], sides[:1])
    for a in range(3):
        edge_ref[a : a + 1, :] = magnet_ref[a, :1, :]
        edge_ref[4 + a : 5 + a, :] = magnet_ref[a, cells - 1 :, :]
    edge_ref[3:4, :] = stiff_ref[:1, :]
    edge_ref[7:8, :] = stiff_ref[cells - 1 :, :]


def spread_kern(kern_ref, held_ref):
    for j in range(6):
        for b in range(32):
            held_ref[pl.ds(j * 128 + b, 4, stride=32), :] = kern_ref[j, :, pl.ds(128 * b, 128)]
    low = lane_index((32, 128)) < 64
    spread = []
    for j in range(6):
        spread.append([])
        for k in range(4):
            part = held_ref[pl.ds(j * 128 + 32 * k, 32), :]
            turned = half_turn(part)
            halves = [jnp.where(low, part, turned), jnp.where(low, turned, part)]
            spread[j].append(jnp.concatenate(halves, 0))
    return spread


def forward_rows_body(in_ref, first_ref, twist_ref, last_ref, out_ref):
    lines = [in_ref[pl.ds(4 * a + i, rows_n, stride=14), :] for i in range(4) for a in range(3)]
    section = stacked_product(first_ref[...], jnp.concatenate(lines, 1))
    cos, sin = twist_ref[0], twist_ref[1]
    turned = []
    for n in range(12):
        re = section[:32, 128 * n : 128 * n + 128]
        im = section[32:, 128 * n : 128 * n + 128]
        turned.append(jnp.concatenate([re * cos + im * sin, im * cos - re * sin], 1))
    result = split_product(last_ref[...], jnp.concatenate(turned, 0), 1)
    for r in range(rows_n):
        for t in range(3):
            out_ref[24 * r + 8 * t : 24 * r + 8 * t + 8, :] = result[
                8 * r : 8 * r + 8, 128 * t : 128 * t + 128
            ]


def forward_cols_body(in_ref, edge_ref, out_ref):
    lane = lane_index((rows_n, 128))
    for k2l in range(4):
        pieces = []
        for part in range(2):
            tiles = [
                in_ref[pl.ds(8 * t + 2 * k2l + part, rows_n, stride=24), :]
                for t in range(3)
            ]
            pieces.append(tiles[0])
            for i in range(1, 4):
                tile, offset = divmod(96 * i, 128)
                piece = pltpu.roll(tiles[tile], 128 - offset, 1)
                if tile < 2:
                    after = pltpu.roll(tiles[tile + 1], 128 - offset, 1)
                    piece = jnp.where(lane < 128 - offset, piece, after)
                pieces.append(piece)
        turned = jnp.concatenate(pieces, 0).T
        for a in range(3):
            for k in range(4):
                out_ref[pl.ds(128 * k2l + 4 * a + k, 8, stride=16), :] = turned[
                    32 * a + 8 * k : 32 * a + 8 * k + 8
                ]
    col = lax.axis_index("col")
    first, last = edge_ref[0:4, :], edge_ref[4:8, :]
    for c in range(cols_n):
        out_ref[16 * c + 12 : 16 * c + 16, :] = jnp.where(c > col, last, first)


def spectral_body(
    in_ref, kern_ref, first_ref, twist_ref, last_ref, lead_ref, back_ref, out_ref, held_ref
):
    columns = [in_ref[pl.ds(j, cols_n, stride=16), :] for j in range(12)]
    section = stacked_product(first_ref[...], jnp.concatenate(columns, 1))
    lane = lane_index((64, 128))
    sign = jnp.where(lane < 64, 1.0, -1.0).astype(f32)
    own, other = twist_ref[0, :64, :], twist_ref[1, :64, :]
    turned = []
    for j in range(12):
        block = section[:, 128 * j : 128 * j + 128]
        block = block[:64] + half_turn(block[64:]) * sign
        block = block * own + half_turn(block) * other
        turned.append(block)
        turned.append(half_turn(block) * sign)
    freq = split_product(last_ref[...], jnp.concatenate(turned, 0), 1)
    kern = spread_kern(kern_ref, held_ref)
    sources = []
    for target in range(3):
        for k in range(4):
            total = None
            for b in range(3):
                j = 4 * b + k
                term = kern[tensor_slots[target][b]][k] * freq[:, 128 * j : 128 * j + 128]
                total = term if total is None else total + term
            sources.append(jnp.concatenate([total, -half_turn(total) * sign], 0))
    section = split_product(lead_ref[...], jnp.concatenate(sources, 1), 0)
    own, other = twist_ref[0, 64:, :], twist_ref[1, 64:, :]
    turned = []
    for j in range(12):
        block = section[:, 128 * j : 128 * j + 128]
        turned.append(block * own + half_turn(block) * other)
    result = split_product(back_ref[...], jnp.concatenate(turned, 0), 1)
    scale = -1.0 / (length * length)
    lane = lane_index((cols_n, 128))
    zero_weight = jnp.where((lane // 4) % 2 == 0, 1.0, 0.0).astype(f32)
    is_zero = jnp.logical_and(lax.axis_index("row") == 0, lax.axis_index("col") == 0)
    for j in range(12):
        block = result[:, 128 * j : 128 * j + 128]
        weight = jnp.full((cols_n, 128), 2.0, f32)
        if j % 4 == 0:
            weight = jnp.where(is_zero, zero_weight, weight)
        out_ref[pl.ds(j, cols_n, stride=12), :] = block * (weight * scale)


def back_cols_body(in_ref, out_ref):
    for a in range(3):
        block = [in_ref[pl.ds(4 * a + k, cols_n, stride=12), :] for k in range(4)]
        turned = jnp.concatenate(block, 0).T
        for r in range(rows_n):
            out_ref[24 * r + 8 * a : 24 * r + 8 * a + 8, :] = turned[8 * r : 8 * r + 8]


def back_rows_body(in_ref, first_ref, twist_ref, last_ref, out_ref):
    columns = []
    for a in range(3):
        for i in range(4):
            re = in_ref[pl.ds(8 * a + i, rows_n, stride=24), :]
            im = in_ref[pl.ds(8 * a + 4 + i, rows_n, stride=24), :]
            columns.append(jnp.concatenate([re, im], 0))
    section = stacked_product(first_ref[...], jnp.concatenate(columns, 1))
    cos, sin = twist_ref[0], twist_ref[1]
    turned = []
    for n in range(12):
        re = section[:32, 128 * n : 128 * n + 128]
        im = section[32:, 128 * n : 128 * n + 128]
        turned.append(jnp.concatenate([re * cos - im * sin, im * cos + re * sin], 1))
    result = split_product(last_ref[...], jnp.concatenate(turned, 0), 1)
    for a in range(3):
        for y2 in range(4):
            out_ref[pl.ds(4 * a + y2, rows_n, stride=12), :] = result[
                16 * y2 : 16 * y2 + 16, 128 * a : 128 * a + 128
            ]


def cross(former, latter):
    return (
        former[1] * latter[2] - former[2] * latter[1],
        former[2] * latter[0] - former[0] * latter[2],
        former[0] * latter[1] - former[1] * latter[0],
    )


def torque_body(in_ref, magnet_ref, stiff_ref, beside_y_ref, beside_x_ref, out_ref, field_ref):
    row, col = lax.axis_index("row"), lax.axis_index("col")
    group = lane_index((rows_n, 128)) // 32
    for a in range(3):
        tiles = [in_ref[pl.ds(4 * a + y2, rows_n, stride=12), :] for y2 in range(4)]
        for i in range(4):
            line = None
            for y2 in range(4):
                shift = (32 * (y2 - i)) % 128
                piece = tiles[y2] if shift == 0 else pltpu.roll(tiles[y2], shift, 1)
                line = piece if line is None else jnp.where(group == y2, piece, line)
            field_ref[a, pl.ds(i, rows_n, stride=4), :] = line
    before_y = beside_y_ref[pl.ds(14 * jnp.maximum(row - 1, 0) + 12, 2), :]
    after_y = beside_y_ref[pl.ds(14 * jnp.minimum(row + 1, rows_n - 1) + 12, 2), :]
    before_x = beside_x_ref[pl.ds(pl.multiple_of(16 * jnp.maximum(col - 1, 0), 16), 16), :]
    after_x = beside_x_ref[pl.ds(pl.multiple_of(16 * jnp.minimum(col + 1, cols_n - 1), 16), 16), :]
    edges = jnp.concatenate([before_y, after_y, jnp.zeros((124, 128), f32)], 0).T
    stack = [magnet_ref[0], magnet_ref[1], magnet_ref[2], stiff_ref[...]]
    lane = lane_index((cells, 128))
    sub = lax.broadcasted_iota(jnp.int32, (cells, 128), 0)

    def neighbour(n, direction):
        centre = stack[n]
        part = slice(64 * (n % 2), 64 * (n % 2) + 64)
        if direction == 0:
            return jnp.where(sub == cells - 1, after_x[12 + n : 13 + n], pltpu.roll(centre, cells - 1, 0))
        if direction == 1:
            return jnp.where(sub == 0, before_x[12 + n : 13 + n], pltpu.roll(centre, 1, 0))
        if direction == 2:
            edge = edges[part, 2 + n // 2 : 3 + n // 2]
            return jnp.where(lane == 127, edge, pltpu.roll(centre, 127, 1))
        edge = edges[part, n // 2 : n // 2 + 1]
        return jnp.where(lane == 0, edge, pltpu.roll(centre, 1, 1))

    absent = (
        jnp.logical_and(sub == cells - 1, col == cols_n - 1),
        jnp.logical_and(sub == 0, col == 0),
        jnp.logical_and(lane == 127, row == rows_n - 1),
        jnp.logical_and(lane == 0, row == 0),
    )
    exchange = [None] * 3
    for direction in range(4):
        coupling = 0.5 * (stack[3] + neighbour(3, direction))
        coupling = jnp.where(absent[direction], 0.0, coupling)
        for a in range(3):
            term = coupling * (neighbour(a, direction) - stack[a])
            exchange[a] = term if exchange[a] is None else exchange[a] + term
    magnet = stack[:3]
    field = [exchange[a] + field_ref[a] for a in range(3)]
    field[2] = field[2] + anisotropy * magnet[2]
    first_cross = cross(magnet, field)
    second_cross = cross(magnet, first_cross)
    factor = -1.0 / (1.0 + damping * damping)
    for a in range(3):
        out_ref[a] = (first_cross[a] + damping * second_cross[a]) * factor


in_vmem = pl.BlockSpec(memory_space=pltpu.VMEM)
in_hbm = pl.BlockSpec(memory_space=pltpu.HBM)


def call(body, out_shapes, *args, scratch=(), in_spec=in_vmem, vmem=32 * 2**20, flops=10**8):
    shapes = [jax.ShapeDtypeStruct(shape, f32) for shape in out_shapes]
    return pl.pallas_call(
        body,
        out_shape=shapes,
        in_specs=[in_spec] * len(args),
        out_specs=[in_vmem] * len(shapes),
        scratch_shapes=list(scratch),
        compiler_params=pltpu.CompilerParams(vmem_limit_bytes=vmem),
        cost_estimate=pl.CostEstimate(flops=flops, bytes_accessed=10**6, transcendentals=0),
    )(*args)


def exchange(array, axis, chunks):
    shape = array.shape
    rows = shape[0] // chunks
    tile = math.gcd(rows, 8)
    array = array.reshape(chunks, rows // tile, tile, shape[1])
    return lax.all_to_all(array, axis, split_axis=0, concat_axis=0, tiled=True).reshape(shape)


def local(magnet, stiffness, kern):
    constant = {name: [jnp.asarray(t) for t in group] for name, group in tables().items()}
    packed, edge = call(
        pack_body,
        [(224, 128), (8, 128)],
        magnet,
        stiffness,
        in_spec=in_hbm,
        vmem=60 * 2**20,
        scratch=[
            pltpu.VMEM((3, cells, lanes), f32),
            pltpu.VMEM((cells, lanes), f32),
            pltpu.SemaphoreType.DMA((2,)),
        ],
    )
    lines = exchange(packed, "row", rows_n)
    (along_y,) = call(forward_rows_body, [(384, 128)], lines, *constant["y"])
    along_y = exchange(along_y, "row", rows_n)
    (columns,) = call(forward_cols_body, [(512, 128)], along_y, edge)
    columns = exchange(columns, "col", cols_n)
    (inverse_x,) = call(
        spectral_body,
        [(384, 128)],
        columns,
        kern,
        *constant["x"],
        scratch=[pltpu.VMEM((768, 128), f32)],
    )
    inverse_x = exchange(inverse_x, "col", cols_n)
    (coef,) = call(back_cols_body, [(384, 128)], inverse_x)
    coef = exchange(coef, "row", rows_n)
    (field,) = call(back_rows_body, [(192, 128)], coef, *constant["z"])
    field = exchange(field, "row", rows_n)
    (torque,) = call(
        torque_body,
        [(3, 64, 128)],
        field,
        magnet,
        stiffness,
        lines,
        columns,
        scratch=[pltpu.VMEM((3, 64, 128), f32)],
    )
    return torque


def solution(mesh):
    in_specs = (P(None, "col", "row"), P("col", "row"), P(None, ("row", "col"), None))
    out_specs = P(None, "col", "row")
    return jax.shard_map(local, mesh=mesh, in_specs=in_specs, out_specs=out_specs, check_vma=False)
```

```python
import math

import jax
import jax.numpy as jnp
import ml_dtypes
import numpy as np
from jax import lax
from jax.experimental import pallas as pl
from jax.experimental.pallas import tpu as pltpu
from jax.sharding import PartitionSpec as P

damping = 0.3
anisotropy = 0.8
tensor_slots = ((0, 3, 4), (3, 1, 5), (4, 5, 2))

rows_n = 16
cols_n = 32
cells = 64
lanes = 128
length = 4096
bf16 = jnp.bfloat16
f32 = jnp.float32


modes = 16


def wave(first, second, period):
    angle = 2.0 * math.pi * (np.outer(first, second) % period) / period
    return np.cos(angle), np.sin(angle)


def split_table(table):
    high = table.astype(ml_dtypes.bfloat16)
    low = (table - high.astype(np.float64)).astype(ml_dtypes.bfloat16)
    return high, low


def thick(table):
    high, low = split_table(table)
    return np.concatenate([high, low, high], 1)


def tall(table):
    return np.concatenate(split_table(table), 0)


def deep(table):
    high, low = split_table(table)
    return np.concatenate(
        [np.concatenate([high, high], 1), np.concatenate([low, np.zeros_like(low)], 1)], 0
    )


def factors(count):
    place = np.arange(lanes) - 0.5 * (lanes - 1)
    angle = 2.0 * math.pi * np.outer(place, place) / length
    values, vectors, units = [], [], []
    for part, unit in ((np.cos(angle), 1.0), (np.sin(angle), -1j)):
        value, vector = np.linalg.eigh(part)
        values.append(value)
        vectors.append(vector * np.where(vector[-1] < 0.0, -1.0, 1.0))
        units.append(np.full(lanes, unit))
    values, vectors = np.concatenate(values), np.concatenate(vectors, 1)
    units = np.concatenate(units)
    kept = np.argsort(-np.abs(values), kind="stable")[:count]
    side = vectors[:, kept] * np.sqrt(np.abs(values[kept]))
    weight = units[kept] * np.sign(values[kept])
    return np.pad(side, ((0, 0), (0, modes - count))), np.pad(weight, (0, modes - count))


def row_transform(count):
    side, weight = factors(count)
    place = np.arange(lanes) - 0.5 * (lanes - 1)
    centre = lanes * np.arange(rows_n) + 0.5 * (lanes - 1)
    turn = np.exp(-2j * math.pi * np.outer(centre, place) / length)
    offset = 0.5 * (lanes - 1)
    phase = np.exp(-2j * math.pi * np.arange(rows_n) * lanes * offset / length)
    constant = np.exp(-2j * math.pi * offset * offset / length)
    gather = side.T[None] * turn[:, None, :] * phase[:, None, None]
    expand = (side * weight)[:, None, :] * turn.T[:, :, None] * phase[None, :, None] * constant
    return gather.reshape(rows_n * modes, lanes), expand.reshape(lanes, rows_n * modes)


def parts(table):
    return np.concatenate([table.real, table.imag], 0)


def tables():
    col = np.arange(cols_n)
    x_l = np.arange(cells)
    k1x = np.arange(64)
    k2x = (2 * np.arange(32)[None, :] + np.arange(2)[:, None]).reshape(-1)
    kappa = (4 * col[None, :] + np.arange(4)[:, None]).reshape(-1)

    gather, expand = row_transform(modes - 1)
    y_gather = deep(parts(gather))
    y_expand = tall(parts(expand[kappa]))
    gather, expand = row_transform(modes)
    z_gather = deep(parts(gather[:, kappa]))
    z_expand = tall(parts(expand))

    cos, sin = wave(k1x, col, 64)
    x_first = thick(np.concatenate([cos, sin], 0))
    x_back = deep(np.concatenate([cos, sin], 0).reshape(2, 64, 32).transpose(2, 0, 1).reshape(32, 128))
    cos, sin = wave(k1x, x_l, length)
    x_twist = np.stack([np.concatenate([cos, cos], 1), np.concatenate([sin, -sin], 1)])
    cos, sin = wave(k2x, x_l, 64)
    x_last = deep(np.concatenate([cos, sin], 1))
    cos, sin = wave(x_l, k2x, 64)
    x_lead = deep(np.concatenate([np.concatenate([cos, sin], 1)] * 2, 0))
    cos, sin = wave(x_l, k1x, length)
    own = np.concatenate([np.concatenate([cos, -cos], 1), np.concatenate([sin, -sin], 1)], 0)
    other = np.concatenate([np.concatenate([-sin, -sin], 1), np.concatenate([cos, cos], 1)], 0)
    x_twists = np.concatenate([x_twist, np.stack([own, other])], 1).astype(np.float32)
    return {
        "y": (y_gather, y_expand),
        "x": (x_first, x_twists, x_last, x_lead, x_back),
        "z": (z_gather, z_expand),
    }


def split(values):
    high = values.astype(bf16)
    low = (values - high.astype(f32)).astype(bf16)
    return high, low


def stacked_product(table, values):
    high, low = split(values)
    return jnp.dot(table, jnp.concatenate([high, high, low], 0), preferred_element_type=f32)


def tall_product(table, values):
    high, low = split(values)
    size = table.shape[0] // 2
    both = jnp.dot(table, high, preferred_element_type=f32)
    rest = jnp.dot(table[:size], low, preferred_element_type=f32)
    return both[:size] + both[size:] + rest


def deep_product(table, values, contract):
    both = jnp.concatenate(split(values), contract)
    dims = (((1,), (contract,)), ((), ()))
    both = lax.dot_general(table, both, dims, preferred_element_type=f32)
    size = table.shape[0] // 2
    return both[:size] + both[size:]


def half_turn(values):
    return pltpu.roll(values, 64, 1)


def lane_index(shape):
    return lax.broadcasted_iota(jnp.int32, shape, len(shape) - 1)


def half_sign(rows):
    return jnp.where(lane_index((rows, 128)) < 64, 1.0, -1.0).astype(f32)


def pack_body(
    magnet_hbm, stiff_hbm, gather_hbm, out_ref, edge_ref, magnet_ref, stiff_ref, gather_ref, sems
):
    copies = [
        pltpu.make_async_copy(magnet_hbm, magnet_ref, sems.at[0]),
        pltpu.make_async_copy(stiff_hbm, stiff_ref, sems.at[1]),
        pltpu.make_async_copy(gather_hbm, gather_ref, sems.at[2]),
    ]
    for copy in copies:
        copy.start()
    for copy in copies:
        copy.wait()
    values = jnp.concatenate([magnet_ref[0], magnet_ref[1], magnet_ref[2]], 0)
    sums = deep_product(gather_ref[...], values, 1)
    size = rows_n * modes
    low = lane_index((size, 128)) < 64
    re, im = sums[:size, :128], sums[size:, :128]
    last = jnp.concatenate([sums[:size, 128:], sums[size:, 128:]], 1)
    blocks = (jnp.where(low, re, half_turn(im)), jnp.where(low, half_turn(re), im), last)
    for a in range(3):
        for r in range(rows_n):
            out_ref[48 * r + 16 * a : 48 * r + 16 * a + 16, :] = blocks[a][16 * r : 16 * r + 16]
    former = jnp.concatenate([magnet_ref[0], magnet_ref[1]], 0).T
    latter = jnp.concatenate([magnet_ref[2], stiff_ref[...]], 0).T
    after = lax.broadcasted_iota(jnp.int32, (rows_n, lanes), 0) > lax.axis_index("row")
    for n, sides in enumerate((former, latter)):
        out_ref[pl.ds(16 * n + 15, rows_n, stride=48), :] = jnp.where(after, sides[127:], sides[:1])
    for a in range(3):
        edge_ref[a : a + 1, :] = magnet_ref[a, :1, :]
        edge_ref[4 + a : 5 + a, :] = magnet_ref[a, cells - 1 :, :]
    edge_ref[3:4, :] = stiff_ref[:1, :]
    edge_ref[7:8, :] = stiff_ref[cells - 1 :, :]


def spread_kern(kern_ref):
    low = lane_index((32, 128)) < 64
    spread = []
    for j in range(6):
        spread.append([])
        for k in range(4):
            part = kern_ref[pl.ds(128 * j + k, 32, stride=4), :]
            turned = half_turn(part)
            halves = [jnp.where(low, part, turned), jnp.where(low, turned, part)]
            spread[j].append(jnp.concatenate(halves, 0))
    return spread


def chunk_blocks(in_ref):
    columns = []
    for a in range(3):
        block = [in_ref[48 * r + 16 * a : 48 * r + 16 * a + 16, :] for r in range(rows_n)]
        columns.append(jnp.concatenate(block, 0))
    return jnp.concatenate(columns, 1)


def forward_body(in_ref, edge_ref, expand_ref, out_ref):
    sums = tall_product(expand_ref[...], chunk_blocks(in_ref))
    sign = half_sign(128)
    for a in range(3):
        block = sums[:, 128 * a : 128 * a + 128]
        block = block[:128] - half_turn(block[128:]) * sign
        for k in range(4):
            out_ref[pl.ds(4 * a + k, cols_n, stride=16), :] = block[32 * k : 32 * k + 32]
    col = lax.axis_index("col")
    first, last = edge_ref[0:4, :], edge_ref[4:8, :]
    for c in range(cols_n):
        out_ref[16 * c + 12 : 16 * c + 16, :] = jnp.where(c > col, last, first)


def spectral_body(
    in_ref, kern_ref, first_ref, twist_ref, last_ref, lead_ref, back_ref, out_ref
):
    columns = [in_ref[pl.ds(j, cols_n, stride=16), :] for j in range(12)]
    section = stacked_product(first_ref[...], jnp.concatenate(columns, 1))
    sign = half_sign(64)
    own, other = twist_ref[0, :64, :], twist_ref[1, :64, :]
    turned = []
    for j in range(12):
        block = section[:, 128 * j : 128 * j + 128]
        block = block[:64] + half_turn(block[64:]) * sign
        block = block * own + half_turn(block) * other
        turned.append(block)
        turned.append(half_turn(block) * sign)
    freq = deep_product(last_ref[...], jnp.concatenate(turned, 0), 1)
    kern = spread_kern(kern_ref)
    sources = []
    for target in range(3):
        for k in range(4):
            total = None
            for b in range(3):
                j = 4 * b + k
                term = kern[tensor_slots[target][b]][k] * freq[:, 128 * j : 128 * j + 128]
                total = term if total is None else total + term
            sources.append(jnp.concatenate([total, -half_turn(total) * sign], 0))
    section = deep_product(lead_ref[...], jnp.concatenate(sources, 1), 0)
    own, other = twist_ref[0, 64:, :], twist_ref[1, 64:, :]
    turned = []
    for j in range(12):
        block = section[:, 128 * j : 128 * j + 128]
        turned.append(block * own + half_turn(block) * other)
    result = deep_product(back_ref[...], jnp.concatenate(turned, 0), 1)
    scale = -1.0 / (length * length)
    lane = lane_index((cols_n, 128))
    zero_weight = jnp.where(lane < 64, 1.0, 0.0).astype(f32)
    is_zero = jnp.logical_and(lax.axis_index("row") == 0, lax.axis_index("col") == 0)
    for j in range(12):
        block = result[:, 128 * j : 128 * j + 128]
        weight = jnp.full((cols_n, 128), 2.0, f32)
        if j % 4 == 0:
            weight = jnp.where(is_zero, zero_weight, weight)
        out_ref[pl.ds(j, cols_n, stride=12), :] = block * (weight * scale)


def back_body(in_ref, gather_ref, out_ref):
    columns = []
    for a in range(3):
        block = [in_ref[pl.ds(4 * a + k, cols_n, stride=12), :] for k in range(4)]
        columns.append(jnp.concatenate(block, 0))
    sums = deep_product(gather_ref[...], jnp.concatenate(columns, 1), 0)
    size = rows_n * modes
    sign = half_sign(size)
    for a in range(3):
        block = sums[:, 128 * a : 128 * a + 128]
        block = block[:size] + half_turn(block[size:]) * sign
        for r in range(rows_n):
            out_ref[48 * r + 16 * a : 48 * r + 16 * a + 16, :] = block[16 * r : 16 * r + 16]


def cross(former, latter):
    return (
        former[1] * latter[2] - former[2] * latter[1],
        former[2] * latter[0] - former[0] * latter[2],
        former[0] * latter[1] - former[1] * latter[0],
    )


def torque_body(in_ref, magnet_ref, stiff_ref, beside_y_ref, beside_x_ref, expand_ref, out_ref):
    row, col = lax.axis_index("row"), lax.axis_index("col")
    sums = tall_product(expand_ref[...], chunk_blocks(in_ref))
    demag = []
    for a in range(3):
        block = sums[:, 128 * a : 128 * a + 128]
        demag.append(block[:128] + half_turn(block[128:]))
    low = lane_index((128, 128)) < 64
    former = jnp.where(low, demag[0], half_turn(demag[1])).T
    demag = [former[:64], former[64:], demag[2].T[:64]]

    def side(index):
        start = 48 * index
        rows = [beside_y_ref[pl.ds(pl.multiple_of(start + 16 * n + 8, 8), 8), :] for n in range(2)]
        return [block[7:8] for block in rows]

    before_y = side(jnp.maximum(row - 1, 0))
    after_y = side(jnp.minimum(row + 1, rows_n - 1))
    before_x = beside_x_ref[pl.ds(pl.multiple_of(16 * jnp.maximum(col - 1, 0), 16), 16), :]
    after_x = beside_x_ref[pl.ds(pl.multiple_of(16 * jnp.minimum(col + 1, cols_n - 1), 16), 16), :]
    edges = jnp.concatenate(before_y + after_y + [jnp.zeros((124, 128), f32)], 0).T
    stack = [magnet_ref[0], magnet_ref[1], magnet_ref[2], stiff_ref[...]]
    lane = lane_index((cells, 128))
    sub = lax.broadcasted_iota(jnp.int32, (cells, 128), 0)

    def neighbour(n, direction):
        centre = stack[n]
        part = slice(64 * (n % 2), 64 * (n % 2) + 64)
        if direction == 0:
            return jnp.where(sub == cells - 1, after_x[12 + n : 13 + n], pltpu.roll(centre, cells - 1, 0))
        if direction == 1:
            return jnp.where(sub == 0, before_x[12 + n : 13 + n], pltpu.roll(centre, 1, 0))
        if direction == 2:
            edge = edges[part, 2 + n // 2 : 3 + n // 2]
            return jnp.where(lane == 127, edge, pltpu.roll(centre, 127, 1))
        edge = edges[part, n // 2 : n // 2 + 1]
        return jnp.where(lane == 0, edge, pltpu.roll(centre, 1, 1))

    absent = (
        jnp.logical_and(sub == cells - 1, col == cols_n - 1),
        jnp.logical_and(sub == 0, col == 0),
        jnp.logical_and(lane == 127, row == rows_n - 1),
        jnp.logical_and(lane == 0, row == 0),
    )
    exchange = [None] * 3
    for direction in range(4):
        coupling = 0.5 * (stack[3] + neighbour(3, direction))
        coupling = jnp.where(absent[direction], 0.0, coupling)
        for a in range(3):
            term = coupling * (neighbour(a, direction) - stack[a])
            exchange[a] = term if exchange[a] is None else exchange[a] + term
    magnet = stack[:3]
    field = [exchange[a] + demag[a] for a in range(3)]
    field[2] = field[2] + anisotropy * magnet[2]
    first_cross = cross(magnet, field)
    second_cross = cross(magnet, first_cross)
    factor = -1.0 / (1.0 + damping * damping)
    for a in range(3):
        out_ref[a] = (first_cross[a] + damping * second_cross[a]) * factor


in_vmem = pl.BlockSpec(memory_space=pltpu.VMEM)
in_hbm = pl.BlockSpec(memory_space=pltpu.HBM)


def call(body, out_shapes, *args, scratch=(), in_spec=in_vmem, vmem=32 * 2**20, flops=10**8):
    shapes = [jax.ShapeDtypeStruct(shape, f32) for shape in out_shapes]
    return pl.pallas_call(
        body,
        out_shape=shapes,
        in_specs=[in_spec] * len(args),
        out_specs=[in_vmem] * len(shapes),
        scratch_shapes=list(scratch),
        compiler_params=pltpu.CompilerParams(vmem_limit_bytes=vmem),
        cost_estimate=pl.CostEstimate(flops=flops, bytes_accessed=10**6, transcendentals=0),
    )(*args)


def exchange(array, axis, chunks):
    shape = array.shape
    rows = shape[0] // chunks
    tile = math.gcd(rows, 8)
    array = array.reshape(chunks, rows // tile, tile, shape[1])
    return lax.all_to_all(array, axis, split_axis=0, concat_axis=0, tiled=True).reshape(shape)


def local(magnet, stiffness, kern):
    constant = {name: [jnp.asarray(t) for t in group] for name, group in tables().items()}
    packed, edge = call(
        pack_body,
        [(768, 128), (8, 128)],
        magnet,
        stiffness,
        constant["y"][0],
        in_spec=in_hbm,
        vmem=55208 * 2**10,
        scratch=[
            pltpu.VMEM((3, cells, lanes), f32),
            pltpu.VMEM((cells, lanes), f32),
            pltpu.VMEM(constant["y"][0].shape, bf16),
            pltpu.SemaphoreType.DMA((3,)),
        ],
    )
    sums = exchange(packed, "row", rows_n)
    (columns,) = call(forward_body, [(512, 128)], sums, edge, constant["y"][1])
    columns = exchange(columns, "col", cols_n)
    tensor = kern.reshape(6, 4, 32, 128).transpose(0, 2, 1, 3).reshape(768, 128)
    (inverse_x,) = call(spectral_body, [(384, 128)], columns, tensor, *constant["x"])
    inverse_x = exchange(inverse_x, "col", cols_n)
    (coef,) = call(back_body, [(768, 128)], inverse_x, constant["z"][0])
    coef = exchange(coef, "row", rows_n)
    (torque,) = call(
        torque_body, [(3, 64, 128)], coef, magnet, stiffness, sums, columns, constant["z"][1]
    )
    return torque


def solution(mesh):
    in_specs = (P(None, "col", "row"), P("col", "row"), P(None, ("row", "col"), None))
    out_specs = P(None, "col", "row")
    return jax.shard_map(local, mesh=mesh, in_specs=in_specs, out_specs=out_specs, check_vma=False)
```

```python
import math

import jax
import jax.numpy as jnp
import ml_dtypes
import numpy as np
from jax import lax
from jax.experimental import pallas as pl
from jax.experimental.pallas import tpu as pltpu
from jax.sharding import PartitionSpec as P

damping = 0.3
anisotropy = 0.8
tensor_slots = ((0, 3, 4), (3, 1, 5), (4, 5, 2))

rows_n = 16
cols_n = 32
cells = 64
lanes = 128
length = 4096
bf16 = jnp.bfloat16
f32 = jnp.float32


modes = 15
sums_rows = 3 * modes
halo_rows = sums_rows + 2


def wave(first, second, period):
    angle = 2.0 * math.pi * (np.outer(first, second) % period) / period
    return np.cos(angle), np.sin(angle)


def split_table(table):
    high = table.astype(ml_dtypes.bfloat16)
    low = (table - high.astype(np.float64)).astype(ml_dtypes.bfloat16)
    return high, low


def thick(table):
    high, low = split_table(table)
    return np.concatenate([high, low, high], 1)


def tall(table):
    return np.concatenate(split_table(table), 0)


def deep(table):
    high, low = split_table(table)
    return np.concatenate(
        [np.concatenate([high, high], 1), np.concatenate([low, np.zeros_like(low)], 1)], 0
    )


def factors(count):
    place = np.arange(lanes) - 0.5 * (lanes - 1)
    angle = 2.0 * math.pi * np.outer(place, place) / length
    values, vectors, units = [], [], []
    for part, unit in ((np.cos(angle), 1.0), (np.sin(angle), -1j)):
        value, vector = np.linalg.eigh(part)
        values.append(value)
        vectors.append(vector * np.where(vector[-1] < 0.0, -1.0, 1.0))
        units.append(np.full(lanes, unit))
    values, vectors = np.concatenate(values), np.concatenate(vectors, 1)
    units = np.concatenate(units)
    kept = np.argsort(-np.abs(values), kind="stable")[:count]
    side = vectors[:, kept] * np.sqrt(np.abs(values[kept]))
    weight = units[kept] * np.sign(values[kept])
    return side, weight


def row_transform():
    side, weight = factors(modes)
    place = np.arange(lanes) - 0.5 * (lanes - 1)
    centre = lanes * np.arange(rows_n) + 0.5 * (lanes - 1)
    turn = np.exp(-2j * math.pi * np.outer(centre, place) / length)
    offset = 0.5 * (lanes - 1)
    phase = np.exp(-2j * math.pi * np.arange(rows_n) * lanes * offset / length)
    constant = np.exp(-2j * math.pi * offset * offset / length)
    gather = side.T[:, None] * turn[None] * phase[None, :, None]
    expand = (side * weight)[:, :, None] * turn.T[:, None, :] * phase * constant
    return gather.reshape(modes * rows_n, lanes), expand.reshape(lanes, modes * rows_n)


def parts(table):
    return np.concatenate([table.real, table.imag], 0)


def tables():
    col = np.arange(cols_n)
    x_l = np.arange(cells)
    k1x = np.arange(64)
    k2x = (2 * np.arange(32)[None, :] + np.arange(2)[:, None]).reshape(-1)
    kappa = (4 * col[None, :] + np.arange(4)[:, None]).reshape(-1)

    gather, expand = row_transform()
    y_gather = deep(parts(gather))
    y_expand = tall(parts(expand[kappa]))
    z_gather = deep(parts(gather[:, kappa]))
    z_expand = tall(parts(expand))

    cos, sin = wave(k1x, col, 64)
    x_first = thick(np.concatenate([cos, sin], 0))
    x_back = deep(np.concatenate([cos, sin], 0).reshape(2, 64, 32).transpose(2, 0, 1).reshape(32, 128))
    cos, sin = wave(k1x, x_l, length)
    x_twist = np.stack([np.concatenate([cos, cos], 1), np.concatenate([sin, -sin], 1)])
    cos, sin = wave(k2x, x_l, 64)
    x_last = deep(np.concatenate([cos, sin], 1))
    cos, sin = wave(x_l, k2x, 64)
    x_lead = deep(np.concatenate([np.concatenate([cos, sin], 1)] * 2, 0))
    cos, sin = wave(x_l, k1x, length)
    own = np.concatenate([np.concatenate([cos, -cos], 1), np.concatenate([sin, -sin], 1)], 0)
    other = np.concatenate([np.concatenate([-sin, -sin], 1), np.concatenate([cos, cos], 1)], 0)
    x_twists = np.concatenate([x_twist, np.stack([own, other])], 1).astype(np.float32)
    return {
        "y": (y_gather, y_expand),
        "x": (x_first, x_twists, x_last, x_lead, x_back),
        "z": (z_gather, z_expand),
    }


def split(values):
    high = values.astype(bf16)
    low = (values - high.astype(f32)).astype(bf16)
    return high, low


def stacked_product(table, values):
    high, low = split(values)
    return jnp.dot(table, jnp.concatenate([high, high, low], 0), preferred_element_type=f32)


def tall_product(table, values):
    high, low = split(values)
    size = table.shape[0] // 2
    both = jnp.dot(table, high, preferred_element_type=f32)
    rest = jnp.dot(table[:size], low, preferred_element_type=f32)
    return both[:size] + both[size:] + rest


def deep_product(table, values, contract):
    both = jnp.concatenate(split(values), contract)
    dims = (((1,), (contract,)), ((), ()))
    both = lax.dot_general(table, both, dims, preferred_element_type=f32)
    size = table.shape[0] // 2
    return both[:size] + both[size:]


def half_turn(values):
    return pltpu.roll(values, 64, 1)


def lane_index(shape):
    return lax.broadcasted_iota(jnp.int32, shape, len(shape) - 1)


def half_sign(rows):
    return jnp.where(lane_index((rows, 128)) < 64, 1.0, -1.0).astype(f32)


def pack_body(
    magnet_hbm, stiff_hbm, gather_hbm, out_ref, edge_ref, magnet_ref, stiff_ref, gather_ref, sems
):
    copies = [
        pltpu.make_async_copy(magnet_hbm, magnet_ref, sems.at[0]),
        pltpu.make_async_copy(stiff_hbm, stiff_ref, sems.at[1]),
        pltpu.make_async_copy(gather_hbm, gather_ref, sems.at[2]),
    ]
    for copy in copies:
        copy.start()
    for copy in copies:
        copy.wait()
    values = jnp.concatenate([magnet_ref[0], magnet_ref[1], magnet_ref[2]], 0)
    sums = deep_product(gather_ref[...], values, 1)
    size = rows_n * modes
    low = lane_index((size, 128)) < 64
    re, im = sums[:size, :128], sums[size:, :128]
    last = jnp.concatenate([sums[:size, 128:], sums[size:, 128:]], 1)
    blocks = (jnp.where(low, re, half_turn(im)), jnp.where(low, half_turn(re), im), last)
    store_chunks(out_ref, halo_rows, blocks)
    former = jnp.concatenate([magnet_ref[0], magnet_ref[1]], 0).T
    latter = jnp.concatenate([magnet_ref[2], stiff_ref[...]], 0).T
    after = lax.broadcasted_iota(jnp.int32, (rows_n, lanes), 0) > lax.axis_index("row")
    for n, sides in enumerate((former, latter)):
        edges = jnp.where(after, sides[127:], sides[:1])
        out_ref[pl.ds(sums_rows + n, rows_n, stride=halo_rows), :] = edges
    for a in range(3):
        edge_ref[a : a + 1, :] = magnet_ref[a, :1, :]
        edge_ref[4 + a : 5 + a, :] = magnet_ref[a, cells - 1 :, :]
    edge_ref[3:4, :] = stiff_ref[:1, :]
    edge_ref[7:8, :] = stiff_ref[cells - 1 :, :]


def spread_kern(kern_ref):
    low = lane_index((32, 128)) < 64
    spread = []
    for j in range(6):
        spread.append([])
        for k in range(4):
            part = kern_ref[pl.ds(128 * j + k, 32, stride=4), :]
            turned = half_turn(part)
            halves = [jnp.where(low, part, turned), jnp.where(low, turned, part)]
            spread[j].append(jnp.concatenate(halves, 0))
    return spread


def store_chunks(out_ref, rows, blocks):
    for a in range(3):
        for n in range(modes):
            out_ref[pl.ds(modes * a + n, rows_n, stride=rows), :] = blocks[a][
                rows_n * n : rows_n * n + rows_n
            ]


def load_chunks(in_ref, rows):
    columns = []
    for a in range(3):
        block = [in_ref[pl.ds(modes * a + n, rows_n, stride=rows), :] for n in range(modes)]
        columns.append(jnp.concatenate(block, 0))
    return jnp.concatenate(columns, 1)


def forward_body(in_ref, edge_ref, expand_ref, out_ref):
    sums = tall_product(expand_ref[...], load_chunks(in_ref, halo_rows))
    sign = half_sign(128)
    for a in range(3):
        block = sums[:, 128 * a : 128 * a + 128]
        block = block[:128] - half_turn(block[128:]) * sign
        for k in range(4):
            out_ref[pl.ds(4 * a + k, cols_n, stride=16), :] = block[32 * k : 32 * k + 32]
    col = lax.axis_index("col")
    first, last = edge_ref[0:4, :], edge_ref[4:8, :]
    for c in range(cols_n):
        out_ref[16 * c + 12 : 16 * c + 16, :] = jnp.where(c > col, last, first)


def spectral_body(
    in_ref, kern_ref, first_ref, twist_ref, last_ref, lead_ref, back_ref, out_ref
):
    columns = [in_ref[pl.ds(j, cols_n, stride=16), :] for j in range(12)]
    section = stacked_product(first_ref[...], jnp.concatenate(columns, 1))
    sign = half_sign(64)
    own, other = twist_ref[0, :64, :], twist_ref[1, :64, :]
    turned = []
    for j in range(12):
        block = section[:, 128 * j : 128 * j + 128]
        block = block[:64] + half_turn(block[64:]) * sign
        block = block * own + half_turn(block) * other
        turned.append(block)
        turned.append(half_turn(block) * sign)
    freq = deep_product(last_ref[...], jnp.concatenate(turned, 0), 1)
    kern = spread_kern(kern_ref)
    sources = []
    for target in range(3):
        for k in range(4):
            total = None
            for b in range(3):
                j = 4 * b + k
                term = kern[tensor_slots[target][b]][k] * freq[:, 128 * j : 128 * j + 128]
                total = term if total is None else total + term
            sources.append(jnp.concatenate([total, -half_turn(total) * sign], 0))
    section = deep_product(lead_ref[...], jnp.concatenate(sources, 1), 0)
    own, other = twist_ref[0, 64:, :], twist_ref[1, 64:, :]
    turned = []
    for j in range(12):
        block = section[:, 128 * j : 128 * j + 128]
        turned.append(block * own + half_turn(block) * other)
    result = deep_product(back_ref[...], jnp.concatenate(turned, 0), 1)
    scale = -1.0 / (length * length)
    lane = lane_index((cols_n, 128))
    zero_weight = jnp.where(lane < 64, 1.0, 0.0).astype(f32)
    is_zero = jnp.logical_and(lax.axis_index("row") == 0, lax.axis_index("col") == 0)
    for j in range(12):
        block = result[:, 128 * j : 128 * j + 128]
        weight = jnp.full((cols_n, 128), 2.0, f32)
        if j % 4 == 0:
            weight = jnp.where(is_zero, zero_weight, weight)
        out_ref[pl.ds(j, cols_n, stride=12), :] = block * (weight * scale)


def back_body(in_ref, gather_ref, out_ref):
    columns = []
    for a in range(3):
        block = [in_ref[pl.ds(4 * a + k, cols_n, stride=12), :] for k in range(4)]
        columns.append(jnp.concatenate(block, 0))
    sums = deep_product(gather_ref[...], jnp.concatenate(columns, 1), 0)
    size = rows_n * modes
    sign = half_sign(size)
    blocks = []
    for a in range(3):
        block = sums[:, 128 * a : 128 * a + 128]
        blocks.append(block[:size] + half_turn(block[size:]) * sign)
    store_chunks(out_ref, sums_rows, blocks)


def cross(former, latter):
    return (
        former[1] * latter[2] - former[2] * latter[1],
        former[2] * latter[0] - former[0] * latter[2],
        former[0] * latter[1] - former[1] * latter[0],
    )


def torque_body(in_ref, magnet_ref, stiff_ref, beside_y_ref, beside_x_ref, expand_ref, out_ref):
    row, col = lax.axis_index("row"), lax.axis_index("col")
    sums = tall_product(expand_ref[...], load_chunks(in_ref, sums_rows))
    demag = []
    for a in range(3):
        block = sums[:, 128 * a : 128 * a + 128]
        demag.append(block[:128] + half_turn(block[128:]))
    low = lane_index((128, 128)) < 64
    former = jnp.where(low, demag[0], half_turn(demag[1])).T
    demag = [former[:64], former[64:], demag[2].T[:64]]

    start = halo_rows * jnp.maximum(row - 1, 0) + sums_rows
    before_y = beside_y_ref[pl.ds(start, 2), :]
    start = halo_rows * jnp.minimum(row + 1, rows_n - 1) + sums_rows
    after_y = beside_y_ref[pl.ds(start, 2), :]
    before_x = beside_x_ref[pl.ds(pl.multiple_of(16 * jnp.maximum(col - 1, 0), 16), 16), :]
    after_x = beside_x_ref[pl.ds(pl.multiple_of(16 * jnp.minimum(col + 1, cols_n - 1), 16), 16), :]
    edges = jnp.concatenate([before_y, after_y, jnp.zeros((124, 128), f32)], 0).T
    stack = [magnet_ref[0], magnet_ref[1], magnet_ref[2], stiff_ref[...]]
    lane = lane_index((cells, 128))
    sub = lax.broadcasted_iota(jnp.int32, (cells, 128), 0)

    def neighbour(n, direction):
        centre = stack[n]
        part = slice(64 * (n % 2), 64 * (n % 2) + 64)
        if direction == 0:
            return jnp.where(sub == cells - 1, after_x[12 + n : 13 + n], pltpu.roll(centre, cells - 1, 0))
        if direction == 1:
            return jnp.where(sub == 0, before_x[12 + n : 13 + n], pltpu.roll(centre, 1, 0))
        if direction == 2:
            edge = edges[part, 2 + n // 2 : 3 + n // 2]
            return jnp.where(lane == 127, edge, pltpu.roll(centre, 127, 1))
        edge = edges[part, n // 2 : n // 2 + 1]
        return jnp.where(lane == 0, edge, pltpu.roll(centre, 1, 1))

    absent = (
        jnp.logical_and(sub == cells - 1, col == cols_n - 1),
        jnp.logical_and(sub == 0, col == 0),
        jnp.logical_and(lane == 127, row == rows_n - 1),
        jnp.logical_and(lane == 0, row == 0),
    )
    exchange = [None] * 3
    for direction in range(4):
        coupling = 0.5 * (stack[3] + neighbour(3, direction))
        coupling = jnp.where(absent[direction], 0.0, coupling)
        for a in range(3):
            term = coupling * (neighbour(a, direction) - stack[a])
            exchange[a] = term if exchange[a] is None else exchange[a] + term
    magnet = stack[:3]
    field = [exchange[a] + demag[a] for a in range(3)]
    field[2] = field[2] + anisotropy * magnet[2]
    first_cross = cross(magnet, field)
    second_cross = cross(magnet, first_cross)
    factor = -1.0 / (1.0 + damping * damping)
    for a in range(3):
        out_ref[a] = (first_cross[a] + damping * second_cross[a]) * factor


in_vmem = pl.BlockSpec(memory_space=pltpu.VMEM)
in_hbm = pl.BlockSpec(memory_space=pltpu.HBM)


def call(body, out_shapes, *args, scratch=(), in_spec=in_vmem, vmem=32 * 2**20, flops=10**8):
    shapes = [jax.ShapeDtypeStruct(shape, f32) for shape in out_shapes]
    return pl.pallas_call(
        body,
        out_shape=shapes,
        in_specs=[in_spec] * len(args),
        out_specs=[in_vmem] * len(shapes),
        scratch_shapes=list(scratch),
        compiler_params=pltpu.CompilerParams(vmem_limit_bytes=vmem),
        cost_estimate=pl.CostEstimate(flops=flops, bytes_accessed=10**6, transcendentals=0),
    )(*args)


def exchange(array, axis, chunks):
    shape = array.shape
    rows = shape[0] // chunks
    tile = math.gcd(rows, 8)
    array = array.reshape(chunks, rows // tile, tile, shape[1])
    return lax.all_to_all(array, axis, split_axis=0, concat_axis=0, tiled=True).reshape(shape)


def local(magnet, stiffness, kern):
    constant = {name: [jnp.asarray(t) for t in group] for name, group in tables().items()}
    packed, edge = call(
        pack_body,
        [(rows_n * halo_rows, 128), (8, 128)],
        magnet,
        stiffness,
        constant["y"][0],
        in_spec=in_hbm,
        vmem=55208 * 2**10,
        scratch=[
            pltpu.VMEM((3, cells, lanes), f32),
            pltpu.VMEM((cells, lanes), f32),
            pltpu.VMEM(constant["y"][0].shape, bf16),
            pltpu.SemaphoreType.DMA((3,)),
        ],
    )
    sums = exchange(packed, "row", rows_n)
    (columns,) = call(forward_body, [(512, 128)], sums, edge, constant["y"][1])
    columns = exchange(columns, "col", cols_n)
    tensor = kern.reshape(6, 4, 32, 128).transpose(0, 2, 1, 3).reshape(768, 128)
    (inverse_x,) = call(spectral_body, [(384, 128)], columns, tensor, *constant["x"])
    inverse_x = exchange(inverse_x, "col", cols_n)
    (coef,) = call(back_body, [(rows_n * sums_rows, 128)], inverse_x, constant["z"][0])
    coef = exchange(coef, "row", rows_n)
    (torque,) = call(
        torque_body, [(3, 64, 128)], coef, magnet, stiffness, sums, columns, constant["z"][1]
    )
    return torque


def solution(mesh):
    in_specs = (P(None, "col", "row"), P("col", "row"), P(None, ("row", "col"), None))
    out_specs = P(None, "col", "row")
    return jax.shard_map(local, mesh=mesh, in_specs=in_specs, out_specs=out_specs, check_vma=False)
```

```python
import math

import jax
import jax.numpy as jnp
import ml_dtypes
import numpy as np
from jax import lax
from jax.experimental import pallas as pl
from jax.experimental.pallas import tpu as pltpu
from jax.sharding import PartitionSpec as P

damping = 0.3
anisotropy = 0.8
tensor_slots = ((0, 3, 4), (3, 1, 5), (4, 5, 2))

rows_n = 16
cols_n = 32
cells = 64
lanes = 128
length = 4096
bf16 = jnp.bfloat16
f32 = jnp.float32


modes = 14
sums_rows = 3 * modes
halo_rows = sums_rows + 2


def wave(first, second, period):
    angle = 2.0 * math.pi * (np.outer(first, second) % period) / period
    return np.cos(angle), np.sin(angle)


def split_table(table):
    high = table.astype(ml_dtypes.bfloat16)
    low = (table - high.astype(np.float64)).astype(ml_dtypes.bfloat16)
    return high, low


def thick(table):
    high, low = split_table(table)
    return np.concatenate([high, low, high], 1)


def tall(table):
    return np.concatenate(split_table(table), 0)


def deep(table):
    high, low = split_table(table)
    return np.concatenate(
        [np.concatenate([high, high], 1), np.concatenate([low, np.zeros_like(low)], 1)], 0
    )


def factors():
    place = np.arange(lanes) - 0.5 * (lanes - 1)
    angle = 2.0 * math.pi * np.outer(place, place) / length
    level = (1.02 - (2.0 * place / lanes) ** 2) ** -0.3
    values, vectors, units = [], [], []
    for part, unit in ((np.cos(angle), 1.0), (np.sin(angle), -1j)):
        value, vector = np.linalg.eigh(part * np.outer(level, level))
        values.append(value)
        vectors.append(vector * np.where(vector[-1] < 0.0, -1.0, 1.0))
        units.append(np.full(lanes, unit))
    values, vectors = np.concatenate(values), np.concatenate(vectors, 1)
    units = np.concatenate(units)
    kept = np.argsort(-np.abs(values), kind="stable")[:modes]
    side = vectors[:, kept] * np.sqrt(np.abs(values[kept])) / level[:, None]
    return side, units[kept] * np.sign(values[kept])


def row_transform():
    side, weight = factors()
    place = np.arange(lanes) - 0.5 * (lanes - 1)
    centre = lanes * np.arange(rows_n) + 0.5 * (lanes - 1)
    turn = np.exp(-2j * math.pi * np.outer(centre, place) / length)
    offset = 0.5 * (lanes - 1)
    phase = np.exp(-2j * math.pi * np.arange(rows_n) * lanes * offset / length)
    constant = np.exp(-2j * math.pi * offset * offset / length)
    turns = turn * phase[:, None]
    gather = side.T[:, None] * turns[None]
    expand = (side * weight)[:, :, None] * turn.T[:, None, :] * phase * constant
    gather, expand = gather.reshape(-1, lanes), expand.reshape(lanes, -1)
    return side.T, turns, gather, expand


def parts(table):
    return np.concatenate([table.real, table.imag], 0)


def tables():
    col = np.arange(cols_n)
    x_l = np.arange(cells)
    k1x = np.arange(64)
    k2x = (2 * np.arange(32)[None, :] + np.arange(2)[:, None]).reshape(-1)
    kappa = (4 * col[None, :] + np.arange(4)[:, None]).reshape(-1)

    sides, turns, gather, expand = row_transform()
    y_gather = np.concatenate([parts(turns), sides], 0).astype(np.float32)
    y_expand = tall(parts(expand[kappa]))
    z_gather = deep(parts(gather[:, kappa]))
    z_expand = tall(parts(expand))

    cos, sin = wave(k1x, col, 64)
    x_first = thick(np.concatenate([cos, sin], 0))
    x_back = deep(np.concatenate([cos, sin], 0).reshape(2, 64, 32).transpose(2, 0, 1).reshape(32, 128))
    cos, sin = wave(k1x, x_l, length)
    x_twist = np.stack([np.concatenate([cos, cos], 1), np.concatenate([sin, -sin], 1)])
    cos, sin = wave(k2x, x_l, 64)
    x_last = deep(np.concatenate([cos, sin], 1))
    cos, sin = wave(x_l, k2x, 64)
    x_lead = deep(np.concatenate([np.concatenate([cos, sin], 1)] * 2, 0))
    cos, sin = wave(x_l, k1x, length)
    own = np.concatenate([np.concatenate([cos, -cos], 1), np.concatenate([sin, -sin], 1)], 0)
    other = np.concatenate([np.concatenate([-sin, -sin], 1), np.concatenate([cos, cos], 1)], 0)
    x_twists = np.concatenate([x_twist, np.stack([own, other])], 1).astype(np.float32)
    return {
        "y": (y_gather, y_expand),
        "x": (x_first, x_twists, x_last, x_lead, x_back),
        "z": (z_gather, z_expand),
    }


def split(values):
    high = values.astype(bf16)
    low = (values - high.astype(f32)).astype(bf16)
    return high, low


def stacked_product(table, values):
    high, low = split(values)
    return jnp.dot(table, jnp.concatenate([high, high, low], 0), preferred_element_type=f32)


def tall_product(table, values):
    high, low = split(values)
    size = table.shape[0] // 2
    both = jnp.dot(table, high, preferred_element_type=f32)
    rest = jnp.dot(table[:size], low, preferred_element_type=f32)
    return both[:size] + both[size:] + rest


def deep_product(table, values, contract):
    both = jnp.concatenate(split(values), contract)
    dims = (((1,), (contract,)), ((), ()))
    both = lax.dot_general(table, both, dims, preferred_element_type=f32)
    size = table.shape[0] // 2
    return both[:size] + both[size:]


def last_dims_product(former, latter):
    dims = (((1,), (1,)), ((), ()))
    return lax.dot_general(former, latter, dims, preferred_element_type=f32)


def half_turn(values):
    return pltpu.roll(values, 64, 1)


def lane_index(shape):
    return lax.broadcasted_iota(jnp.int32, shape, len(shape) - 1)


def half_sign(rows):
    return jnp.where(lane_index((rows, 128)) < 64, 1.0, -1.0).astype(f32)


def pack_body(
    magnet_hbm, stiff_hbm, gather_hbm, out_ref, edge_ref, magnet_ref, stiff_ref, gather_ref, sems
):
    copies = [
        pltpu.make_async_copy(magnet_hbm, magnet_ref, sems.at[0]),
        pltpu.make_async_copy(stiff_hbm, stiff_ref, sems.at[1]),
        pltpu.make_async_copy(gather_hbm, gather_ref, sems.at[2]),
    ]
    for copy in copies:
        copy.start()
    for copy in copies:
        copy.wait()
    values = jnp.concatenate([magnet_ref[0], magnet_ref[1], magnet_ref[2]], 0)
    size = rows_n * modes
    turns = gather_ref[0 : 2 * rows_n, :]
    sides = [gather_ref[2 * rows_n + n : 2 * rows_n + n + 1, :] for n in range(modes)]
    re = [turns[:rows_n] * side for side in sides]
    im = [turns[rows_n:] * side for side in sides]
    table_high, table_low = split(jnp.concatenate(re + im, 0))
    high, low = split(values)
    sums = last_dims_product(
        jnp.concatenate([table_high, table_high], 1), jnp.concatenate([high, low], 1)
    ) + last_dims_product(table_low, high)
    low = lane_index((size, 128)) < 64
    re, im = sums[:size, :128], sums[size:, :128]
    last = jnp.concatenate([sums[:size, 128:], sums[size:, 128:]], 1)
    blocks = (jnp.where(low, re, half_turn(im)), jnp.where(low, half_turn(re), im), last)
    store_chunks(out_ref, halo_rows, blocks)
    former = jnp.concatenate([magnet_ref[0], magnet_ref[1]], 0).T
    latter = jnp.concatenate([magnet_ref[2], stiff_ref[...]], 0).T
    after = lax.broadcasted_iota(jnp.int32, (rows_n, lanes), 0) > lax.axis_index("row")
    for n, sides in enumerate((former, latter)):
        edges = jnp.where(after, sides[127:], sides[:1])
        out_ref[pl.ds(sums_rows + n, rows_n, stride=halo_rows), :] = edges
    for a in range(3):
        edge_ref[a : a + 1, :] = magnet_ref[a, :1, :]
        edge_ref[4 + a : 5 + a, :] = magnet_ref[a, cells - 1 :, :]
    edge_ref[3:4, :] = stiff_ref[:1, :]
    edge_ref[7:8, :] = stiff_ref[cells - 1 :, :]


def spread_kern(kern_ref):
    low = lane_index((32, 128)) < 64
    spread = []
    for j in range(6):
        spread.append([])
        for k in range(4):
            part = kern_ref[pl.ds(128 * j + k, 32, stride=4), :]
            turned = half_turn(part)
            halves = [jnp.where(low, part, turned), jnp.where(low, turned, part)]
            spread[j].append(jnp.concatenate(halves, 0))
    return spread


def store_chunks(out_ref, rows, blocks):
    for a in range(3):
        for n in range(modes):
            out_ref[pl.ds(modes * a + n, rows_n, stride=rows), :] = blocks[a][
                rows_n * n : rows_n * n + rows_n
            ]


def load_chunks(in_ref, rows):
    columns = []
    for a in range(3):
        block = [in_ref[pl.ds(modes * a + n, rows_n, stride=rows), :] for n in range(modes)]
        columns.append(jnp.concatenate(block, 0))
    return jnp.concatenate(columns, 1)


def forward_body(in_ref, edge_ref, expand_ref, out_ref):
    sums = tall_product(expand_ref[...], load_chunks(in_ref, halo_rows))
    sign = half_sign(128)
    for a in range(3):
        block = sums[:, 128 * a : 128 * a + 128]
        block = block[:128] - half_turn(block[128:]) * sign
        for k in range(4):
            out_ref[pl.ds(4 * a + k, cols_n, stride=16), :] = block[32 * k : 32 * k + 32]
    col = lax.axis_index("col")
    first, last = edge_ref[0:4, :], edge_ref[4:8, :]
    for c in range(cols_n):
        out_ref[16 * c + 12 : 16 * c + 16, :] = jnp.where(c > col, last, first)


def spectral_body(
    in_ref, kern_ref, first_ref, twist_ref, last_ref, lead_ref, back_ref, out_ref
):
    columns = [in_ref[pl.ds(j, cols_n, stride=16), :] for j in range(12)]
    section = stacked_product(first_ref[...], jnp.concatenate(columns, 1))
    sign = half_sign(64)
    own, other = twist_ref[0, :64, :], twist_ref[1, :64, :]
    turned = []
    for j in range(12):
        block = section[:, 128 * j : 128 * j + 128]
        block = block[:64] + half_turn(block[64:]) * sign
        block = block * own + half_turn(block) * other
        turned.append(block)
        turned.append(half_turn(block) * sign)
    freq = deep_product(last_ref[...], jnp.concatenate(turned, 0), 1)
    kern = spread_kern(kern_ref)
    sources = []
    for target in range(3):
        for k in range(4):
            total = None
            for b in range(3):
                j = 4 * b + k
                term = kern[tensor_slots[target][b]][k] * freq[:, 128 * j : 128 * j + 128]
                total = term if total is None else total + term
            sources.append(jnp.concatenate([total, -half_turn(total) * sign], 0))
    section = deep_product(lead_ref[...], jnp.concatenate(sources, 1), 0)
    own, other = twist_ref[0, 64:, :], twist_ref[1, 64:, :]
    turned = []
    for j in range(12):
        block = section[:, 128 * j : 128 * j + 128]
        turned.append(block * own + half_turn(block) * other)
    result = deep_product(back_ref[...], jnp.concatenate(turned, 0), 1)
    scale = -1.0 / (length * length)
    lane = lane_index((cols_n, 128))
    zero_weight = jnp.where(lane < 64, 1.0, 0.0).astype(f32)
    is_zero = jnp.logical_and(lax.axis_index("row") == 0, lax.axis_index("col") == 0)
    for j in range(12):
        block = result[:, 128 * j : 128 * j + 128]
        weight = jnp.full((cols_n, 128), 2.0, f32)
        if j % 4 == 0:
            weight = jnp.where(is_zero, zero_weight, weight)
        out_ref[pl.ds(j, cols_n, stride=12), :] = block * (weight * scale)


def back_body(in_ref, gather_ref, out_ref):
    columns = []
    for a in range(3):
        block = [in_ref[pl.ds(4 * a + k, cols_n, stride=12), :] for k in range(4)]
        columns.append(jnp.concatenate(block, 0))
    sums = deep_product(gather_ref[...], jnp.concatenate(columns, 1), 0)
    size = rows_n * modes
    sign = half_sign(size)
    blocks = []
    for a in range(3):
        block = sums[:, 128 * a : 128 * a + 128]
        blocks.append(block[:size] + half_turn(block[size:]) * sign)
    store_chunks(out_ref, sums_rows, blocks)


def cross(former, latter):
    return (
        former[1] * latter[2] - former[2] * latter[1],
        former[2] * latter[0] - former[0] * latter[2],
        former[0] * latter[1] - former[1] * latter[0],
    )


def torque_body(in_ref, magnet_ref, stiff_ref, beside_y_ref, beside_x_ref, expand_ref, out_ref):
    row, col = lax.axis_index("row"), lax.axis_index("col")
    sums = tall_product(expand_ref[...], load_chunks(in_ref, sums_rows))
    demag = []
    for a in range(3):
        block = sums[:, 128 * a : 128 * a + 128]
        demag.append(block[:128] + half_turn(block[128:]))
    low = lane_index((128, 128)) < 64
    former = jnp.where(low, demag[0], half_turn(demag[1])).T
    demag = [former[:64], former[64:], demag[2].T[:64]]

    start = halo_rows * jnp.maximum(row - 1, 0) + sums_rows
    before_y = beside_y_ref[pl.ds(start, 2), :]
    start = halo_rows * jnp.minimum(row + 1, rows_n - 1) + sums_rows
    after_y = beside_y_ref[pl.ds(start, 2), :]
    before_x = beside_x_ref[pl.ds(pl.multiple_of(16 * jnp.maximum(col - 1, 0), 16), 16), :]
    after_x = beside_x_ref[pl.ds(pl.multiple_of(16 * jnp.minimum(col + 1, cols_n - 1), 16), 16), :]
    edges = jnp.concatenate([before_y, after_y, jnp.zeros((124, 128), f32)], 0).T
    stack = [magnet_ref[0], magnet_ref[1], magnet_ref[2], stiff_ref[...]]
    lane = lane_index((cells, 128))
    sub = lax.broadcasted_iota(jnp.int32, (cells, 128), 0)

    def neighbour(n, direction):
        centre = stack[n]
        part = slice(64 * (n % 2), 64 * (n % 2) + 64)
        if direction == 0:
            return jnp.where(sub == cells - 1, after_x[12 + n : 13 + n], pltpu.roll(centre, cells - 1, 0))
        if direction == 1:
            return jnp.where(sub == 0, before_x[12 + n : 13 + n], pltpu.roll(centre, 1, 0))
        if direction == 2:
            edge = edges[part, 2 + n // 2 : 3 + n // 2]
            return jnp.where(lane == 127, edge, pltpu.roll(centre, 127, 1))
        edge = edges[part, n // 2 : n // 2 + 1]
        return jnp.where(lane == 0, edge, pltpu.roll(centre, 1, 1))

    absent = (
        jnp.logical_and(sub == cells - 1, col == cols_n - 1),
        jnp.logical_and(sub == 0, col == 0),
        jnp.logical_and(lane == 127, row == rows_n - 1),
        jnp.logical_and(lane == 0, row == 0),
    )
    exchange = [None] * 3
    for direction in range(4):
        coupling = 0.5 * (stack[3] + neighbour(3, direction))
        coupling = jnp.where(absent[direction], 0.0, coupling)
        for a in range(3):
            term = coupling * (neighbour(a, direction) - stack[a])
            exchange[a] = term if exchange[a] is None else exchange[a] + term
    magnet = stack[:3]
    field = [exchange[a] + demag[a] for a in range(3)]
    field[2] = field[2] + anisotropy * magnet[2]
    first_cross = cross(magnet, field)
    second_cross = cross(magnet, first_cross)
    factor = -1.0 / (1.0 + damping * damping)
    for a in range(3):
        out_ref[a] = (first_cross[a] + damping * second_cross[a]) * factor


in_vmem = pl.BlockSpec(memory_space=pltpu.VMEM)
in_hbm = pl.BlockSpec(memory_space=pltpu.HBM)


def call(body, out_shapes, *args, scratch=(), in_spec=in_vmem, vmem=32 * 2**20, flops=10**8):
    shapes = [jax.ShapeDtypeStruct(shape, f32) for shape in out_shapes]
    return pl.pallas_call(
        body,
        out_shape=shapes,
        in_specs=[in_spec] * len(args),
        out_specs=[in_vmem] * len(shapes),
        scratch_shapes=list(scratch),
        compiler_params=pltpu.CompilerParams(vmem_limit_bytes=vmem),
        cost_estimate=pl.CostEstimate(flops=flops, bytes_accessed=10**6, transcendentals=0),
    )(*args)


def exchange(array, axis, chunks):
    shape = array.shape
    rows = shape[0] // chunks
    tile = math.gcd(rows, 8)
    array = array.reshape(chunks, rows // tile, tile, shape[1])
    return lax.all_to_all(array, axis, split_axis=0, concat_axis=0, tiled=True).reshape(shape)


def local(magnet, stiffness, kern):
    constant = {name: [jnp.asarray(t) for t in group] for name, group in tables().items()}
    packed, edge = call(
        pack_body,
        [(rows_n * halo_rows, 128), (8, 128)],
        magnet,
        stiffness,
        constant["y"][0],
        in_spec=in_hbm,
        vmem=55208 * 2**10,
        scratch=[
            pltpu.VMEM((3, cells, lanes), f32),
            pltpu.VMEM((cells, lanes), f32),
            pltpu.VMEM(constant["y"][0].shape, f32),
            pltpu.SemaphoreType.DMA((3,)),
        ],
    )
    sums = exchange(packed, "row", rows_n)
    (columns,) = call(forward_body, [(512, 128)], sums, edge, constant["y"][1])
    columns = exchange(columns, "col", cols_n)
    tensor = kern.reshape(6, 4, 32, 128).transpose(0, 2, 1, 3).reshape(768, 128)
    (inverse_x,) = call(spectral_body, [(384, 128)], columns, tensor, *constant["x"])
    inverse_x = exchange(inverse_x, "col", cols_n)
    (coef,) = call(back_body, [(rows_n * sums_rows, 128)], inverse_x, constant["z"][0])
    coef = exchange(coef, "row", rows_n)
    (torque,) = call(
        torque_body, [(3, 64, 128)], coef, magnet, stiffness, sums, columns, constant["z"][1]
    )
    return torque


def solution(mesh):
    in_specs = (P(None, "col", "row"), P("col", "row"), P(None, ("row", "col"), None))
    out_specs = P(None, "col", "row")
    return jax.shard_map(local, mesh=mesh, in_specs=in_specs, out_specs=out_specs, check_vma=False)
```

```python
import math

import jax
import jax.numpy as jnp
import ml_dtypes
import numpy as np
from jax import lax
from jax.experimental import pallas as pl
from jax.experimental.pallas import tpu as pltpu
from jax.sharding import PartitionSpec as P

damping = 0.3
anisotropy = 0.8
tensor_slots = ((0, 3, 4), (3, 1, 5), (4, 5, 2))

rows_n = 16
cols_n = 32
cells = 64
lanes = 128
length = 4096
bf16 = jnp.bfloat16
f32 = jnp.float32


modes = 14
sums_rows = 3 * modes
halo_rows = sums_rows + 2


def wave(first, second, period):
    angle = 2.0 * math.pi * (np.outer(first, second) % period) / period
    return np.cos(angle), np.sin(angle)


def split_table(table):
    high = table.astype(ml_dtypes.bfloat16)
    low = (table - high.astype(np.float64)).astype(ml_dtypes.bfloat16)
    return high, low


def thick(table):
    high, low = split_table(table)
    return np.concatenate([high, low, high], 1)


def tall(table):
    return np.concatenate(split_table(table), 0)


def deep(table):
    high, low = split_table(table)
    return np.concatenate(
        [np.concatenate([high, high], 1), np.concatenate([low, np.zeros_like(low)], 1)], 0
    )


def factors():
    place = np.arange(lanes) - 0.5 * (lanes - 1)
    angle = 2.0 * math.pi * np.outer(place, place) / length
    level = (1.02 - (2.0 * place / lanes) ** 2) ** -0.3
    values, vectors, units = [], [], []
    for part, unit in ((np.cos(angle), 1.0), (np.sin(angle), -1j)):
        value, vector = np.linalg.eigh(part * np.outer(level, level))
        values.append(value)
        vectors.append(vector * np.where(vector[-1] < 0.0, -1.0, 1.0))
        units.append(np.full(lanes, unit))
    values, vectors = np.concatenate(values), np.concatenate(vectors, 1)
    units = np.concatenate(units)
    kept = np.argsort(-np.abs(values), kind="stable")[:modes]
    side = vectors[:, kept] * np.sqrt(np.abs(values[kept])) / level[:, None]
    return side, units[kept] * np.sign(values[kept])


def row_transform():
    side, weight = factors()
    place = np.arange(lanes) - 0.5 * (lanes - 1)
    centre = lanes * np.arange(rows_n) + 0.5 * (lanes - 1)
    turn = np.exp(-2j * math.pi * np.outer(centre, place) / length)
    offset = 0.5 * (lanes - 1)
    phase = np.exp(-2j * math.pi * np.arange(rows_n) * lanes * offset / length)
    constant = np.exp(-2j * math.pi * offset * offset / length)
    turns = turn * phase[:, None]
    gather = side.T[:, None] * turns[None]
    expand = (side * weight)[:, :, None] * turn.T[:, None, :] * phase * constant
    gather, expand = gather.reshape(-1, lanes), expand.reshape(lanes, -1)
    return side.T, turns, gather, expand


def parts(table):
    return np.concatenate([table.real, table.imag], 0)


def tables():
    col = np.arange(cols_n)
    x_l = np.arange(cells)
    k1x = np.arange(64)
    k2x = (2 * np.arange(32)[None, :] + np.arange(2)[:, None]).reshape(-1)
    kappa = (4 * col[None, :] + np.arange(4)[:, None]).reshape(-1)

    sides, turns, gather, expand = row_transform()
    y_gather = np.concatenate([parts(turns), sides], 0).astype(np.float32)
    y_expand = tall(parts(expand[kappa]))
    z_gather = deep(parts(gather[:, kappa]))
    z_expand = tall(parts(expand))

    cos, sin = wave(k1x, col, 64)
    x_first = thick(np.concatenate([cos, sin], 0))
    x_back = deep(np.concatenate([cos, sin], 0).reshape(2, 64, 32).transpose(2, 0, 1).reshape(32, 128))
    cos, sin = wave(k1x, x_l, length)
    x_twist = np.stack([np.concatenate([cos, cos], 1), np.concatenate([sin, -sin], 1)])
    cos, sin = wave(k2x, x_l, 64)
    x_last = deep(np.concatenate([cos, sin], 1))
    cos, sin = wave(x_l, k2x, 64)
    x_lead = deep(np.concatenate([cos, sin], 1))
    cos, sin = wave(x_l, k1x, length)
    own = [np.concatenate([cos, -cos], 1), np.concatenate([sin, -sin], 1)]
    other = [np.concatenate([-sin, -sin], 1), np.concatenate([cos, cos], 1)]
    x_twists = np.concatenate([x_twist, np.stack(own + other)], 0).astype(np.float32)
    return {
        "y": (y_gather, y_expand),
        "x": (x_first, x_twists, x_last, x_lead, x_back),
        "z": (z_gather, z_expand),
    }


def split(values):
    high = values.astype(bf16)
    low = (values - high.astype(f32)).astype(bf16)
    return high, low


def stacked_product(table, values):
    high, low = split(values)
    return jnp.dot(table, jnp.concatenate([high, high, low], 0), preferred_element_type=f32)


def tall_product(table, values):
    high, low = split(values)
    size = table.shape[0] // 2
    both = jnp.dot(table, high, preferred_element_type=f32)
    rest = jnp.dot(table[:size], low, preferred_element_type=f32)
    return both[:size] + both[size:] + rest


def deep_product(table, values, contract):
    both = jnp.concatenate(split(values), contract)
    dims = (((1,), (contract,)), ((), ()))
    both = lax.dot_general(table, both, dims, preferred_element_type=f32)
    size = table.shape[0] // 2
    return both[:size] + both[size:]


def last_dims_product(former, latter):
    dims = (((1,), (1,)), ((), ()))
    return lax.dot_general(former, latter, dims, preferred_element_type=f32)


def half_turn(values):
    return pltpu.roll(values, 64, 1)


def lane_index(shape):
    return lax.broadcasted_iota(jnp.int32, shape, len(shape) - 1)


def half_sign(rows):
    return jnp.where(lane_index((rows, 128)) < 64, 1.0, -1.0).astype(f32)


def pack_body(
    magnet_hbm, stiff_hbm, gather_hbm, out_ref, edge_ref, magnet_ref, stiff_ref, gather_ref, sems
):
    copies = [
        pltpu.make_async_copy(magnet_hbm, magnet_ref, sems.at[0]),
        pltpu.make_async_copy(stiff_hbm, stiff_ref, sems.at[1]),
        pltpu.make_async_copy(gather_hbm, gather_ref, sems.at[2]),
    ]
    for copy in copies:
        copy.start()
    for copy in copies:
        copy.wait()
    values = jnp.concatenate([magnet_ref[0], magnet_ref[1], magnet_ref[2]], 0)
    size = rows_n * modes
    turns = gather_ref[0 : 2 * rows_n, :]
    sides = [gather_ref[2 * rows_n + n : 2 * rows_n + n + 1, :] for n in range(modes)]
    re = [turns[:rows_n] * side for side in sides]
    im = [turns[rows_n:] * side for side in sides]
    table_high, table_low = split(jnp.concatenate(re + im, 0))
    high, low = split(values)
    sums = last_dims_product(
        jnp.concatenate([table_high, table_high], 1), jnp.concatenate([high, low], 1)
    ) + last_dims_product(table_low, high)
    low = lane_index((size, 128)) < 64
    re, im = sums[:size, :128], sums[size:, :128]
    last = jnp.concatenate([sums[:size, 128:], sums[size:, 128:]], 1)
    blocks = (jnp.where(low, re, half_turn(im)), jnp.where(low, half_turn(re), im), last)
    store_chunks(out_ref, halo_rows, blocks)
    former = jnp.concatenate([magnet_ref[0], magnet_ref[1]], 0).T
    latter = jnp.concatenate([magnet_ref[2], stiff_ref[...]], 0).T
    after = lax.broadcasted_iota(jnp.int32, (rows_n, lanes), 0) > lax.axis_index("row")
    for n, sides in enumerate((former, latter)):
        edges = jnp.where(after, sides[127:], sides[:1])
        out_ref[pl.ds(sums_rows + n, rows_n, stride=halo_rows), :] = edges
    for a in range(3):
        edge_ref[a : a + 1, :] = magnet_ref[a, :1, :]
        edge_ref[4 + a : 5 + a, :] = magnet_ref[a, cells - 1 :, :]
    edge_ref[3:4, :] = stiff_ref[:1, :]
    edge_ref[7:8, :] = stiff_ref[cells - 1 :, :]


def spread_kern(kern_ref):
    low = lane_index((32, 128)) < 64
    spread = []
    for j in range(6):
        spread.append([])
        for k in range(4):
            part = kern_ref[pl.ds(128 * j + k, 32, stride=4), :]
            turned = half_turn(part)
            halves = [jnp.where(low, part, turned), jnp.where(low, turned, part)]
            spread[j].append(jnp.concatenate(halves, 0))
    return spread


def store_chunks(out_ref, rows, blocks):
    for a in range(3):
        for n in range(modes):
            out_ref[pl.ds(modes * a + n, rows_n, stride=rows), :] = blocks[a][
                rows_n * n : rows_n * n + rows_n
            ]


def load_chunks(in_ref, rows):
    columns = []
    for a in range(3):
        block = [in_ref[pl.ds(modes * a + n, rows_n, stride=rows), :] for n in range(modes)]
        columns.append(jnp.concatenate(block, 0))
    return jnp.concatenate(columns, 1)


def forward_body(in_ref, edge_ref, expand_ref, out_ref):
    sums = tall_product(expand_ref[...], load_chunks(in_ref, halo_rows))
    sign = half_sign(128)
    for a in range(3):
        block = sums[:, 128 * a : 128 * a + 128]
        block = block[:128] - half_turn(block[128:]) * sign
        for k in range(4):
            out_ref[pl.ds(4 * a + k, cols_n, stride=16), :] = block[32 * k : 32 * k + 32]
    col = lax.axis_index("col")
    first, last = edge_ref[0:4, :], edge_ref[4:8, :]
    for c in range(cols_n):
        out_ref[16 * c + 12 : 16 * c + 16, :] = jnp.where(c > col, last, first)


def spectral_body(
    in_ref, kern_ref, first_ref, twist_ref, last_ref, lead_ref, back_ref, out_ref
):
    sign = half_sign(64)
    own, other = twist_ref[0], twist_ref[1]
    kern = spread_kern(kern_ref)
    scale = -1.0 / (length * length)
    lane = lane_index((cols_n, 128))
    zero_weight = jnp.where(lane < 64, 1.0, 0.0).astype(f32)
    is_zero = jnp.logical_and(lax.axis_index("row") == 0, lax.axis_index("col") == 0)

    def enter(ks):
        columns = [in_ref[pl.ds(4 * a + k, cols_n, stride=16), :] for a in range(3) for k in ks]
        return stacked_product(first_ref[...], jnp.concatenate(columns, 1))

    def spread(section):
        turned = []
        for j in range(section.shape[1] // 128):
            block = section[:, 128 * j : 128 * j + 128]
            block = block[:64] + half_turn(block[64:]) * sign
            block = block * own + half_turn(block) * other
            turned.append(block)
            turned.append(half_turn(block) * sign)
        return deep_product(last_ref[...], jnp.concatenate(turned, 0), 1)

    def multiply(freq, ks):
        sources = []
        for target in range(3):
            for n, k in enumerate(ks):
                total = None
                for b in range(3):
                    j = len(ks) * b + n
                    term = kern[tensor_slots[target][b]][k] * freq[:, 128 * j : 128 * j + 128]
                    total = term if total is None else total + term
                sources.append(jnp.concatenate([total, -half_turn(total) * sign], 0))
        return deep_product(lead_ref[...], jnp.concatenate(sources, 1), 0)

    def leave(section):
        turned = []
        for j in range(section.shape[1] // 128):
            block = section[:, 128 * j : 128 * j + 128]
            aside = half_turn(block)
            turned.append(block * twist_ref[2] + aside * twist_ref[4])
            turned.append(block * twist_ref[3] + aside * twist_ref[5])
        return deep_product(back_ref[...], jnp.concatenate(turned, 0), 1)

    def store(result, ks):
        for a in range(3):
            for n, k in enumerate(ks):
                j = len(ks) * a + n
                block = result[:, 128 * j : 128 * j + 128]
                weight = jnp.full((cols_n, 128), 2.0, f32)
                if k == 0:
                    weight = jnp.where(is_zero, zero_weight, weight)
                out_ref[pl.ds(4 * a + k, cols_n, stride=12), :] = block * (weight * scale)

    groups = ((0,), (1,), (2,), (3,))
    states = [enter(ks) for ks in groups]
    states = [spread(state) for state in states]
    states = [multiply(state, ks) for state, ks in zip(states, groups)]
    states = [leave(state) for state in states]
    for state, ks in zip(states, groups):
        store(state, ks)


def back_body(in_ref, gather_ref, out_ref):
    columns = []
    for a in range(3):
        block = [in_ref[pl.ds(4 * a + k, cols_n, stride=12), :] for k in range(4)]
        columns.append(jnp.concatenate(block, 0))
    sums = deep_product(gather_ref[...], jnp.concatenate(columns, 1), 0)
    size = rows_n * modes
    sign = half_sign(size)
    blocks = []
    for a in range(3):
        block = sums[:, 128 * a : 128 * a + 128]
        blocks.append(block[:size] + half_turn(block[size:]) * sign)
    store_chunks(out_ref, sums_rows, blocks)


def cross(former, latter):
    return (
        former[1] * latter[2] - former[2] * latter[1],
        former[2] * latter[0] - former[0] * latter[2],
        former[0] * latter[1] - former[1] * latter[0],
    )


def torque_body(in_ref, magnet_ref, stiff_ref, beside_y_ref, beside_x_ref, expand_ref, out_ref):
    row, col = lax.axis_index("row"), lax.axis_index("col")
    sums = tall_product(expand_ref[...], load_chunks(in_ref, sums_rows))
    demag = []
    for a in range(3):
        block = sums[:, 128 * a : 128 * a + 128]
        demag.append(block[:128] + half_turn(block[128:]))
    low = lane_index((128, 128)) < 64
    former = jnp.where(low, demag[0], half_turn(demag[1])).T
    demag = [former[:64], former[64:], demag[2].T[:64]]

    device = lax.broadcasted_iota(jnp.int32, (rows_n, 128), 0)

    def side(index):
        rows = []
        for n in range(2):
            halo = beside_y_ref[pl.ds(sums_rows + n, rows_n, stride=halo_rows), :]
            rows.append(jnp.sum(jnp.where(device == index, halo, 0.0), 0, keepdims=True))
        return rows

    before_y, after_y = side(row - 1), side(row + 1)
    before_x = beside_x_ref[pl.ds(pl.multiple_of(16 * jnp.maximum(col - 1, 0), 16), 16), :]
    after_x = beside_x_ref[pl.ds(pl.multiple_of(16 * jnp.minimum(col + 1, cols_n - 1), 16), 16), :]
    edges = jnp.concatenate(before_y + after_y + [jnp.zeros((124, 128), f32)], 0).T
    stack = [magnet_ref[0], magnet_ref[1], magnet_ref[2], stiff_ref[...]]
    lane = lane_index((cells, 128))
    sub = lax.broadcasted_iota(jnp.int32, (cells, 128), 0)

    def neighbour(n, direction):
        centre = stack[n]
        part = slice(64 * (n % 2), 64 * (n % 2) + 64)
        if direction == 0:
            return jnp.where(sub == cells - 1, after_x[12 + n : 13 + n], pltpu.roll(centre, cells - 1, 0))
        if direction == 1:
            return jnp.where(sub == 0, before_x[12 + n : 13 + n], pltpu.roll(centre, 1, 0))
        if direction == 2:
            edge = edges[part, 2 + n // 2 : 3 + n // 2]
            return jnp.where(lane == 127, edge, pltpu.roll(centre, 127, 1))
        edge = edges[part, n // 2 : n // 2 + 1]
        return jnp.where(lane == 0, edge, pltpu.roll(centre, 1, 1))

    absent = (
        jnp.logical_and(sub == cells - 1, col == cols_n - 1),
        jnp.logical_and(sub == 0, col == 0),
        jnp.logical_and(lane == 127, row == rows_n - 1),
        jnp.logical_and(lane == 0, row == 0),
    )
    exchange = [None] * 3
    for direction in range(4):
        coupling = 0.5 * (stack[3] + neighbour(3, direction))
        coupling = jnp.where(absent[direction], 0.0, coupling)
        for a in range(3):
            term = coupling * (neighbour(a, direction) - stack[a])
            exchange[a] = term if exchange[a] is None else exchange[a] + term
    magnet = stack[:3]
    field = [exchange[a] + demag[a] for a in range(3)]
    field[2] = field[2] + anisotropy * magnet[2]
    first_cross = cross(magnet, field)
    second_cross = cross(magnet, first_cross)
    factor = -1.0 / (1.0 + damping * damping)
    for a in range(3):
        out_ref[a] = (first_cross[a] + damping * second_cross[a]) * factor


in_vmem = pl.BlockSpec(memory_space=pltpu.VMEM)
in_hbm = pl.BlockSpec(memory_space=pltpu.HBM)


def call(body, out_shapes, *args, scratch=(), in_spec=in_vmem, vmem=32 * 2**20, flops=10**8):
    shapes = [jax.ShapeDtypeStruct(shape, f32) for shape in out_shapes]
    return pl.pallas_call(
        body,
        out_shape=shapes,
        in_specs=[in_spec] * len(args),
        out_specs=[in_vmem] * len(shapes),
        scratch_shapes=list(scratch),
        compiler_params=pltpu.CompilerParams(vmem_limit_bytes=vmem),
        cost_estimate=pl.CostEstimate(flops=flops, bytes_accessed=10**6, transcendentals=0),
    )(*args)


def exchange(array, axis, chunks):
    shape = array.shape
    rows = shape[0] // chunks
    tile = math.gcd(rows, 8)
    array = array.reshape(chunks, rows // tile, tile, shape[1])
    return lax.all_to_all(array, axis, split_axis=0, concat_axis=0, tiled=True).reshape(shape)


def local(magnet, stiffness, kern):
    constant = {name: [jnp.asarray(t) for t in group] for name, group in tables().items()}
    packed, edge = call(
        pack_body,
        [(rows_n * halo_rows, 128), (8, 128)],
        magnet,
        stiffness,
        constant["y"][0],
        in_spec=in_hbm,
        vmem=55208 * 2**10,
        scratch=[
            pltpu.VMEM((3, cells, lanes), f32),
            pltpu.VMEM((cells, lanes), f32),
            pltpu.VMEM(constant["y"][0].shape, f32),
            pltpu.SemaphoreType.DMA((3,)),
        ],
    )
    sums = exchange(packed, "row", rows_n)
    (columns,) = call(forward_body, [(512, 128)], sums, edge, constant["y"][1])
    columns = exchange(columns, "col", cols_n)
    tensor = kern.reshape(6, 4, 32, 128).transpose(0, 2, 1, 3).reshape(768, 128)
    (inverse_x,) = call(spectral_body, [(384, 128)], columns, tensor, *constant["x"])
    inverse_x = exchange(inverse_x, "col", cols_n)
    (coef,) = call(back_body, [(rows_n * sums_rows, 128)], inverse_x, constant["z"][0])
    coef = exchange(coef, "row", rows_n)
    (torque,) = call(
        torque_body, [(3, 64, 128)], coef, magnet, stiffness, sums, columns, constant["z"][1]
    )
    return torque


def solution(mesh):
    in_specs = (P(None, "col", "row"), P("col", "row"), P(None, ("row", "col"), None))
    out_specs = P(None, "col", "row")
    return jax.shard_map(local, mesh=mesh, in_specs=in_specs, out_specs=out_specs, check_vma=False)
```

```python
import math

import jax
import jax.numpy as jnp
import ml_dtypes
import numpy as np
from jax import lax
from jax.experimental import pallas as pl
from jax.experimental.pallas import tpu as pltpu
from jax.sharding import PartitionSpec as P

damping = 0.3
anisotropy = 0.8
tensor_slots = ((0, 3, 4), (3, 1, 5), (4, 5, 2))

rows_n = 16
cols_n = 32
cells = 64
lanes = 128
length = 4096
bf16 = jnp.bfloat16
f32 = jnp.float32


modes = 14
sums_rows = 3 * modes
halo_rows = sums_rows + 2


def wave(first, second, period):
    angle = 2.0 * math.pi * (np.outer(first, second) % period) / period
    return np.cos(angle), np.sin(angle)


def split_table(table):
    high = table.astype(ml_dtypes.bfloat16)
    low = (table - high.astype(np.float64)).astype(ml_dtypes.bfloat16)
    return high, low


def thick(table):
    high, low = split_table(table)
    return np.concatenate([high, low, high], 1)


def tall(table):
    return np.concatenate(split_table(table), 0)


def deep(table):
    high, low = split_table(table)
    return np.concatenate(
        [np.concatenate([high, high], 1), np.concatenate([low, np.zeros_like(low)], 1)], 0
    )


def factors():
    place = np.arange(lanes) - 0.5 * (lanes - 1)
    angle = 2.0 * math.pi * np.outer(place, place) / length
    level = (1.02 - (2.0 * place / lanes) ** 2) ** -0.3
    values, vectors, units = [], [], []
    for part, unit in ((np.cos(angle), 1.0), (np.sin(angle), -1j)):
        value, vector = np.linalg.eigh(part * np.outer(level, level))
        values.append(value)
        vectors.append(vector * np.where(vector[-1] < 0.0, -1.0, 1.0))
        units.append(np.full(lanes, unit))
    values, vectors = np.concatenate(values), np.concatenate(vectors, 1)
    units = np.concatenate(units)
    kept = np.argsort(-np.abs(values), kind="stable")[:modes]
    side = vectors[:, kept] * np.sqrt(np.abs(values[kept])) / level[:, None]
    return side, units[kept] * np.sign(values[kept])


def row_transform():
    side, weight = factors()
    place = np.arange(lanes) - 0.5 * (lanes - 1)
    centre = lanes * np.arange(rows_n) + 0.5 * (lanes - 1)
    turn = np.exp(-2j * math.pi * np.outer(centre, place) / length)
    offset = 0.5 * (lanes - 1)
    phase = np.exp(-2j * math.pi * np.arange(rows_n) * lanes * offset / length)
    constant = np.exp(-2j * math.pi * offset * offset / length)
    turns = turn * phase[:, None]
    gather = side.T[:, None] * turns[None]
    expand = (side * weight)[:, :, None] * turn.T[:, None, :] * phase * constant
    gather, expand = gather.reshape(-1, lanes), expand.reshape(lanes, -1)
    return side.T, turns, gather, expand


def parts(table):
    return np.concatenate([table.real, table.imag], 0)


def tables():
    col = np.arange(cols_n)
    x_l = np.arange(cells)
    k1x = np.arange(64)
    k2x = (2 * np.arange(32)[None, :] + np.arange(2)[:, None]).reshape(-1)
    kappa = (4 * col[None, :] + np.arange(4)[:, None]).reshape(-1)

    sides, turns, gather, expand = row_transform()
    y_gather = np.concatenate([parts(turns), sides], 0).astype(np.float32)
    y_expand = tall(parts(expand[kappa]))
    z_gather = deep(parts(gather[:, kappa]))
    z_expand = tall(parts(expand))

    cos, sin = wave(k1x, col, 64)
    x_first = thick(np.concatenate([cos, sin], 0))
    x_back = deep(np.concatenate([cos, sin], 0).reshape(2, 64, 32).transpose(2, 0, 1).reshape(32, 128))
    cos, sin = wave(k1x, x_l, length)
    x_twist = np.stack([np.concatenate([cos, cos], 1), np.concatenate([sin, -sin], 1)])
    cos, sin = wave(k2x, x_l, 64)
    x_last = deep(np.concatenate([cos, sin], 1))
    cos, sin = wave(x_l, k2x, 64)
    x_lead = deep(np.concatenate([cos, sin], 1))
    cos, sin = wave(x_l, k1x, length)
    own = [np.concatenate([cos, -cos], 1), np.concatenate([sin, -sin], 1)]
    other = [np.concatenate([-sin, -sin], 1), np.concatenate([cos, cos], 1)]
    x_twists = np.concatenate([x_twist, np.stack(own + other)], 0).astype(np.float32)
    return {
        "y": (y_gather, y_expand),
        "x": (x_first, x_twists, x_last, x_lead, x_back),
        "z": (z_gather, z_expand),
    }


def split(values):
    high = values.astype(bf16)
    low = (values - high.astype(f32)).astype(bf16)
    return high, low


def stacked_product(table, values):
    high, low = split(values)
    return jnp.dot(table, jnp.concatenate([high, high, low], 0), preferred_element_type=f32)


def tall_product(table, values):
    high, low = split(values)
    size = table.shape[0] // 2
    both = jnp.dot(table, high, preferred_element_type=f32)
    rest = jnp.dot(table[:size], low, preferred_element_type=f32)
    return both[:size] + both[size:] + rest


def deep_product(table, values, contract):
    both = jnp.concatenate(split(values), contract)
    dims = (((1,), (contract,)), ((), ()))
    both = lax.dot_general(table, both, dims, preferred_element_type=f32)
    size = table.shape[0] // 2
    return both[:size] + both[size:]


def last_dims_product(former, latter):
    dims = (((1,), (1,)), ((), ()))
    return lax.dot_general(former, latter, dims, preferred_element_type=f32)


def half_turn(values):
    return pltpu.roll(values, 64, 1)


def lane_index(shape):
    return lax.broadcasted_iota(jnp.int32, shape, len(shape) - 1)


def half_sign(rows):
    return jnp.where(lane_index((rows, 128)) < 64, 1.0, -1.0).astype(f32)


def pack_body(film_ref, gather_ref, out_ref, edge_ref):
    values = jnp.concatenate([film_ref[a] for a in range(3)], 0)
    size = rows_n * modes
    turns = gather_ref[0 : 2 * rows_n, :]
    sides = [gather_ref[2 * rows_n + n : 2 * rows_n + n + 1, :] for n in range(modes)]
    re = [turns[:rows_n] * side for side in sides]
    im = [turns[rows_n:] * side for side in sides]
    table_high, table_low = split(jnp.concatenate(re + im, 0))
    high, low = split(values)
    sums = last_dims_product(
        jnp.concatenate([table_high, table_high], 1), jnp.concatenate([high, low], 1)
    ) + last_dims_product(table_low, high)
    low = lane_index((size, 128)) < 64
    re, im = sums[:size, :128], sums[size:, :128]
    last = jnp.concatenate([sums[:size, 128:], sums[size:, 128:]], 1)
    blocks = (jnp.where(low, re, half_turn(im)), jnp.where(low, half_turn(re), im), last)
    store_chunks(out_ref, halo_rows, blocks)
    former = jnp.concatenate([film_ref[0], film_ref[1]], 0).T
    latter = jnp.concatenate([film_ref[2], film_ref[3]], 0).T
    after = lax.broadcasted_iota(jnp.int32, (rows_n, lanes), 0) > lax.axis_index("row")
    for n, sides in enumerate((former, latter)):
        edges = jnp.where(after, sides[127:], sides[:1])
        out_ref[pl.ds(sums_rows + n, rows_n, stride=halo_rows), :] = edges
    for n in range(4):
        edge_ref[n : n + 1, :] = film_ref[n, :1, :]
        edge_ref[4 + n : 5 + n, :] = film_ref[n, cells - 1 :, :]


def spread_kern(kern_ref):
    low = lane_index((32, 128)) < 64
    spread = []
    for j in range(6):
        spread.append([])
        for k in range(4):
            part = kern_ref[pl.ds(128 * j + k, 32, stride=4), :]
            turned = half_turn(part)
            halves = [jnp.where(low, part, turned), jnp.where(low, turned, part)]
            spread[j].append(jnp.concatenate(halves, 0))
    return spread


def store_chunks(out_ref, rows, blocks):
    for a in range(3):
        for n in range(modes):
            out_ref[pl.ds(modes * a + n, rows_n, stride=rows), :] = blocks[a][
                rows_n * n : rows_n * n + rows_n
            ]


def load_chunks(in_ref, rows):
    columns = []
    for a in range(3):
        block = [in_ref[pl.ds(modes * a + n, rows_n, stride=rows), :] for n in range(modes)]
        columns.append(jnp.concatenate(block, 0))
    return jnp.concatenate(columns, 1)


def forward_body(in_ref, edge_ref, expand_ref, out_ref):
    sums = tall_product(expand_ref[...], load_chunks(in_ref, halo_rows))
    sign = half_sign(128)
    for a in range(3):
        block = sums[:, 128 * a : 128 * a + 128]
        block = block[:128] - half_turn(block[128:]) * sign
        for k in range(4):
            out_ref[pl.ds(4 * a + k, cols_n, stride=16), :] = block[32 * k : 32 * k + 32]
    col = lax.axis_index("col")
    first, last = edge_ref[0:4, :], edge_ref[4:8, :]
    for c in range(cols_n):
        out_ref[16 * c + 12 : 16 * c + 16, :] = jnp.where(c > col, last, first)


def spectral_body(
    in_ref, kern_ref, first_ref, twist_ref, last_ref, lead_ref, back_ref, out_ref
):
    sign = half_sign(64)
    own, other = twist_ref[0], twist_ref[1]
    kern = spread_kern(kern_ref)
    scale = -1.0 / (length * length)
    lane = lane_index((cols_n, 128))
    zero_weight = jnp.where(lane < 64, 1.0, 0.0).astype(f32)
    is_zero = jnp.logical_and(lax.axis_index("row") == 0, lax.axis_index("col") == 0)

    def enter(ks):
        columns = [in_ref[pl.ds(4 * a + k, cols_n, stride=16), :] for a in range(3) for k in ks]
        return stacked_product(first_ref[...], jnp.concatenate(columns, 1))

    def spread(section):
        turned = []
        for j in range(section.shape[1] // 128):
            block = section[:, 128 * j : 128 * j + 128]
            block = block[:64] + half_turn(block[64:]) * sign
            block = block * own + half_turn(block) * other
            turned.append(block)
            turned.append(half_turn(block) * sign)
        return deep_product(last_ref[...], jnp.concatenate(turned, 0), 1)

    def multiply(freq, ks):
        sources = []
        for target in range(3):
            for n, k in enumerate(ks):
                total = None
                for b in range(3):
                    j = len(ks) * b + n
                    term = kern[tensor_slots[target][b]][k] * freq[:, 128 * j : 128 * j + 128]
                    total = term if total is None else total + term
                sources.append(jnp.concatenate([total, -half_turn(total) * sign], 0))
        return deep_product(lead_ref[...], jnp.concatenate(sources, 1), 0)

    def leave(section):
        turned = []
        for j in range(section.shape[1] // 128):
            block = section[:, 128 * j : 128 * j + 128]
            aside = half_turn(block)
            turned.append(block * twist_ref[2] + aside * twist_ref[4])
            turned.append(block * twist_ref[3] + aside * twist_ref[5])
        return deep_product(back_ref[...], jnp.concatenate(turned, 0), 1)

    def store(result, ks):
        for a in range(3):
            for n, k in enumerate(ks):
                j = len(ks) * a + n
                block = result[:, 128 * j : 128 * j + 128]
                weight = jnp.full((cols_n, 128), 2.0, f32)
                if k == 0:
                    weight = jnp.where(is_zero, zero_weight, weight)
                out_ref[pl.ds(4 * a + k, cols_n, stride=12), :] = block * (weight * scale)

    groups = ((0,), (1,), (2,), (3,))
    states = [enter(ks) for ks in groups]
    states = [spread(state) for state in states]
    states = [multiply(state, ks) for state, ks in zip(states, groups)]
    states = [leave(state) for state in states]
    for state, ks in zip(states, groups):
        store(state, ks)


def back_body(in_ref, gather_ref, out_ref):
    columns = []
    for a in range(3):
        block = [in_ref[pl.ds(4 * a + k, cols_n, stride=12), :] for k in range(4)]
        columns.append(jnp.concatenate(block, 0))
    sums = deep_product(gather_ref[...], jnp.concatenate(columns, 1), 0)
    size = rows_n * modes
    sign = half_sign(size)
    blocks = []
    for a in range(3):
        block = sums[:, 128 * a : 128 * a + 128]
        blocks.append(block[:size] + half_turn(block[size:]) * sign)
    store_chunks(out_ref, sums_rows, blocks)


def cross(former, latter):
    return (
        former[1] * latter[2] - former[2] * latter[1],
        former[2] * latter[0] - former[0] * latter[2],
        former[0] * latter[1] - former[1] * latter[0],
    )


def torque_body(in_ref, film_ref, beside_y_ref, beside_x_ref, expand_ref, out_ref):
    row, col = lax.axis_index("row"), lax.axis_index("col")
    sums = tall_product(expand_ref[...], load_chunks(in_ref, sums_rows))
    demag = []
    for a in range(3):
        block = sums[:, 128 * a : 128 * a + 128]
        demag.append(block[:128] + half_turn(block[128:]))
    low = lane_index((128, 128)) < 64
    former = jnp.where(low, demag[0], half_turn(demag[1])).T
    demag = [former[:64], former[64:], demag[2].T[:64]]

    device = lax.broadcasted_iota(jnp.int32, (rows_n, 128), 0)

    def side(index):
        rows = []
        for n in range(2):
            halo = beside_y_ref[pl.ds(sums_rows + n, rows_n, stride=halo_rows), :]
            rows.append(jnp.sum(jnp.where(device == index, halo, 0.0), 0, keepdims=True))
        return rows

    before_y, after_y = side(row - 1), side(row + 1)
    before_x = beside_x_ref[pl.ds(pl.multiple_of(16 * jnp.maximum(col - 1, 0), 16), 16), :]
    after_x = beside_x_ref[pl.ds(pl.multiple_of(16 * jnp.minimum(col + 1, cols_n - 1), 16), 16), :]
    edges = jnp.concatenate(before_y + after_y + [jnp.zeros((124, 128), f32)], 0).T
    stack = [film_ref[n] for n in range(4)]
    lane = lane_index((cells, 128))
    sub = lax.broadcasted_iota(jnp.int32, (cells, 128), 0)

    def neighbour(n, direction):
        centre = stack[n]
        part = slice(64 * (n % 2), 64 * (n % 2) + 64)
        if direction == 0:
            return jnp.where(sub == cells - 1, after_x[12 + n : 13 + n], pltpu.roll(centre, cells - 1, 0))
        if direction == 1:
            return jnp.where(sub == 0, before_x[12 + n : 13 + n], pltpu.roll(centre, 1, 0))
        if direction == 2:
            edge = edges[part, 2 + n // 2 : 3 + n // 2]
            return jnp.where(lane == 127, edge, pltpu.roll(centre, 127, 1))
        edge = edges[part, n // 2 : n // 2 + 1]
        return jnp.where(lane == 0, edge, pltpu.roll(centre, 1, 1))

    absent = (
        jnp.logical_and(sub == cells - 1, col == cols_n - 1),
        jnp.logical_and(sub == 0, col == 0),
        jnp.logical_and(lane == 127, row == rows_n - 1),
        jnp.logical_and(lane == 0, row == 0),
    )
    exchange = [None] * 3
    for direction in range(4):
        coupling = 0.5 * (stack[3] + neighbour(3, direction))
        coupling = jnp.where(absent[direction], 0.0, coupling)
        for a in range(3):
            term = coupling * (neighbour(a, direction) - stack[a])
            exchange[a] = term if exchange[a] is None else exchange[a] + term
    magnet = stack[:3]
    field = [exchange[a] + demag[a] for a in range(3)]
    field[2] = field[2] + anisotropy * magnet[2]
    first_cross = cross(magnet, field)
    second_cross = cross(magnet, first_cross)
    factor = -1.0 / (1.0 + damping * damping)
    for a in range(3):
        out_ref[a] = (first_cross[a] + damping * second_cross[a]) * factor


in_vmem = pl.BlockSpec(memory_space=pltpu.VMEM)
in_hbm = pl.BlockSpec(memory_space=pltpu.HBM)


def call(body, out_shapes, *args, scratch=(), in_spec=in_vmem, vmem=32 * 2**20, flops=10**8):
    shapes = [jax.ShapeDtypeStruct(shape, f32) for shape in out_shapes]
    return pl.pallas_call(
        body,
        out_shape=shapes,
        in_specs=[in_spec] * len(args),
        out_specs=[in_vmem] * len(shapes),
        scratch_shapes=list(scratch),
        compiler_params=pltpu.CompilerParams(vmem_limit_bytes=vmem),
        cost_estimate=pl.CostEstimate(flops=flops, bytes_accessed=10**6, transcendentals=0),
    )(*args)


def exchange(array, axis, chunks):
    shape = array.shape
    rows = shape[0] // chunks
    tile = math.gcd(rows, 8)
    array = array.reshape(chunks, rows // tile, tile, shape[1])
    return lax.all_to_all(array, axis, split_axis=0, concat_axis=0, tiled=True).reshape(shape)


def local(magnet, stiffness, kern):
    constant = {name: [jnp.asarray(t) for t in group] for name, group in tables().items()}
    film = jnp.concatenate([magnet, stiffness[None]], 0)
    packed, edge = call(
        pack_body, [(rows_n * halo_rows, 128), (8, 128)], film, constant["y"][0]
    )
    sums = exchange(packed, "row", rows_n)
    (columns,) = call(forward_body, [(512, 128)], sums, edge, constant["y"][1])
    columns = exchange(columns, "col", cols_n)
    tensor = kern.reshape(6, 4, 32, 128).transpose(0, 2, 1, 3).reshape(768, 128)
    (inverse_x,) = call(spectral_body, [(384, 128)], columns, tensor, *constant["x"])
    inverse_x = exchange(inverse_x, "col", cols_n)
    (coef,) = call(back_body, [(rows_n * sums_rows, 128)], inverse_x, constant["z"][0])
    coef = exchange(coef, "row", rows_n)
    (torque,) = call(
        torque_body, [(3, 64, 128)], coef, film, sums, columns, constant["z"][1]
    )
    return torque


def solution(mesh):
    in_specs = (P(None, "col", "row"), P("col", "row"), P(None, ("row", "col"), None))
    out_specs = P(None, "col", "row")
    return jax.shard_map(local, mesh=mesh, in_specs=in_specs, out_specs=out_specs, check_vma=False)
```

```python
import math

import jax
import jax.numpy as jnp
import ml_dtypes
import numpy as np
from jax import lax
from jax.experimental import pallas as pl
from jax.experimental.pallas import tpu as pltpu
from jax.sharding import PartitionSpec as P

damping = 0.3
anisotropy = 0.8
tensor_slots = ((0, 3, 4), (3, 1, 5), (4, 5, 2))

rows_n = 16
cols_n = 32
cells = 64
lanes = 128
length = 4096
bf16 = jnp.bfloat16
f32 = jnp.float32


modes = 21
sums_rows = 3 * modes
halo_rows = sums_rows + 2


def wave(first, second, period):
    angle = 2.0 * math.pi * (np.outer(first, second) % period) / period
    return np.cos(angle), np.sin(angle)


def split_table(table):
    high = table.astype(ml_dtypes.bfloat16)
    low = (table - high.astype(np.float64)).astype(ml_dtypes.bfloat16)
    return high, low


def thick(table):
    high, low = split_table(table)
    return np.concatenate([high, low, high], 1)


def tall(table):
    return np.concatenate(split_table(table), 0)


def deep(table):
    high, low = split_table(table)
    return np.concatenate(
        [np.concatenate([high, high], 1), np.concatenate([low, np.zeros_like(low)], 1)], 0
    )


def factors():
    place = np.arange(lanes) - 0.5 * (lanes - 1)
    angle = 2.0 * math.pi * np.outer(place, place) / length
    level = (1.02 - (2.0 * place / lanes) ** 2) ** -0.3
    values, vectors, units = [], [], []
    for part, unit in ((np.cos(angle), 1.0), (np.sin(angle), -1j)):
        value, vector = np.linalg.eigh(part * np.outer(level, level))
        values.append(value)
        vectors.append(vector * np.where(vector[-1] < 0.0, -1.0, 1.0))
        units.append(np.full(lanes, unit))
    values, vectors = np.concatenate(values), np.concatenate(vectors, 1)
    units = np.concatenate(units)
    kept = np.argsort(-np.abs(values), kind="stable")[:modes]
    side = vectors[:, kept] * np.sqrt(np.abs(values[kept])) / level[:, None]
    return side, units[kept] * np.sign(values[kept])


def row_transform():
    side, weight = factors()
    place = np.arange(lanes) - 0.5 * (lanes - 1)
    centre = lanes * np.arange(rows_n) + 0.5 * (lanes - 1)
    turn = np.exp(-2j * math.pi * np.outer(centre, place) / length)
    offset = 0.5 * (lanes - 1)
    phase = np.exp(-2j * math.pi * np.arange(rows_n) * lanes * offset / length)
    constant = np.exp(-2j * math.pi * offset * offset / length)
    turns = turn * phase[:, None]
    gather = side.T[:, None] * turns[None]
    expand = (side * weight)[:, :, None] * turn.T[:, None, :] * phase * constant
    gather, expand = gather.reshape(-1, lanes), expand.reshape(lanes, -1)
    return side.T, turns, gather, expand


def parts(table):
    return np.concatenate([table.real, table.imag], 0)


def tables():
    col = np.arange(cols_n)
    x_l = np.arange(cells)
    k1x = np.arange(64)
    k2x = (2 * np.arange(32)[None, :] + np.arange(2)[:, None]).reshape(-1)
    kappa = (4 * col[None, :] + np.arange(4)[:, None]).reshape(-1)

    sides, turns, gather, expand = row_transform()
    y_gather = np.concatenate([parts(turns), sides], 0).astype(np.float32)
    y_expand = tall(parts(expand[kappa]))
    z_gather = deep(parts(gather[:, kappa]))
    z_expand = tall(parts(expand))

    cos, sin = wave(k1x, col, 64)
    x_first = thick(np.concatenate([cos, sin], 0))
    x_back = deep(np.concatenate([cos, sin], 0).reshape(2, 64, 32).transpose(2, 0, 1).reshape(32, 128))
    cos, sin = wave(k1x, x_l, length)
    x_twist = np.stack([np.concatenate([cos, cos], 1), np.concatenate([sin, -sin], 1)])
    cos, sin = wave(k2x, x_l, 64)
    x_last = deep(np.concatenate([cos, sin], 1))
    cos, sin = wave(x_l, k2x, 64)
    x_lead = deep(np.concatenate([cos, sin], 1))
    cos, sin = wave(x_l, k1x, length)
    own = [np.concatenate([cos, -cos], 1), np.concatenate([sin, -sin], 1)]
    other = [np.concatenate([-sin, -sin], 1), np.concatenate([cos, cos], 1)]
    x_twists = np.concatenate([x_twist, np.stack(own + other)], 0).astype(np.float32)
    return {
        "y": (y_gather, y_expand),
        "x": (x_first, x_twists, x_last, x_lead, x_back),
        "z": (z_gather, z_expand),
    }


def split(values):
    high = values.astype(bf16)
    low = (values - high.astype(f32)).astype(bf16)
    return high, low


def stacked_product(table, values):
    high, low = split(values)
    return jnp.dot(table, jnp.concatenate([high, high, low], 0), preferred_element_type=f32)


def tall_product(table, values):
    high, low = split(values)
    size = table.shape[0] // 2
    both = jnp.dot(table, high, preferred_element_type=f32)
    rest = jnp.dot(table[:size], low, preferred_element_type=f32)
    return both[:size] + both[size:] + rest


def deep_product(table, values, contract):
    both = jnp.concatenate(split(values), contract)
    dims = (((1,), (contract,)), ((), ()))
    both = lax.dot_general(table, both, dims, preferred_element_type=f32)
    size = table.shape[0] // 2
    return both[:size] + both[size:]


def last_dims_product(former, latter):
    dims = (((1,), (1,)), ((), ()))
    return lax.dot_general(former, latter, dims, preferred_element_type=f32)


def half_turn(values):
    return pltpu.roll(values, 64, 1)


def lane_index(shape):
    return lax.broadcasted_iota(jnp.int32, shape, len(shape) - 1)


def half_sign(rows):
    return jnp.where(lane_index((rows, 128)) < 64, 1.0, -1.0).astype(f32)


def pack_body(film_ref, gather_ref, out_ref, edge_ref):
    values = jnp.concatenate([film_ref[a] for a in range(3)], 0)
    size = rows_n * modes
    turns = gather_ref[0 : 2 * rows_n, :]
    sides = [gather_ref[2 * rows_n + n : 2 * rows_n + n + 1, :] for n in range(modes)]
    re = [turns[:rows_n] * side for side in sides]
    im = [turns[rows_n:] * side for side in sides]
    table_high, table_low = split(jnp.concatenate(re + im, 0))
    high, low = split(values)
    sums = last_dims_product(
        jnp.concatenate([table_high, table_high], 1), jnp.concatenate([high, low], 1)
    ) + last_dims_product(table_low, high)
    low = lane_index((size, 128)) < 64
    re, im = sums[:size, :128], sums[size:, :128]
    last = jnp.concatenate([sums[:size, 128:], sums[size:, 128:]], 1)
    blocks = (jnp.where(low, re, half_turn(im)), jnp.where(low, half_turn(re), im), last)
    store_chunks(out_ref, halo_rows, blocks)
    former = jnp.concatenate([film_ref[0], film_ref[1]], 0).T
    latter = jnp.concatenate([film_ref[2], film_ref[3]], 0).T
    after = lax.broadcasted_iota(jnp.int32, (rows_n, lanes), 0) > lax.axis_index("row")
    for n, sides in enumerate((former, latter)):
        edges = jnp.where(after, sides[127:], sides[:1])
        out_ref[pl.ds(sums_rows + n, rows_n, stride=halo_rows), :] = edges
    for n in range(4):
        edge_ref[n : n + 1, :] = film_ref[n, :1, :]
        edge_ref[4 + n : 5 + n, :] = film_ref[n, cells - 1 :, :]


def spread_kern(kern_ref):
    low = lane_index((32, 128)) < 64
    spread = []
    for j in range(6):
        spread.append([])
        for k in range(4):
            part = kern_ref[pl.ds(128 * j + k, 32, stride=4), :]
            turned = half_turn(part)
            halves = [jnp.where(low, part, turned), jnp.where(low, turned, part)]
            spread[j].append(jnp.concatenate(halves, 0))
    return spread


def store_chunks(out_ref, rows, blocks):
    for a in range(3):
        for n in range(modes):
            out_ref[pl.ds(modes * a + n, rows_n, stride=rows), :] = blocks[a][
                rows_n * n : rows_n * n + rows_n
            ]


def load_chunks(in_ref, rows):
    columns = []
    for a in range(3):
        block = [in_ref[pl.ds(modes * a + n, rows_n, stride=rows), :] for n in range(modes)]
        columns.append(jnp.concatenate(block, 0))
    return jnp.concatenate(columns, 1)


def forward_body(in_ref, edge_ref, expand_ref, out_ref):
    sums = tall_product(expand_ref[...], load_chunks(in_ref, halo_rows))
    sign = half_sign(128)
    for a in range(3):
        block = sums[:, 128 * a : 128 * a + 128]
        block = block[:128] - half_turn(block[128:]) * sign
        for k in range(4):
            out_ref[pl.ds(4 * a + k, cols_n, stride=16), :] = block[32 * k : 32 * k + 32]
    col = lax.axis_index("col")
    first, last = edge_ref[0:4, :], edge_ref[4:8, :]
    for c in range(cols_n):
        out_ref[16 * c + 12 : 16 * c + 16, :] = jnp.where(c > col, last, first)


def spectral_body(
    in_ref, kern_ref, first_ref, twist_ref, last_ref, lead_ref, back_ref, out_ref
):
    sign = half_sign(64)
    own, other = twist_ref[0], twist_ref[1]
    kern = spread_kern(kern_ref)
    scale = -1.0 / (length * length)
    lane = lane_index((cols_n, 128))
    zero_weight = jnp.where(lane < 64, 1.0, 0.0).astype(f32)
    is_zero = jnp.logical_and(lax.axis_index("row") == 0, lax.axis_index("col") == 0)

    def enter(ks):
        columns = [in_ref[pl.ds(4 * a + k, cols_n, stride=16), :] for a in range(3) for k in ks]
        return stacked_product(first_ref[...], jnp.concatenate(columns, 1))

    def spread(section):
        turned = []
        for j in range(section.shape[1] // 128):
            block = section[:, 128 * j : 128 * j + 128]
            block = block[:64] + half_turn(block[64:]) * sign
            block = block * own + half_turn(block) * other
            turned.append(block)
            turned.append(half_turn(block) * sign)
        return deep_product(last_ref[...], jnp.concatenate(turned, 0), 1)

    def multiply(freq, ks):
        sources = []
        for target in range(3):
            for n, k in enumerate(ks):
                total = None
                for b in range(3):
                    j = len(ks) * b + n
                    term = kern[tensor_slots[target][b]][k] * freq[:, 128 * j : 128 * j + 128]
                    total = term if total is None else total + term
                sources.append(jnp.concatenate([total, -half_turn(total) * sign], 0))
        return deep_product(lead_ref[...], jnp.concatenate(sources, 1), 0)

    def leave(section):
        turned = []
        for j in range(section.shape[1] // 128):
            block = section[:, 128 * j : 128 * j + 128]
            aside = half_turn(block)
            turned.append(block * twist_ref[2] + aside * twist_ref[4])
            turned.append(block * twist_ref[3] + aside * twist_ref[5])
        return deep_product(back_ref[...], jnp.concatenate(turned, 0), 1)

    def store(result, ks):
        for a in range(3):
            for n, k in enumerate(ks):
                j = len(ks) * a + n
                block = result[:, 128 * j : 128 * j + 128]
                weight = jnp.full((cols_n, 128), 2.0, f32)
                if k == 0:
                    weight = jnp.where(is_zero, zero_weight, weight)
                out_ref[pl.ds(4 * a + k, cols_n, stride=12), :] = block * (weight * scale)

    groups = ((0,), (1,), (2,), (3,))
    states = [enter(ks) for ks in groups]
    states = [spread(state) for state in states]
    states = [multiply(state, ks) for state, ks in zip(states, groups)]
    states = [leave(state) for state in states]
    for state, ks in zip(states, groups):
        store(state, ks)


def back_body(in_ref, gather_ref, out_ref):
    columns = []
    for a in range(3):
        block = [in_ref[pl.ds(4 * a + k, cols_n, stride=12), :] for k in range(4)]
        columns.append(jnp.concatenate(block, 0))
    sums = deep_product(gather_ref[...], jnp.concatenate(columns, 1), 0)
    size = rows_n * modes
    sign = half_sign(size)
    blocks = []
    for a in range(3):
        block = sums[:, 128 * a : 128 * a + 128]
        blocks.append(block[:size] + half_turn(block[size:]) * sign)
    store_chunks(out_ref, sums_rows, blocks)


def cross(former, latter):
    return (
        former[1] * latter[2] - former[2] * latter[1],
        former[2] * latter[0] - former[0] * latter[2],
        former[0] * latter[1] - former[1] * latter[0],
    )


def torque_body(in_ref, film_ref, beside_y_ref, beside_x_ref, expand_ref, out_ref):
    row, col = lax.axis_index("row"), lax.axis_index("col")
    sums = tall_product(expand_ref[...], load_chunks(in_ref, sums_rows))
    demag = []
    for a in range(3):
        block = sums[:, 128 * a : 128 * a + 128]
        demag.append(block[:128] + half_turn(block[128:]))
    low = lane_index((128, 128)) < 64
    former = jnp.where(low, demag[0], half_turn(demag[1])).T
    demag = [former[:64], former[64:], demag[2].T[:64]]

    device = lax.broadcasted_iota(jnp.int32, (rows_n, 128), 0)

    def side(index):
        rows = []
        for n in range(2):
            halo = beside_y_ref[pl.ds(sums_rows + n, rows_n, stride=halo_rows), :]
            rows.append(jnp.sum(jnp.where(device == index, halo, 0.0), 0, keepdims=True))
        return rows

    before_y, after_y = side(row - 1), side(row + 1)
    before_x = beside_x_ref[pl.ds(pl.multiple_of(16 * jnp.maximum(col - 1, 0), 16), 16), :]
    after_x = beside_x_ref[pl.ds(pl.multiple_of(16 * jnp.minimum(col + 1, cols_n - 1), 16), 16), :]
    edges = jnp.concatenate(before_y + after_y + [jnp.zeros((124, 128), f32)], 0).T
    stack = [film_ref[n] for n in range(4)]
    lane = lane_index((cells, 128))
    sub = lax.broadcasted_iota(jnp.int32, (cells, 128), 0)

    def neighbour(n, direction):
        centre = stack[n]
        part = slice(64 * (n % 2), 64 * (n % 2) + 64)
        if direction == 0:
            return jnp.where(sub == cells - 1, after_x[12 + n : 13 + n], pltpu.roll(centre, cells - 1, 0))
        if direction == 1:
            return jnp.where(sub == 0, before_x[12 + n : 13 + n], pltpu.roll(centre, 1, 0))
        if direction == 2:
            edge = edges[part, 2 + n // 2 : 3 + n // 2]
            return jnp.where(lane == 127, edge, pltpu.roll(centre, 127, 1))
        edge = edges[part, n // 2 : n // 2 + 1]
        return jnp.where(lane == 0, edge, pltpu.roll(centre, 1, 1))

    absent = (
        jnp.logical_and(sub == cells - 1, col == cols_n - 1),
        jnp.logical_and(sub == 0, col == 0),
        jnp.logical_and(lane == 127, row == rows_n - 1),
        jnp.logical_and(lane == 0, row == 0),
    )
    exchange = [None] * 3
    for direction in range(4):
        coupling = 0.5 * (stack[3] + neighbour(3, direction))
        coupling = jnp.where(absent[direction], 0.0, coupling)
        for a in range(3):
            term = coupling * (neighbour(a, direction) - stack[a])
            exchange[a] = term if exchange[a] is None else exchange[a] + term
    magnet = stack[:3]
    field = [exchange[a] + demag[a] for a in range(3)]
    field[2] = field[2] + anisotropy * magnet[2]
    first_cross = cross(magnet, field)
    second_cross = cross(magnet, first_cross)
    factor = -1.0 / (1.0 + damping * damping)
    for a in range(3):
        out_ref[a] = (first_cross[a] + damping * second_cross[a]) * factor


in_vmem = pl.BlockSpec(memory_space=pltpu.VMEM)
in_hbm = pl.BlockSpec(memory_space=pltpu.HBM)


def call(body, out_shapes, *args, scratch=(), in_spec=in_vmem, vmem=32 * 2**20, flops=10**8):
    shapes = [jax.ShapeDtypeStruct(shape, f32) for shape in out_shapes]
    return pl.pallas_call(
        body,
        out_shape=shapes,
        in_specs=[in_spec] * len(args),
        out_specs=[in_vmem] * len(shapes),
        scratch_shapes=list(scratch),
        compiler_params=pltpu.CompilerParams(vmem_limit_bytes=vmem),
        cost_estimate=pl.CostEstimate(flops=flops, bytes_accessed=10**6, transcendentals=0),
    )(*args)


def exchange(array, axis, chunks):
    shape = array.shape
    rows = shape[0] // chunks
    tile = math.gcd(rows, 8)
    array = array.reshape(chunks, rows // tile, tile, shape[1])
    return lax.all_to_all(array, axis, split_axis=0, concat_axis=0, tiled=True).reshape(shape)


def local(magnet, stiffness, kern):
    constant = {name: [jnp.asarray(t) for t in group] for name, group in tables().items()}
    film = jnp.concatenate([magnet, stiffness[None]], 0)
    packed, edge = call(
        pack_body, [(rows_n * halo_rows, 128), (8, 128)], film, constant["y"][0]
    )
    sums = exchange(packed, "row", rows_n)
    (columns,) = call(forward_body, [(512, 128)], sums, edge, constant["y"][1])
    columns = exchange(columns, "col", cols_n)
    tensor = kern.reshape(6, 4, 32, 128).transpose(0, 2, 1, 3).reshape(768, 128)
    (inverse_x,) = call(spectral_body, [(384, 128)], columns, tensor, *constant["x"])
    inverse_x = exchange(inverse_x, "col", cols_n)
    (coef,) = call(back_body, [(rows_n * sums_rows, 128)], inverse_x, constant["z"][0])
    coef = exchange(coef, "row", rows_n)
    (torque,) = call(
        torque_body, [(3, 64, 128)], coef, film, sums, columns, constant["z"][1]
    )
    return torque


def solution(mesh):
    in_specs = (P(None, "col", "row"), P("col", "row"), P(None, ("row", "col"), None))
    out_specs = P(None, "col", "row")
    return jax.shard_map(local, mesh=mesh, in_specs=in_specs, out_specs=out_specs, check_vma=False)
```

```python
import math

import jax
import jax.numpy as jnp
import ml_dtypes
import numpy as np
from jax import lax
from jax.experimental import pallas as pl
from jax.experimental.pallas import tpu as pltpu
from jax.sharding import PartitionSpec as P

damping = 0.3
anisotropy = 0.8
tensor_slots = ((0, 3, 4), (3, 1, 5), (4, 5, 2))

rows_n = 16
cols_n = 32
cells = 64
lanes = 128
length = 4096
bf16 = jnp.bfloat16
f32 = jnp.float32


modes = 14
sums_rows = 3 * modes
halo_rows = sums_rows + 2


def wave(first, second, period):
    angle = 2.0 * math.pi * (np.outer(first, second) % period) / period
    return np.cos(angle), np.sin(angle)


def split_table(table):
    high = table.astype(ml_dtypes.bfloat16)
    low = (table - high.astype(np.float64)).astype(ml_dtypes.bfloat16)
    return high, low


def thick(table):
    high, low = split_table(table)
    return np.concatenate([high, low, high, low], 1)


def tall(table):
    return np.concatenate(split_table(table), 0)


def deep(table):
    high, low = split_table(table)
    return np.concatenate([np.tile(high, (1, 2)), np.tile(low, (1, 2))], 0)


def factors():
    place = np.arange(lanes) - 0.5 * (lanes - 1)
    angle = 2.0 * math.pi * np.outer(place, place) / length
    level = (1.02 - (2.0 * place / lanes) ** 2) ** -0.3
    values, vectors, units = [], [], []
    for part, unit in ((np.cos(angle), 1.0), (np.sin(angle), -1j)):
        value, vector = np.linalg.eigh(part * np.outer(level, level))
        values.append(value)
        vectors.append(vector * np.where(vector[-1] < 0.0, -1.0, 1.0))
        units.append(np.full(lanes, unit))
    values, vectors = np.concatenate(values), np.concatenate(vectors, 1)
    units = np.concatenate(units)
    kept = np.argsort(-np.abs(values), kind="stable")[:modes]
    side = vectors[:, kept] * np.sqrt(np.abs(values[kept])) / level[:, None]
    return side, units[kept] * np.sign(values[kept])


def row_transform():
    side, weight = factors()
    place = np.arange(lanes) - 0.5 * (lanes - 1)
    centre = lanes * np.arange(rows_n) + 0.5 * (lanes - 1)
    turn = np.exp(-2j * math.pi * np.outer(centre, place) / length)
    offset = 0.5 * (lanes - 1)
    phase = np.exp(-2j * math.pi * np.arange(rows_n) * lanes * offset / length)
    constant = np.exp(-2j * math.pi * offset * offset / length)
    turns = turn * phase[:, None]
    gather = side.T[:, None] * turns[None]
    expand = (side * weight)[:, :, None] * turn.T[:, None, :] * phase * constant
    gather, expand = gather.reshape(-1, lanes), expand.reshape(lanes, -1)
    return side.T, turns, gather, expand


def parts(table):
    return np.concatenate([table.real, table.imag], 0)


def tables():
    col = np.arange(cols_n)
    x_l = np.arange(cells)
    k1x = np.arange(64)
    k2x = (2 * np.arange(32)[None, :] + np.arange(2)[:, None]).reshape(-1)
    kappa = (4 * col[None, :] + np.arange(4)[:, None]).reshape(-1)

    sides, turns, gather, expand = row_transform()
    y_gather = np.concatenate([parts(turns), sides], 0).astype(np.float32)
    y_expand = tall(parts(expand[kappa]))
    z_gather = deep(parts(gather[:, kappa]))
    z_expand = tall(parts(expand))

    cos, sin = wave(k1x, col, 64)
    x_first = thick(np.concatenate([cos, sin], 0))
    x_back = deep(np.concatenate([cos, sin], 0).reshape(2, 64, 32).transpose(2, 0, 1).reshape(32, 128))
    cos, sin = wave(k1x, x_l, length)
    x_twist = np.stack([np.concatenate([cos, cos], 1), np.concatenate([sin, -sin], 1)])
    cos, sin = wave(k2x, x_l, 64)
    x_last = deep(np.concatenate([cos, sin], 1))
    cos, sin = wave(x_l, k2x, 64)
    x_lead = deep(np.concatenate([cos, sin], 1))
    cos, sin = wave(x_l, k1x, length)
    own = [np.concatenate([cos, -cos], 1), np.concatenate([sin, -sin], 1)]
    other = [np.concatenate([-sin, -sin], 1), np.concatenate([cos, cos], 1)]
    x_twists = np.concatenate([x_twist, np.stack(own + other)], 0).astype(np.float32)
    return {
        "y": (y_gather, y_expand),
        "x": (x_first, x_twists, x_last, x_lead, x_back),
        "z": (z_gather, z_expand),
    }


def split(values):
    high = values.astype(bf16)
    low = (values - high.astype(f32)).astype(bf16)
    return high, low


def stacked_product(table, values):
    high, low = split(values)
    return jnp.dot(table, jnp.concatenate([high, high, low, low], 0), preferred_element_type=f32)


def tall_product(table, values):
    high, low = split(values)
    size = table.shape[0] // 2
    both = jnp.dot(table, high, preferred_element_type=f32)
    rest = jnp.dot(table[:size], low, preferred_element_type=f32)
    return both[:size] + both[size:] + rest


def deep_product(table, values, contract):
    both = jnp.concatenate(split(values), contract)
    dims = (((1,), (contract,)), ((), ()))
    both = lax.dot_general(table, both, dims, preferred_element_type=f32)
    size = table.shape[0] // 2
    return both[:size] + both[size:]


def half_turn(values):
    return pltpu.roll(values, 64, 1)


def lane_index(shape):
    return lax.broadcasted_iota(jnp.int32, shape, len(shape) - 1)


def half_sign(rows):
    return jnp.where(lane_index((rows, 128)) < 64, 1.0, -1.0).astype(f32)


def pack_body(film_ref, gather_ref, out_ref, edge_ref):
    values = jnp.concatenate([film_ref[a] for a in range(3)], 0)
    size = rows_n * modes
    turns = gather_ref[0 : 2 * rows_n, :]
    sides = [gather_ref[2 * rows_n + n : 2 * rows_n + n + 1, :] for n in range(modes)]
    re = [turns[:rows_n] * side for side in sides]
    im = [turns[rows_n:] * side for side in sides]
    table_high, table_low = split(jnp.concatenate(re + im, 0))
    table = jnp.concatenate([table_high, table_low], 0)
    sums = deep_product(jnp.concatenate([table, table], 1), values, 1)
    low = lane_index((size, 128)) < 64
    re, im = sums[:size, :128], sums[size:, :128]
    last = jnp.concatenate([sums[:size, 128:], sums[size:, 128:]], 1)
    blocks = (jnp.where(low, re, half_turn(im)), jnp.where(low, half_turn(re), im), last)
    store_chunks(out_ref, halo_rows, blocks)
    former = jnp.concatenate([film_ref[0], film_ref[1]], 0).T
    latter = jnp.concatenate([film_ref[2], film_ref[3]], 0).T
    after = lax.broadcasted_iota(jnp.int32, (rows_n, lanes), 0) > lax.axis_index("row")
    for n, sides in enumerate((former, latter)):
        edges = jnp.where(after, sides[127:], sides[:1])
        out_ref[pl.ds(sums_rows + n, rows_n, stride=halo_rows), :] = edges
    for n in range(4):
        edge_ref[n : n + 1, :] = film_ref[n, :1, :]
        edge_ref[4 + n : 5 + n, :] = film_ref[n, cells - 1 :, :]


def spread_kern(kern_ref):
    low = lane_index((32, 128)) < 64
    spread = []
    for j in range(6):
        spread.append([])
        for k in range(4):
            part = kern_ref[pl.ds(128 * j + k, 32, stride=4), :]
            turned = half_turn(part)
            halves = [jnp.where(low, part, turned), jnp.where(low, turned, part)]
            spread[j].append(jnp.concatenate(halves, 0))
    return spread


def store_chunks(out_ref, rows, blocks):
    for a in range(3):
        for n in range(modes):
            out_ref[pl.ds(modes * a + n, rows_n, stride=rows), :] = blocks[a][
                rows_n * n : rows_n * n + rows_n
            ]


def load_chunks(in_ref, rows):
    columns = []
    for a in range(3):
        block = [in_ref[pl.ds(modes * a + n, rows_n, stride=rows), :] for n in range(modes)]
        columns.append(jnp.concatenate(block, 0))
    return jnp.concatenate(columns, 1)


def forward_body(in_ref, edge_ref, expand_ref, out_ref):
    sums = tall_product(expand_ref[...], load_chunks(in_ref, halo_rows))
    sign = half_sign(128)
    for a in range(3):
        block = sums[:, 128 * a : 128 * a + 128]
        block = block[:128] - half_turn(block[128:]) * sign
        for k in range(4):
            out_ref[pl.ds(4 * a + k, cols_n, stride=16), :] = block[32 * k : 32 * k + 32]
    col = lax.axis_index("col")
    first, last = edge_ref[0:4, :], edge_ref[4:8, :]
    for c in range(cols_n):
        out_ref[16 * c + 12 : 16 * c + 16, :] = jnp.where(c > col, last, first)


def spectral_body(
    in_ref, kern_ref, first_ref, twist_ref, last_ref, lead_ref, back_ref, out_ref
):
    sign = half_sign(64)
    own, other = twist_ref[0], twist_ref[1]
    kern = spread_kern(kern_ref)
    scale = -1.0 / (length * length)
    lane = lane_index((cols_n, 128))
    zero_weight = jnp.where(lane < 64, 1.0, 0.0).astype(f32)
    is_zero = jnp.logical_and(lax.axis_index("row") == 0, lax.axis_index("col") == 0)

    def enter(ks):
        columns = [in_ref[pl.ds(4 * a + k, cols_n, stride=16), :] for a in range(3) for k in ks]
        return stacked_product(first_ref[...], jnp.concatenate(columns, 1))

    def spread(section):
        turned = []
        for j in range(section.shape[1] // 128):
            block = section[:, 128 * j : 128 * j + 128]
            block = block[:64] + half_turn(block[64:]) * sign
            block = block * own + half_turn(block) * other
            turned.append(block)
            turned.append(half_turn(block) * sign)
        return deep_product(last_ref[...], jnp.concatenate(turned, 0), 1)

    def multiply(freq, ks):
        sources = []
        for target in range(3):
            for n, k in enumerate(ks):
                total = None
                for b in range(3):
                    j = len(ks) * b + n
                    term = kern[tensor_slots[target][b]][k] * freq[:, 128 * j : 128 * j + 128]
                    total = term if total is None else total + term
                sources.append(jnp.concatenate([total, -half_turn(total) * sign], 0))
        return deep_product(lead_ref[...], jnp.concatenate(sources, 1), 0)

    def leave(section):
        turned = []
        for j in range(section.shape[1] // 128):
            block = section[:, 128 * j : 128 * j + 128]
            aside = half_turn(block)
            turned.append(block * twist_ref[2] + aside * twist_ref[4])
            turned.append(block * twist_ref[3] + aside * twist_ref[5])
        return deep_product(back_ref[...], jnp.concatenate(turned, 0), 1)

    def store(result, ks):
        for a in range(3):
            for n, k in enumerate(ks):
                j = len(ks) * a + n
                block = result[:, 128 * j : 128 * j + 128]
                weight = jnp.full((cols_n, 128), 2.0, f32)
                if k == 0:
                    weight = jnp.where(is_zero, zero_weight, weight)
                out_ref[pl.ds(4 * a + k, cols_n, stride=12), :] = block * (weight * scale)

    groups = ((0,), (1,), (2,), (3,))
    states = [enter(ks) for ks in groups]
    states = [spread(state) for state in states]
    states = [multiply(state, ks) for state, ks in zip(states, groups)]
    states = [leave(state) for state in states]
    for state, ks in zip(states, groups):
        store(state, ks)


def back_body(in_ref, gather_ref, out_ref):
    columns = []
    for a in range(3):
        block = [in_ref[pl.ds(4 * a + k, cols_n, stride=12), :] for k in range(4)]
        columns.append(jnp.concatenate(block, 0))
    sums = deep_product(gather_ref[...], jnp.concatenate(columns, 1), 0)
    size = rows_n * modes
    sign = half_sign(size)
    blocks = []
    for a in range(3):
        block = sums[:, 128 * a : 128 * a + 128]
        blocks.append(block[:size] + half_turn(block[size:]) * sign)
    store_chunks(out_ref, sums_rows, blocks)


def cross(former, latter):
    return (
        former[1] * latter[2] - former[2] * latter[1],
        former[2] * latter[0] - former[0] * latter[2],
        former[0] * latter[1] - former[1] * latter[0],
    )


def torque_body(in_ref, film_ref, beside_y_ref, beside_x_ref, expand_ref, out_ref):
    row, col = lax.axis_index("row"), lax.axis_index("col")
    sums = tall_product(expand_ref[...], load_chunks(in_ref, sums_rows))
    demag = []
    for a in range(3):
        block = sums[:, 128 * a : 128 * a + 128]
        demag.append(block[:128] + half_turn(block[128:]))
    low = lane_index((128, 128)) < 64
    former = jnp.where(low, demag[0], half_turn(demag[1])).T
    demag = [former[:64], former[64:], demag[2].T[:64]]

    device = lax.broadcasted_iota(jnp.int32, (rows_n, 128), 0)

    def side(index):
        rows = []
        for n in range(2):
            halo = beside_y_ref[pl.ds(sums_rows + n, rows_n, stride=halo_rows), :]
            rows.append(jnp.sum(jnp.where(device == index, halo, 0.0), 0, keepdims=True))
        return rows

    before_y, after_y = side(row - 1), side(row + 1)
    before_x = beside_x_ref[pl.ds(pl.multiple_of(16 * jnp.maximum(col - 1, 0), 16), 16), :]
    after_x = beside_x_ref[pl.ds(pl.multiple_of(16 * jnp.minimum(col + 1, cols_n - 1), 16), 16), :]
    edges = jnp.concatenate(before_y + after_y + [jnp.zeros((124, 128), f32)], 0).T
    stack = [film_ref[n] for n in range(4)]
    lane = lane_index((cells, 128))
    sub = lax.broadcasted_iota(jnp.int32, (cells, 128), 0)

    def neighbour(n, direction):
        centre = stack[n]
        part = slice(64 * (n % 2), 64 * (n % 2) + 64)
        if direction == 0:
            return jnp.where(sub == cells - 1, after_x[12 + n : 13 + n], pltpu.roll(centre, cells - 1, 0))
        if direction == 1:
            return jnp.where(sub == 0, before_x[12 + n : 13 + n], pltpu.roll(centre, 1, 0))
        if direction == 2:
            edge = edges[part, 2 + n // 2 : 3 + n // 2]
            return jnp.where(lane == 127, edge, pltpu.roll(centre, 127, 1))
        edge = edges[part, n // 2 : n // 2 + 1]
        return jnp.where(lane == 0, edge, pltpu.roll(centre, 1, 1))

    absent = (
        jnp.logical_and(sub == cells - 1, col == cols_n - 1),
        jnp.logical_and(sub == 0, col == 0),
        jnp.logical_and(lane == 127, row == rows_n - 1),
        jnp.logical_and(lane == 0, row == 0),
    )
    exchange = [None] * 3
    for direction in range(4):
        coupling = 0.5 * (stack[3] + neighbour(3, direction))
        coupling = jnp.where(absent[direction], 0.0, coupling)
        for a in range(3):
            term = coupling * (neighbour(a, direction) - stack[a])
            exchange[a] = term if exchange[a] is None else exchange[a] + term
    magnet = stack[:3]
    field = [exchange[a] + demag[a] for a in range(3)]
    field[2] = field[2] + anisotropy * magnet[2]
    first_cross = cross(magnet, field)
    second_cross = cross(magnet, first_cross)
    factor = -1.0 / (1.0 + damping * damping)
    for a in range(3):
        out_ref[a] = (first_cross[a] + damping * second_cross[a]) * factor


in_vmem = pl.BlockSpec(memory_space=pltpu.VMEM)
in_hbm = pl.BlockSpec(memory_space=pltpu.HBM)


def call(body, out_shapes, *args, scratch=(), in_spec=in_vmem, vmem=32 * 2**20, flops=10**8):
    shapes = [jax.ShapeDtypeStruct(shape, f32) for shape in out_shapes]
    return pl.pallas_call(
        body,
        out_shape=shapes,
        in_specs=[in_spec] * len(args),
        out_specs=[in_vmem] * len(shapes),
        scratch_shapes=list(scratch),
        compiler_params=pltpu.CompilerParams(vmem_limit_bytes=vmem),
        cost_estimate=pl.CostEstimate(flops=flops, bytes_accessed=10**6, transcendentals=0),
    )(*args)


def exchange(array, axis, chunks):
    shape = array.shape
    rows = shape[0] // chunks
    tile = math.gcd(rows, 8)
    array = array.reshape(chunks, rows // tile, tile, shape[1])
    return lax.all_to_all(array, axis, split_axis=0, concat_axis=0, tiled=True).reshape(shape)


def local(magnet, stiffness, kern):
    constant = {name: [jnp.asarray(t) for t in group] for name, group in tables().items()}
    film = jnp.concatenate([magnet, stiffness[None]], 0)
    packed, edge = call(
        pack_body, [(rows_n * halo_rows, 128), (8, 128)], film, constant["y"][0]
    )
    sums = exchange(packed, "row", rows_n)
    (columns,) = call(forward_body, [(512, 128)], sums, edge, constant["y"][1])
    columns = exchange(columns, "col", cols_n)
    tensor = kern.reshape(6, 4, 32, 128).transpose(0, 2, 1, 3).reshape(768, 128)
    (inverse_x,) = call(spectral_body, [(384, 128)], columns, tensor, *constant["x"])
    inverse_x = exchange(inverse_x, "col", cols_n)
    (coef,) = call(back_body, [(rows_n * sums_rows, 128)], inverse_x, constant["z"][0])
    coef = exchange(coef, "row", rows_n)
    (torque,) = call(
        torque_body, [(3, 64, 128)], coef, film, sums, columns, constant["z"][1]
    )
    return torque


def solution(mesh):
    in_specs = (P(None, "col", "row"), P("col", "row"), P(None, ("row", "col"), None))
    out_specs = P(None, "col", "row")
    return jax.shard_map(local, mesh=mesh, in_specs=in_specs, out_specs=out_specs, check_vma=False)
```

```python
import math

import jax
import jax.numpy as jnp
import ml_dtypes
import numpy as np
from jax import lax
from jax.experimental import pallas as pl
from jax.experimental.pallas import tpu as pltpu
from jax.sharding import PartitionSpec as P

damping = 0.3
anisotropy = 0.8
tensor_slots = ((0, 3, 4), (3, 1, 5), (4, 5, 2))

rows_n = 16
cols_n = 32
cells = 64
lanes = 128
length = 4096
bf16 = jnp.bfloat16
f32 = jnp.float32


modes = 14
sums_rows = 3 * modes
halo_rows = sums_rows + 2


def wave(first, second, period):
    angle = 2.0 * math.pi * (np.outer(first, second) % period) / period
    return np.cos(angle), np.sin(angle)


def split_table(table):
    high = table.astype(ml_dtypes.bfloat16)
    low = (table - high.astype(np.float64)).astype(ml_dtypes.bfloat16)
    return high, low


def thick(table):
    high, low = split_table(table)
    return np.concatenate([high, low, high, low], 1)


def tall(table):
    return np.concatenate(split_table(table), 0)


def deep(table):
    high, low = split_table(table)
    return np.concatenate([np.tile(high, (1, 2)), np.tile(low, (1, 2))], 0)


def factors():
    place = np.arange(lanes) - 0.5 * (lanes - 1)
    angle = 2.0 * math.pi * np.outer(place, place) / length
    level = (1.02 - (2.0 * place / lanes) ** 2) ** -0.3
    values, vectors, units = [], [], []
    for part, unit in ((np.cos(angle), 1.0), (np.sin(angle), -1j)):
        value, vector = np.linalg.eigh(part * np.outer(level, level))
        values.append(value)
        vectors.append(vector * np.where(vector[-1] < 0.0, -1.0, 1.0))
        units.append(np.full(lanes, unit))
    values, vectors = np.concatenate(values), np.concatenate(vectors, 1)
    units = np.concatenate(units)
    kept = np.argsort(-np.abs(values), kind="stable")[:modes]
    side = vectors[:, kept] * np.sqrt(np.abs(values[kept])) / level[:, None]
    return side, units[kept] * np.sign(values[kept])


def row_transform():
    side, weight = factors()
    place = np.arange(lanes) - 0.5 * (lanes - 1)
    centre = lanes * np.arange(rows_n) + 0.5 * (lanes - 1)
    turn = np.exp(-2j * math.pi * np.outer(centre, place) / length)
    offset = 0.5 * (lanes - 1)
    phase = np.exp(-2j * math.pi * np.arange(rows_n) * lanes * offset / length)
    constant = np.exp(-2j * math.pi * offset * offset / length)
    turns = turn * phase[:, None]
    gather = side.T[:, None] * turns[None]
    expand = (side * weight)[:, :, None] * turn.T[:, None, :] * phase * constant
    gather, expand = gather.reshape(-1, lanes), expand.reshape(lanes, -1)
    return side.T, turns, gather, expand


def parts(table):
    return np.concatenate([table.real, table.imag], 0)


def tables():
    col = np.arange(cols_n)
    x_l = np.arange(cells)
    k1x = np.arange(64)
    k2x = (2 * np.arange(32)[None, :] + np.arange(2)[:, None]).reshape(-1)
    kappa = (4 * col[None, :] + np.arange(4)[:, None]).reshape(-1)

    sides, turns, gather, expand = row_transform()
    y_gather = np.concatenate([parts(turns), sides], 0).astype(np.float32)
    y_expand = tall(parts(expand[kappa]))
    z_gather = deep(parts(gather[:, kappa]))
    z_expand = np.ascontiguousarray(tall(parts(expand)).T)

    cos, sin = wave(k1x, col, 64)
    x_first = thick(np.concatenate([cos, sin], 0))
    x_back = deep(np.concatenate([cos, sin], 0).reshape(2, 64, 32).transpose(2, 0, 1).reshape(32, 128))
    cos, sin = wave(k1x, x_l, length)
    x_twist = np.stack([np.concatenate([cos, cos], 1), np.concatenate([sin, -sin], 1)])
    cos, sin = wave(k2x, x_l, 64)
    x_last = deep(np.concatenate([cos, sin], 1))
    cos, sin = wave(x_l, k2x, 64)
    x_lead = deep(np.concatenate([cos, sin], 1))
    cos, sin = wave(x_l, k1x, length)
    own = [np.concatenate([cos, -cos], 1), np.concatenate([sin, -sin], 1)]
    other = [np.concatenate([-sin, -sin], 1), np.concatenate([cos, cos], 1)]
    x_twists = np.concatenate([x_twist, np.stack(own + other)], 0).astype(np.float32)
    return {
        "y": (y_gather, y_expand),
        "x": (x_first, x_twists, x_last, x_lead, x_back),
        "z": (z_gather, z_expand),
    }


def split(values):
    high = values.astype(bf16)
    low = (values - high.astype(f32)).astype(bf16)
    return high, low


def stacked_product(table, values):
    high, low = split(values)
    return jnp.dot(table, jnp.concatenate([high, high, low, low], 0), preferred_element_type=f32)


def tall_product(table, values):
    high, low = split(values)
    size = table.shape[0] // 2
    both = jnp.dot(table, high, preferred_element_type=f32)
    rest = jnp.dot(table[:size], low, preferred_element_type=f32)
    return both[:size] + both[size:] + rest


def deep_product(table, values, contract):
    both = jnp.concatenate(split(values), contract)
    dims = (((1,), (contract,)), ((), ()))
    both = lax.dot_general(table, both, dims, preferred_element_type=f32)
    size = table.shape[0] // 2
    return both[:size] + both[size:]


def half_turn(values):
    return pltpu.roll(values, 64, 1)


def lane_index(shape):
    return lax.broadcasted_iota(jnp.int32, shape, len(shape) - 1)


def half_sign(rows):
    return jnp.where(lane_index((rows, 128)) < 64, 1.0, -1.0).astype(f32)


def pack_body(film_ref, gather_ref, out_ref, edge_ref):
    values = jnp.concatenate([film_ref[a] for a in range(3)], 0)
    size = rows_n * modes
    turns = gather_ref[0 : 2 * rows_n, :]
    sides = [gather_ref[2 * rows_n + n : 2 * rows_n + n + 1, :] for n in range(modes)]
    re = [turns[:rows_n] * side for side in sides]
    im = [turns[rows_n:] * side for side in sides]
    table_high, table_low = split(jnp.concatenate(re + im, 0))
    table = jnp.concatenate([table_high, table_low], 0)
    sums = deep_product(jnp.concatenate([table, table], 1), values, 1)
    low = lane_index((size, 128)) < 64
    re, im = sums[:size, :128], sums[size:, :128]
    last = jnp.concatenate([sums[:size, 128:], sums[size:, 128:]], 1)
    blocks = (jnp.where(low, re, half_turn(im)), jnp.where(low, half_turn(re), im), last)
    store_chunks(out_ref, halo_rows, blocks)
    former = jnp.concatenate([film_ref[0], film_ref[1]], 0).T
    latter = jnp.concatenate([film_ref[2], film_ref[3]], 0).T
    after = lax.broadcasted_iota(jnp.int32, (rows_n, lanes), 0) > lax.axis_index("row")
    for n, sides in enumerate((former, latter)):
        edges = jnp.where(after, sides[127:], sides[:1])
        out_ref[pl.ds(sums_rows + n, rows_n, stride=halo_rows), :] = edges
    for n in range(4):
        edge_ref[n : n + 1, :] = film_ref[n, :1, :]
        edge_ref[4 + n : 5 + n, :] = film_ref[n, cells - 1 :, :]


def spread_kern(kern_ref):
    low = lane_index((32, 128)) < 64
    spread = []
    for j in range(6):
        spread.append([])
        for k in range(4):
            part = kern_ref[pl.ds(128 * j + k, 32, stride=4), :]
            turned = half_turn(part)
            halves = [jnp.where(low, part, turned), jnp.where(low, turned, part)]
            spread[j].append(jnp.concatenate(halves, 0))
    return spread


def store_chunks(out_ref, rows, blocks):
    for a in range(3):
        for n in range(modes):
            out_ref[pl.ds(modes * a + n, rows_n, stride=rows), :] = blocks[a][
                rows_n * n : rows_n * n + rows_n
            ]


def load_chunks(in_ref, rows):
    columns = []
    for a in range(3):
        block = [in_ref[pl.ds(modes * a + n, rows_n, stride=rows), :] for n in range(modes)]
        columns.append(jnp.concatenate(block, 0))
    return jnp.concatenate(columns, 1)


def forward_body(in_ref, edge_ref, expand_ref, out_ref):
    sums = tall_product(expand_ref[...], load_chunks(in_ref, halo_rows))
    sign = half_sign(128)
    for a in range(3):
        block = sums[:, 128 * a : 128 * a + 128]
        block = block[:128] - half_turn(block[128:]) * sign
        for k in range(4):
            out_ref[pl.ds(4 * a + k, cols_n, stride=16), :] = block[32 * k : 32 * k + 32]
    col = lax.axis_index("col")
    first, last = edge_ref[0:4, :], edge_ref[4:8, :]
    for c in range(cols_n):
        out_ref[16 * c + 12 : 16 * c + 16, :] = jnp.where(c > col, last, first)


def spectral_body(
    in_ref, kern_ref, first_ref, twist_ref, last_ref, lead_ref, back_ref, out_ref
):
    sign = half_sign(64)
    own, other = twist_ref[0], twist_ref[1]
    kern = spread_kern(kern_ref)
    scale = -1.0 / (length * length)
    lane = lane_index((cols_n, 128))
    zero_weight = jnp.where(lane < 64, 1.0, 0.0).astype(f32)
    is_zero = jnp.logical_and(lax.axis_index("row") == 0, lax.axis_index("col") == 0)

    def enter(ks):
        columns = [in_ref[pl.ds(4 * a + k, cols_n, stride=16), :] for a in range(3) for k in ks]
        return stacked_product(first_ref[...], jnp.concatenate(columns, 1))

    def spread(section):
        turned = []
        for j in range(section.shape[1] // 128):
            block = section[:, 128 * j : 128 * j + 128]
            block = block[:64] + half_turn(block[64:]) * sign
            block = block * own + half_turn(block) * other
            turned.append(block)
            turned.append(half_turn(block) * sign)
        return deep_product(last_ref[...], jnp.concatenate(turned, 0), 1)

    def multiply(freq, ks):
        sources = []
        for target in range(3):
            for n, k in enumerate(ks):
                total = None
                for b in range(3):
                    j = len(ks) * b + n
                    term = kern[tensor_slots[target][b]][k] * freq[:, 128 * j : 128 * j + 128]
                    total = term if total is None else total + term
                sources.append(jnp.concatenate([total, -half_turn(total) * sign], 0))
        return deep_product(lead_ref[...], jnp.concatenate(sources, 1), 0)

    def leave(section):
        turned = []
        for j in range(section.shape[1] // 128):
            block = section[:, 128 * j : 128 * j + 128]
            aside = half_turn(block)
            turned.append(block * twist_ref[2] + aside * twist_ref[4])
            turned.append(block * twist_ref[3] + aside * twist_ref[5])
        return deep_product(back_ref[...], jnp.concatenate(turned, 0), 1)

    def store(result, ks):
        for a in range(3):
            for n, k in enumerate(ks):
                j = len(ks) * a + n
                block = result[:, 128 * j : 128 * j + 128]
                weight = jnp.full((cols_n, 128), 2.0, f32)
                if k == 0:
                    weight = jnp.where(is_zero, zero_weight, weight)
                out_ref[pl.ds(4 * a + k, cols_n, stride=12), :] = block * (weight * scale)

    groups = ((0,), (1,), (2,), (3,))
    states = [enter(ks) for ks in groups]
    states = [spread(state) for state in states]
    states = [multiply(state, ks) for state, ks in zip(states, groups)]
    states = [leave(state) for state in states]
    for state, ks in zip(states, groups):
        store(state, ks)


def back_body(in_ref, gather_ref, out_ref):
    columns = []
    for a in range(3):
        block = [in_ref[pl.ds(4 * a + k, cols_n, stride=12), :] for k in range(4)]
        columns.append(jnp.concatenate(block, 0))
    sums = deep_product(gather_ref[...], jnp.concatenate(columns, 1), 0)
    size = rows_n * modes
    sign = half_sign(size)
    blocks = []
    for a in range(3):
        block = sums[:, 128 * a : 128 * a + 128]
        blocks.append(block[:size] + half_turn(block[size:]) * sign)
    store_chunks(out_ref, sums_rows, blocks)


def cross(former, latter):
    return (
        former[1] * latter[2] - former[2] * latter[1],
        former[2] * latter[0] - former[0] * latter[2],
        former[0] * latter[1] - former[1] * latter[0],
    )


def torque_body(in_ref, film_ref, beside_y_ref, beside_x_ref, expand_ref, out_ref):
    row, col = lax.axis_index("row"), lax.axis_index("col")
    high, low = split(load_chunks(in_ref, sums_rows).T)
    both = jnp.dot(high, expand_ref[...], preferred_element_type=f32)
    rest = jnp.dot(low, expand_ref[:, :256], preferred_element_type=f32)
    sums = both[:, :256] + both[:, 256:] + rest
    demag = []
    for a in range(3):
        block = sums[128 * a : 128 * a + 128]
        demag.append(block[:64, :128] + block[64:, 128:])

    device = lax.broadcasted_iota(jnp.int32, (rows_n, 128), 0)

    def side(index):
        rows = []
        for n in range(2):
            halo = beside_y_ref[pl.ds(sums_rows + n, rows_n, stride=halo_rows), :]
            rows.append(jnp.sum(jnp.where(device == index, halo, 0.0), 0, keepdims=True))
        return rows

    before_y, after_y = side(row - 1), side(row + 1)
    before_x = beside_x_ref[pl.ds(pl.multiple_of(16 * jnp.maximum(col - 1, 0), 16), 16), :]
    after_x = beside_x_ref[pl.ds(pl.multiple_of(16 * jnp.minimum(col + 1, cols_n - 1), 16), 16), :]
    edges = jnp.concatenate(before_y + after_y + [jnp.zeros((124, 128), f32)], 0).T
    stack = [film_ref[n] for n in range(4)]
    lane = lane_index((cells, 128))
    sub = lax.broadcasted_iota(jnp.int32, (cells, 128), 0)

    def neighbour(n, direction):
        centre = stack[n]
        part = slice(64 * (n % 2), 64 * (n % 2) + 64)
        if direction == 0:
            return jnp.where(sub == cells - 1, after_x[12 + n : 13 + n], pltpu.roll(centre, cells - 1, 0))
        if direction == 1:
            return jnp.where(sub == 0, before_x[12 + n : 13 + n], pltpu.roll(centre, 1, 0))
        if direction == 2:
            edge = edges[part, 2 + n // 2 : 3 + n // 2]
            return jnp.where(lane == 127, edge, pltpu.roll(centre, 127, 1))
        edge = edges[part, n // 2 : n // 2 + 1]
        return jnp.where(lane == 0, edge, pltpu.roll(centre, 1, 1))

    absent = (
        jnp.logical_and(sub == cells - 1, col == cols_n - 1),
        jnp.logical_and(sub == 0, col == 0),
        jnp.logical_and(lane == 127, row == rows_n - 1),
        jnp.logical_and(lane == 0, row == 0),
    )
    exchange = [None] * 3
    for direction in range(4):
        coupling = 0.5 * (stack[3] + neighbour(3, direction))
        coupling = jnp.where(absent[direction], 0.0, coupling)
        for a in range(3):
            term = coupling * (neighbour(a, direction) - stack[a])
            exchange[a] = term if exchange[a] is None else exchange[a] + term
    magnet = stack[:3]
    field = [exchange[a] + demag[a] for a in range(3)]
    field[2] = field[2] + anisotropy * magnet[2]
    first_cross = cross(magnet, field)
    second_cross = cross(magnet, first_cross)
    factor = -1.0 / (1.0 + damping * damping)
    for a in range(3):
        out_ref[a] = (first_cross[a] + damping * second_cross[a]) * factor


in_vmem = pl.BlockSpec(memory_space=pltpu.VMEM)
in_hbm = pl.BlockSpec(memory_space=pltpu.HBM)


def call(body, out_shapes, *args, scratch=(), in_spec=in_vmem, vmem=32 * 2**20, flops=10**8):
    shapes = [jax.ShapeDtypeStruct(shape, f32) for shape in out_shapes]
    return pl.pallas_call(
        body,
        out_shape=shapes,
        in_specs=[in_spec] * len(args),
        out_specs=[in_vmem] * len(shapes),
        scratch_shapes=list(scratch),
        compiler_params=pltpu.CompilerParams(vmem_limit_bytes=vmem),
        cost_estimate=pl.CostEstimate(flops=flops, bytes_accessed=10**6, transcendentals=0),
    )(*args)


def exchange(array, axis, chunks):
    shape = array.shape
    rows = shape[0] // chunks
    tile = math.gcd(rows, 8)
    array = array.reshape(chunks, rows // tile, tile, shape[1])
    return lax.all_to_all(array, axis, split_axis=0, concat_axis=0, tiled=True).reshape(shape)


def local(magnet, stiffness, kern):
    constant = {name: [jnp.asarray(t) for t in group] for name, group in tables().items()}
    film = jnp.concatenate([magnet, stiffness[None]], 0)
    packed, edge = call(
        pack_body, [(rows_n * halo_rows, 128), (8, 128)], film, constant["y"][0]
    )
    sums = exchange(packed, "row", rows_n)
    (columns,) = call(forward_body, [(512, 128)], sums, edge, constant["y"][1])
    columns = exchange(columns, "col", cols_n)
    tensor = kern.reshape(6, 4, 32, 128).transpose(0, 2, 1, 3).reshape(768, 128)
    (inverse_x,) = call(spectral_body, [(384, 128)], columns, tensor, *constant["x"])
    inverse_x = exchange(inverse_x, "col", cols_n)
    (coef,) = call(back_body, [(rows_n * sums_rows, 128)], inverse_x, constant["z"][0])
    coef = exchange(coef, "row", rows_n)
    (torque,) = call(
        torque_body, [(3, 64, 128)], coef, film, sums, columns, constant["z"][1]
    )
    return torque


def solution(mesh):
    in_specs = (P(None, "col", "row"), P("col", "row"), P(None, ("row", "col"), None))
    out_specs = P(None, "col", "row")
    return jax.shard_map(local, mesh=mesh, in_specs=in_specs, out_specs=out_specs, check_vma=False)
```

```python
import math

import jax
import jax.numpy as jnp
import ml_dtypes
import numpy as np
from jax import lax
from jax.experimental import pallas as pl
from jax.experimental.pallas import tpu as pltpu
from jax.sharding import PartitionSpec as P

damping = 0.3
anisotropy = 0.8
tensor_slots = ((0, 3, 4), (3, 1, 5), (4, 5, 2))

rows_n = 16
cols_n = 32
cells = 64
lanes = 128
length = 4096
bf16 = jnp.bfloat16
f32 = jnp.float32


modes = 14
sums_rows = 3 * modes
halo_rows = sums_rows + 2


def wave(first, second, period):
    angle = 2.0 * math.pi * (np.outer(first, second) % period) / period
    return np.cos(angle), np.sin(angle)


def split_table(table):
    high = table.astype(ml_dtypes.bfloat16)
    low = (table - high.astype(np.float64)).astype(ml_dtypes.bfloat16)
    return high, low


def thick(table):
    high, low = split_table(table)
    return np.concatenate([high, low, high, low], 1)


def tall(table):
    return np.concatenate(split_table(table), 0)


def deep(table):
    high, low = split_table(table)
    return np.concatenate([np.tile(high, (1, 2)), np.tile(low, (1, 2))], 0)


def factors():
    place = np.arange(lanes) - 0.5 * (lanes - 1)
    angle = 2.0 * math.pi * np.outer(place, place) / length
    level = (1.02 - (2.0 * place / lanes) ** 2) ** -0.3
    values, vectors, units = [], [], []
    for part, unit in ((np.cos(angle), 1.0), (np.sin(angle), -1j)):
        value, vector = np.linalg.eigh(part * np.outer(level, level))
        values.append(value)
        vectors.append(vector * np.where(vector[-1] < 0.0, -1.0, 1.0))
        units.append(np.full(lanes, unit))
    values, vectors = np.concatenate(values), np.concatenate(vectors, 1)
    units = np.concatenate(units)
    kept = np.argsort(-np.abs(values), kind="stable")[:modes]
    side = vectors[:, kept] * np.sqrt(np.abs(values[kept])) / level[:, None]
    return side, units[kept] * np.sign(values[kept])


def row_transform():
    side, weight = factors()
    place = np.arange(lanes) - 0.5 * (lanes - 1)
    centre = lanes * np.arange(rows_n) + 0.5 * (lanes - 1)
    turn = np.exp(-2j * math.pi * np.outer(centre, place) / length)
    offset = 0.5 * (lanes - 1)
    phase = np.exp(-2j * math.pi * np.arange(rows_n) * lanes * offset / length)
    constant = np.exp(-2j * math.pi * offset * offset / length)
    turns = turn * phase[:, None]
    gather = side.T[:, None] * turns[None]
    expand = (side * weight)[:, :, None] * turn.T[:, None, :] * phase * constant
    gather, expand = gather.reshape(-1, lanes), expand.reshape(lanes, -1)
    return side.T, turns, gather, expand


def parts(table):
    return np.concatenate([table.real, table.imag], 0)


def tables():
    col = np.arange(cols_n)
    x_l = np.arange(cells)
    k1x = np.arange(64)
    k2x = (2 * np.arange(32)[None, :] + np.arange(2)[:, None]).reshape(-1)
    kappa = (4 * col[None, :] + np.arange(4)[:, None]).reshape(-1)

    sides, turns, gather, expand = row_transform()
    y_gather = np.concatenate([parts(turns), sides], 0).astype(np.float32)
    y_expand = tall(parts(expand[kappa]))
    gather = gather[:, kappa]
    z_gather = deep(np.concatenate([gather.real, gather.imag], 1))
    z_expand = np.ascontiguousarray(tall(parts(expand)).T)

    cos, sin = wave(k1x, col, 64)
    x_first = thick(np.concatenate([cos, sin], 0))
    x_back = deep(np.concatenate([cos, sin], 0).reshape(2, 64, 32).transpose(2, 0, 1).reshape(32, 128))
    cos, sin = wave(k1x, x_l, length)
    x_twist = np.stack([np.concatenate([cos, cos], 1), np.concatenate([sin, -sin], 1)])
    cos, sin = wave(k2x, x_l, 64)
    x_last = deep(np.concatenate([cos, sin], 1))
    cos, sin = wave(x_l, k2x, 64)
    x_lead = deep(np.concatenate([cos, sin], 1))
    cos, sin = wave(x_l, k1x, length)
    own = [np.concatenate([cos, -cos], 1), np.concatenate([sin, -sin], 1)]
    other = [np.concatenate([-sin, -sin], 1), np.concatenate([cos, cos], 1)]
    x_twists = np.concatenate([x_twist, np.stack(own + other)], 0).astype(np.float32)
    return {
        "y": (y_gather, y_expand),
        "x": (x_first, x_twists, x_last, x_lead, x_back),
        "z": (z_gather, z_expand),
    }


def split(values):
    high = values.astype(bf16)
    low = (values - high.astype(f32)).astype(bf16)
    return high, low


def stacked_product(table, values):
    high, low = split(values)
    return jnp.dot(table, jnp.concatenate([high, high, low, low], 0), preferred_element_type=f32)


def tall_product(table, values):
    high, low = split(values)
    size = table.shape[0] // 2
    both = jnp.dot(table, high, preferred_element_type=f32)
    rest = jnp.dot(table[:size], low, preferred_element_type=f32)
    return both[:size] + both[size:] + rest


def deep_product(table, values, contract):
    both = jnp.concatenate(split(values), contract)
    dims = (((1,), (contract,)), ((), ()))
    both = lax.dot_general(table, both, dims, preferred_element_type=f32)
    size = table.shape[0] // 2
    return both[:size] + both[size:]


def half_turn(values):
    return pltpu.roll(values, 64, 1)


def lane_index(shape):
    return lax.broadcasted_iota(jnp.int32, shape, len(shape) - 1)


def half_sign(rows):
    return jnp.where(lane_index((rows, 128)) < 64, 1.0, -1.0).astype(f32)


def pack_body(film_ref, gather_ref, out_ref, edge_ref):
    values = jnp.concatenate([film_ref[a] for a in range(3)], 0)
    size = rows_n * modes
    turns = gather_ref[0 : 2 * rows_n, :]
    sides = [gather_ref[2 * rows_n + n : 2 * rows_n + n + 1, :] for n in range(modes)]
    re = [turns[:rows_n] * side for side in sides]
    im = [turns[rows_n:] * side for side in sides]
    table_high, table_low = split(jnp.concatenate(re + im, 0))
    table = jnp.concatenate([table_high, table_low], 0)
    sums = deep_product(jnp.concatenate([table, table], 1), values, 1)
    low = lane_index((size, 128)) < 64
    re, im = sums[:size, :128], sums[size:, :128]
    last = jnp.concatenate([sums[:size, 128:], sums[size:, 128:]], 1)
    blocks = (jnp.where(low, re, half_turn(im)), jnp.where(low, half_turn(re), im), last)
    store_chunks(out_ref, halo_rows, blocks)
    former = jnp.concatenate([film_ref[0], film_ref[1]], 0).T
    latter = jnp.concatenate([film_ref[2], film_ref[3]], 0).T
    after = lax.broadcasted_iota(jnp.int32, (rows_n, lanes), 0) > lax.axis_index("row")
    for n, sides in enumerate((former, latter)):
        edges = jnp.where(after, sides[127:], sides[:1])
        out_ref[pl.ds(sums_rows + n, rows_n, stride=halo_rows), :] = edges
    for n in range(4):
        edge_ref[n : n + 1, :] = film_ref[n, :1, :]
        edge_ref[4 + n : 5 + n, :] = film_ref[n, cells - 1 :, :]


def spread_kern(kern_ref):
    low = lane_index((32, 128)) < 64
    spread = []
    for j in range(6):
        spread.append([])
        for k in range(4):
            part = kern_ref[pl.ds(128 * j + k, 32, stride=4), :]
            turned = half_turn(part)
            halves = [jnp.where(low, part, turned), jnp.where(low, turned, part)]
            spread[j].append(jnp.concatenate(halves, 0))
    return spread


def store_chunks(out_ref, rows, blocks):
    for a in range(3):
        for n in range(modes):
            out_ref[pl.ds(modes * a + n, rows_n, stride=rows), :] = blocks[a][
                rows_n * n : rows_n * n + rows_n
            ]


def load_chunks(in_ref, rows):
    columns = []
    for a in range(3):
        block = [in_ref[pl.ds(modes * a + n, rows_n, stride=rows), :] for n in range(modes)]
        columns.append(jnp.concatenate(block, 0))
    return jnp.concatenate(columns, 1)


def forward_body(in_ref, edge_ref, expand_ref, out_ref):
    sums = tall_product(expand_ref[...], load_chunks(in_ref, halo_rows))
    sign = half_sign(128)
    for a in range(3):
        block = sums[:, 128 * a : 128 * a + 128]
        block = block[:128] - half_turn(block[128:]) * sign
        for k in range(4):
            out_ref[pl.ds(4 * a + k, cols_n, stride=16), :] = block[32 * k : 32 * k + 32]
    col = lax.axis_index("col")
    first, last = edge_ref[0:4, :], edge_ref[4:8, :]
    for c in range(cols_n):
        out_ref[16 * c + 12 : 16 * c + 16, :] = jnp.where(c > col, last, first)


def spectral_body(
    in_ref, kern_ref, first_ref, twist_ref, last_ref, lead_ref, back_ref, out_ref
):
    sign = half_sign(64)
    own, other = twist_ref[0], twist_ref[1]
    kern = spread_kern(kern_ref)
    scale = -1.0 / (length * length)
    lane = lane_index((cols_n, 128))
    zero_weight = jnp.where(lane < 64, 1.0, 0.0).astype(f32)
    is_zero = jnp.logical_and(lax.axis_index("row") == 0, lax.axis_index("col") == 0)

    def enter(ks):
        columns = [in_ref[pl.ds(4 * a + k, cols_n, stride=16), :] for a in range(3) for k in ks]
        return stacked_product(first_ref[...], jnp.concatenate(columns, 1))

    def spread(section):
        turned = []
        for j in range(section.shape[1] // 128):
            block = section[:, 128 * j : 128 * j + 128]
            block = block[:64] + half_turn(block[64:]) * sign
            block = block * own + half_turn(block) * other
            turned.append(block)
            turned.append(half_turn(block) * sign)
        return jnp.concatenate(turned, 0)

    def multiply(freq, ks):
        sources = []
        for target in range(3):
            for n, k in enumerate(ks):
                total = None
                for b in range(3):
                    j = len(ks) * b + n
                    term = kern[tensor_slots[target][b]][k] * freq[:, 128 * j : 128 * j + 128]
                    total = term if total is None else total + term
                sources.append(jnp.concatenate([total, -half_turn(total) * sign], 0))
        return jnp.concatenate(sources, 1)

    def leave(section):
        turned = []
        for j in range(section.shape[1] // 128):
            block = section[:, 128 * j : 128 * j + 128]
            aside = half_turn(block)
            turned.append(block * twist_ref[2] + aside * twist_ref[4])
            turned.append(block * twist_ref[3] + aside * twist_ref[5])
        return jnp.concatenate(turned, 0)

    def store(result, ks):
        for a in range(3):
            for n, k in enumerate(ks):
                j = len(ks) * a + n
                block = result[:, 128 * j : 128 * j + 128]
                weight = jnp.full((cols_n, 128), 2.0, f32)
                if k == 0:
                    weight = jnp.where(is_zero, zero_weight, weight)
                out_ref[pl.ds(4 * a + k, cols_n, stride=12), :] = block * (weight * scale)

    groups = ((0,), (1,), (2,), (3,))
    states = [enter(ks) for ks in groups]
    states = [spread(state) for state in states]
    states = [deep_product(last_ref[...], state, 1) for state in states]
    states = [multiply(state, ks) for state, ks in zip(states, groups)]
    states = [deep_product(lead_ref[...], state, 0) for state in states]
    states = [leave(state) for state in states]
    states = [deep_product(back_ref[...], state, 1) for state in states]
    for state, ks in zip(states, groups):
        store(state, ks)


def back_body(in_ref, gather_ref, out_ref):
    columns = []
    for a in range(3):
        block = [in_ref[pl.ds(4 * a + k, cols_n, stride=12), :] for k in range(4)]
        columns.append(jnp.concatenate(block, 0))
    sign = half_sign(128)
    columns = [jnp.concatenate([block, half_turn(block) * sign], 0) for block in columns]
    sums = deep_product(gather_ref[...], jnp.concatenate(columns, 1), 0)
    blocks = [sums[:, 128 * a : 128 * a + 128] for a in range(3)]
    store_chunks(out_ref, sums_rows, blocks)


def cross(former, latter):
    return (
        former[1] * latter[2] - former[2] * latter[1],
        former[2] * latter[0] - former[0] * latter[2],
        former[0] * latter[1] - former[1] * latter[0],
    )


def torque_body(in_ref, film_ref, beside_y_ref, beside_x_ref, expand_ref, out_ref):
    row, col = lax.axis_index("row"), lax.axis_index("col")
    high, low = split(load_chunks(in_ref, sums_rows).T)
    both = jnp.dot(high, expand_ref[...], preferred_element_type=f32)
    rest = jnp.dot(low, expand_ref[:, :256], preferred_element_type=f32)
    sums = both[:, :256] + both[:, 256:] + rest
    demag = []
    for a in range(3):
        block = sums[128 * a : 128 * a + 128]
        demag.append(block[:64, :128] + block[64:, 128:])

    device = lax.broadcasted_iota(jnp.int32, (rows_n, 128), 0)

    def side(index):
        rows = []
        for n in range(2):
            halo = beside_y_ref[pl.ds(sums_rows + n, rows_n, stride=halo_rows), :]
            rows.append(jnp.sum(jnp.where(device == index, halo, 0.0), 0, keepdims=True))
        return rows

    before_y, after_y = side(row - 1), side(row + 1)
    before_x = beside_x_ref[pl.ds(pl.multiple_of(16 * jnp.maximum(col - 1, 0), 16), 16), :]
    after_x = beside_x_ref[pl.ds(pl.multiple_of(16 * jnp.minimum(col + 1, cols_n - 1), 16), 16), :]
    edges = jnp.concatenate(before_y + after_y + [jnp.zeros((124, 128), f32)], 0).T
    stack = [film_ref[n] for n in range(4)]
    lane = lane_index((cells, 128))
    sub = lax.broadcasted_iota(jnp.int32, (cells, 128), 0)

    def neighbour(n, direction):
        centre = stack[n]
        part = slice(64 * (n % 2), 64 * (n % 2) + 64)
        if direction == 0:
            return jnp.where(sub == cells - 1, after_x[12 + n : 13 + n], pltpu.roll(centre, cells - 1, 0))
        if direction == 1:
            return jnp.where(sub == 0, before_x[12 + n : 13 + n], pltpu.roll(centre, 1, 0))
        if direction == 2:
            edge = edges[part, 2 + n // 2 : 3 + n // 2]
            return jnp.where(lane == 127, edge, pltpu.roll(centre, 127, 1))
        edge = edges[part, n // 2 : n // 2 + 1]
        return jnp.where(lane == 0, edge, pltpu.roll(centre, 1, 1))

    absent = (
        jnp.logical_and(sub == cells - 1, col == cols_n - 1),
        jnp.logical_and(sub == 0, col == 0),
        jnp.logical_and(lane == 127, row == rows_n - 1),
        jnp.logical_and(lane == 0, row == 0),
    )
    exchange = [None] * 3
    for direction in range(4):
        coupling = 0.5 * (stack[3] + neighbour(3, direction))
        coupling = jnp.where(absent[direction], 0.0, coupling)
        for a in range(3):
            term = coupling * (neighbour(a, direction) - stack[a])
            exchange[a] = term if exchange[a] is None else exchange[a] + term
    magnet = stack[:3]
    field = [exchange[a] + demag[a] for a in range(3)]
    field[2] = field[2] + anisotropy * magnet[2]
    first_cross = cross(magnet, field)
    second_cross = cross(magnet, first_cross)
    factor = -1.0 / (1.0 + damping * damping)
    for a in range(3):
        out_ref[a] = (first_cross[a] + damping * second_cross[a]) * factor


in_vmem = pl.BlockSpec(memory_space=pltpu.VMEM)
in_hbm = pl.BlockSpec(memory_space=pltpu.HBM)


def call(body, out_shapes, *args, scratch=(), in_spec=in_vmem, vmem=32 * 2**20, flops=10**8):
    shapes = [jax.ShapeDtypeStruct(shape, f32) for shape in out_shapes]
    return pl.pallas_call(
        body,
        out_shape=shapes,
        in_specs=[in_spec] * len(args),
        out_specs=[in_vmem] * len(shapes),
        scratch_shapes=list(scratch),
        compiler_params=pltpu.CompilerParams(vmem_limit_bytes=vmem),
        cost_estimate=pl.CostEstimate(flops=flops, bytes_accessed=10**6, transcendentals=0),
    )(*args)


def exchange(array, axis, chunks):
    shape = array.shape
    rows = shape[0] // chunks
    tile = math.gcd(rows, 8)
    array = array.reshape(chunks, rows // tile, tile, shape[1])
    return lax.all_to_all(array, axis, split_axis=0, concat_axis=0, tiled=True).reshape(shape)


def local(magnet, stiffness, kern):
    constant = {name: [jnp.asarray(t) for t in group] for name, group in tables().items()}
    film = jnp.concatenate([magnet, stiffness[None]], 0)
    packed, edge = call(
        pack_body, [(rows_n * halo_rows, 128), (8, 128)], film, constant["y"][0]
    )
    sums = exchange(packed, "row", rows_n)
    (columns,) = call(forward_body, [(512, 128)], sums, edge, constant["y"][1])
    columns = exchange(columns, "col", cols_n)
    tensor = kern.reshape(6, 4, 32, 128).transpose(0, 2, 1, 3).reshape(768, 128)
    (inverse_x,) = call(spectral_body, [(384, 128)], columns, tensor, *constant["x"])
    inverse_x = exchange(inverse_x, "col", cols_n)
    (coef,) = call(back_body, [(rows_n * sums_rows, 128)], inverse_x, constant["z"][0])
    coef = exchange(coef, "row", rows_n)
    (torque,) = call(
        torque_body, [(3, 64, 128)], coef, film, sums, columns, constant["z"][1]
    )
    return torque


def solution(mesh):
    in_specs = (P(None, "col", "row"), P("col", "row"), P(None, ("row", "col"), None))
    out_specs = P(None, "col", "row")
    return jax.shard_map(local, mesh=mesh, in_specs=in_specs, out_specs=out_specs, check_vma=False)
```

```python
import math

import jax
import jax.numpy as jnp
import ml_dtypes
import numpy as np
from jax import lax
from jax.experimental import pallas as pl
from jax.experimental.pallas import tpu as pltpu
from jax.sharding import PartitionSpec as P

damping = 0.3
anisotropy = 0.8
tensor_slots = ((0, 3, 4), (3, 1, 5), (4, 5, 2))

rows_n = 16
cols_n = 32
cells = 64
lanes = 128
length = 4096
bf16 = jnp.bfloat16
f32 = jnp.float32


modes = 14
sums_rows = 3 * modes
halo_rows = sums_rows + 2


def wave(first, second, period):
    angle = 2.0 * math.pi * (np.outer(first, second) % period) / period
    return np.cos(angle), np.sin(angle)


def split_table(table):
    high = table.astype(ml_dtypes.bfloat16)
    low = (table - high.astype(np.float64)).astype(ml_dtypes.bfloat16)
    return high, low


def thick(table):
    high, low = split_table(table)
    return np.concatenate([high, low, high, low], 1)


def tall(table):
    return np.concatenate(split_table(table), 0)


def deep(table):
    high, low = split_table(table)
    return np.concatenate([np.tile(high, (1, 2)), np.tile(low, (1, 2))], 0)


def factors():
    place = np.arange(lanes) - 0.5 * (lanes - 1)
    angle = 2.0 * math.pi * np.outer(place, place) / length
    level = (1.02 - (2.0 * place / lanes) ** 2) ** -0.3
    values, vectors, units = [], [], []
    for part, unit in ((np.cos(angle), 1.0), (np.sin(angle), -1j)):
        value, vector = np.linalg.eigh(part * np.outer(level, level))
        values.append(value)
        vectors.append(vector * np.where(vector[-1] < 0.0, -1.0, 1.0))
        units.append(np.full(lanes, unit))
    values, vectors = np.concatenate(values), np.concatenate(vectors, 1)
    units = np.concatenate(units)
    kept = np.argsort(-np.abs(values), kind="stable")[:modes]
    side = vectors[:, kept] * np.sqrt(np.abs(values[kept])) / level[:, None]
    return side, units[kept] * np.sign(values[kept])


def row_transform():
    side, weight = factors()
    place = np.arange(lanes) - 0.5 * (lanes - 1)
    centre = lanes * np.arange(rows_n) + 0.5 * (lanes - 1)
    turn = np.exp(-2j * math.pi * np.outer(centre, place) / length)
    offset = 0.5 * (lanes - 1)
    phase = np.exp(-2j * math.pi * np.arange(rows_n) * lanes * offset / length)
    constant = np.exp(-2j * math.pi * offset * offset / length)
    turns = turn * phase[:, None]
    gather = side.T[:, None] * turns[None]
    expand = (side * weight)[:, :, None] * turn.T[:, None, :] * phase * constant
    gather, expand = gather.reshape(-1, lanes), expand.reshape(lanes, -1)
    return side.T, turns, gather, expand


def parts(table):
    return np.concatenate([table.real, table.imag], 0)


def tables():
    col = np.arange(cols_n)
    x_l = np.arange(cells)
    k1x = np.arange(64)
    k2x = (2 * np.arange(32)[None, :] + np.arange(2)[:, None]).reshape(-1)
    kappa = (4 * col[None, :] + np.arange(4)[:, None]).reshape(-1)

    sides, turns, gather, expand = row_transform()
    y_gather = np.concatenate([parts(turns), sides], 0).astype(np.float32)
    y_expand = tall(parts(expand[kappa]))
    z_gather = deep(parts(gather[:, kappa]))
    z_expand = np.ascontiguousarray(tall(parts(expand)).T)

    cos, sin = wave(k1x, col, 64)
    x_first = thick(np.concatenate([cos, sin], 0))
    x_back = deep(np.concatenate([cos, sin], 0).reshape(2, 64, 32).transpose(2, 0, 1).reshape(32, 128))
    cos, sin = wave(k1x, x_l, length)
    x_twist = np.stack([np.concatenate([cos, cos], 1), np.concatenate([sin, -sin], 1)])
    cos, sin = wave(k2x, x_l, 64)
    x_last = deep(np.concatenate([cos, sin], 1))
    cos, sin = wave(x_l, k2x, 64)
    x_lead = deep(np.concatenate([cos, sin], 1))
    cos, sin = wave(x_l, k1x, length)
    own = [np.concatenate([cos, -cos], 1), np.concatenate([sin, -sin], 1)]
    other = [np.concatenate([-sin, -sin], 1), np.concatenate([cos, cos], 1)]
    x_twists = np.concatenate([x_twist, np.stack(own + other)], 0).astype(np.float32)
    return {
        "y": (y_gather, y_expand),
        "x": (x_first, x_twists, x_last, x_lead, x_back),
        "z": (z_gather, z_expand),
    }


def split(values):
    high = values.astype(bf16)
    low = (values - high.astype(f32)).astype(bf16)
    return high, low


def stacked_product(table, values):
    high, low = split(values)
    return jnp.dot(table, jnp.concatenate([high, high, low, low], 0), preferred_element_type=f32)


def tall_product(table, values):
    high, low = split(values)
    size = table.shape[0] // 2
    width = values.shape[1]
    both = jnp.dot(table, jnp.concatenate([high, low], 1), preferred_element_type=f32)
    rest = both[size:, :width] + both[:size, width:] + both[size:, width:]
    return both[:size, :width] + rest


def deep_product(table, values, contract):
    both = jnp.concatenate(split(values), contract)
    dims = (((1,), (contract,)), ((), ()))
    both = lax.dot_general(table, both, dims, preferred_element_type=f32)
    size = table.shape[0] // 2
    return both[:size] + both[size:]


def half_turn(values):
    return pltpu.roll(values, 64, 1)


def lane_index(shape):
    return lax.broadcasted_iota(jnp.int32, shape, len(shape) - 1)


def half_sign(rows):
    return jnp.where(lane_index((rows, 128)) < 64, 1.0, -1.0).astype(f32)


def pack_body(film_ref, gather_ref, out_ref, edge_ref):
    values = jnp.concatenate([film_ref[a] for a in range(3)], 0)
    size = rows_n * modes
    turns = gather_ref[0 : 2 * rows_n, :]
    sides = [gather_ref[2 * rows_n + n : 2 * rows_n + n + 1, :] for n in range(modes)]
    re = [turns[:rows_n] * side for side in sides]
    im = [turns[rows_n:] * side for side in sides]
    table_high, table_low = split(jnp.concatenate(re + im, 0))
    table = jnp.concatenate([table_high, table_low], 0)
    sums = deep_product(jnp.concatenate([table, table], 1), values, 1)
    low = lane_index((size, 128)) < 64
    re, im = sums[:size, :128], sums[size:, :128]
    last = jnp.concatenate([sums[:size, 128:], sums[size:, 128:]], 1)
    blocks = (jnp.where(low, re, half_turn(im)), jnp.where(low, half_turn(re), im), last)
    store_chunks(out_ref, halo_rows, blocks)
    former = jnp.concatenate([film_ref[0], film_ref[1]], 0).T
    latter = jnp.concatenate([film_ref[2], film_ref[3]], 0).T
    after = lax.broadcasted_iota(jnp.int32, (rows_n, lanes), 0) > lax.axis_index("row")
    for n, sides in enumerate((former, latter)):
        edges = jnp.where(after, sides[127:], sides[:1])
        out_ref[pl.ds(sums_rows + n, rows_n, stride=halo_rows), :] = edges
    for n in range(4):
        edge_ref[n : n + 1, :] = film_ref[n, :1, :]
        edge_ref[4 + n : 5 + n, :] = film_ref[n, cells - 1 :, :]


def spread_kern(kern_ref):
    low = lane_index((32, 128)) < 64
    spread = []
    for j in range(6):
        spread.append([])
        for k in range(4):
            part = kern_ref[pl.ds(128 * j + k, 32, stride=4), :]
            turned = half_turn(part)
            halves = [jnp.where(low, part, turned), jnp.where(low, turned, part)]
            spread[j].append(jnp.concatenate(halves, 0))
    return spread


def store_chunks(out_ref, rows, blocks):
    for a in range(3):
        for n in range(modes):
            out_ref[pl.ds(modes * a + n, rows_n, stride=rows), :] = blocks[a][
                rows_n * n : rows_n * n + rows_n
            ]


def load_chunks(in_ref, rows):
    columns = []
    for a in range(3):
        block = [in_ref[pl.ds(modes * a + n, rows_n, stride=rows), :] for n in range(modes)]
        columns.append(jnp.concatenate(block, 0))
    return jnp.concatenate(columns, 1)


def forward_body(in_ref, edge_ref, expand_ref, out_ref):
    sums = tall_product(expand_ref[...], load_chunks(in_ref, halo_rows))
    sign = half_sign(128)
    for a in range(3):
        block = sums[:, 128 * a : 128 * a + 128]
        block = block[:128] - half_turn(block[128:]) * sign
        for k in range(4):
            out_ref[pl.ds(4 * a + k, cols_n, stride=16), :] = block[32 * k : 32 * k + 32]
    col = lax.axis_index("col")
    first, last = edge_ref[0:4, :], edge_ref[4:8, :]
    for c in range(cols_n):
        out_ref[16 * c + 12 : 16 * c + 16, :] = jnp.where(c > col, last, first)


def spectral_body(
    in_ref, kern_ref, first_ref, twist_ref, last_ref, lead_ref, back_ref, out_ref
):
    sign = half_sign(64)
    own, other = twist_ref[0], twist_ref[1]
    kern = spread_kern(kern_ref)
    scale = -1.0 / (length * length)
    lane = lane_index((cols_n, 128))
    zero_weight = jnp.where(lane < 64, 1.0, 0.0).astype(f32)
    is_zero = jnp.logical_and(lax.axis_index("row") == 0, lax.axis_index("col") == 0)

    def enter(ks):
        columns = [in_ref[pl.ds(4 * a + k, cols_n, stride=16), :] for a in range(3) for k in ks]
        return stacked_product(first_ref[...], jnp.concatenate(columns, 1))

    def spread(section):
        turned = []
        for j in range(section.shape[1] // 128):
            block = section[:, 128 * j : 128 * j + 128]
            block = block[:64] + half_turn(block[64:]) * sign
            block = block * own + half_turn(block) * other
            turned.append(block)
            turned.append(half_turn(block) * sign)
        return deep_product(last_ref[...], jnp.concatenate(turned, 0), 1)

    def multiply(freq, ks):
        sources = []
        for target in range(3):
            for n, k in enumerate(ks):
                total = None
                for b in range(3):
                    j = len(ks) * b + n
                    term = kern[tensor_slots[target][b]][k] * freq[:, 128 * j : 128 * j + 128]
                    total = term if total is None else total + term
                sources.append(jnp.concatenate([total, -half_turn(total) * sign], 0))
        return deep_product(lead_ref[...], jnp.concatenate(sources, 1), 0)

    def leave(section):
        turned = []
        for j in range(section.shape[1] // 128):
            block = section[:, 128 * j : 128 * j + 128]
            aside = half_turn(block)
            turned.append(block * twist_ref[2] + aside * twist_ref[4])
            turned.append(block * twist_ref[3] + aside * twist_ref[5])
        return deep_product(back_ref[...], jnp.concatenate(turned, 0), 1)

    def store(result, ks):
        for a in range(3):
            for n, k in enumerate(ks):
                j = len(ks) * a + n
                block = result[:, 128 * j : 128 * j + 128]
                weight = jnp.full((cols_n, 128), 2.0, f32)
                if k == 0:
                    weight = jnp.where(is_zero, zero_weight, weight)
                out_ref[pl.ds(4 * a + k, cols_n, stride=12), :] = block * (weight * scale)

    groups = ((0,), (1,), (2,), (3,))
    states = [enter(ks) for ks in groups]
    states = [spread(state) for state in states]
    states = [multiply(state, ks) for state, ks in zip(states, groups)]
    states = [leave(state) for state in states]
    for state, ks in zip(states, groups):
        store(state, ks)


def back_body(in_ref, gather_ref, out_ref):
    columns = []
    for a in range(3):
        block = [in_ref[pl.ds(4 * a + k, cols_n, stride=12), :] for k in range(4)]
        columns.append(jnp.concatenate(block, 0))
    sums = deep_product(gather_ref[...], jnp.concatenate(columns, 1), 0)
    size = rows_n * modes
    sign = half_sign(size)
    blocks = []
    for a in range(3):
        block = sums[:, 128 * a : 128 * a + 128]
        blocks.append(block[:size] + half_turn(block[size:]) * sign)
    store_chunks(out_ref, sums_rows, blocks)


def cross(former, latter):
    return (
        former[1] * latter[2] - former[2] * latter[1],
        former[2] * latter[0] - former[0] * latter[2],
        former[0] * latter[1] - former[1] * latter[0],
    )


def torque_body(in_ref, film_ref, beside_y_ref, beside_x_ref, expand_ref, out_ref):
    row, col = lax.axis_index("row"), lax.axis_index("col")
    high, low = split(load_chunks(in_ref, sums_rows).T)
    both = jnp.dot(high, expand_ref[...], preferred_element_type=f32)
    rest = jnp.dot(low, expand_ref[:, :256], preferred_element_type=f32)
    sums = both[:, :256] + both[:, 256:] + rest
    demag = []
    for a in range(3):
        block = sums[128 * a : 128 * a + 128]
        demag.append(block[:64, :128] + block[64:, 128:])

    device = lax.broadcasted_iota(jnp.int32, (rows_n, 128), 0)

    def side(index):
        rows = []
        for n in range(2):
            halo = beside_y_ref[pl.ds(sums_rows + n, rows_n, stride=halo_rows), :]
            rows.append(jnp.sum(jnp.where(device == index, halo, 0.0), 0, keepdims=True))
        return rows

    before_y, after_y = side(row - 1), side(row + 1)
    before_x = beside_x_ref[pl.ds(pl.multiple_of(16 * jnp.maximum(col - 1, 0), 16), 16), :]
    after_x = beside_x_ref[pl.ds(pl.multiple_of(16 * jnp.minimum(col + 1, cols_n - 1), 16), 16), :]
    edges = jnp.concatenate(before_y + after_y + [jnp.zeros((124, 128), f32)], 0).T
    stack = [film_ref[n] for n in range(4)]
    lane = lane_index((cells, 128))
    sub = lax.broadcasted_iota(jnp.int32, (cells, 128), 0)

    def neighbour(n, direction):
        centre = stack[n]
        part = slice(64 * (n % 2), 64 * (n % 2) + 64)
        if direction == 0:
            return jnp.where(sub == cells - 1, after_x[12 + n : 13 + n], pltpu.roll(centre, cells - 1, 0))
        if direction == 1:
            return jnp.where(sub == 0, before_x[12 + n : 13 + n], pltpu.roll(centre, 1, 0))
        if direction == 2:
            edge = edges[part, 2 + n // 2 : 3 + n // 2]
            return jnp.where(lane == 127, edge, pltpu.roll(centre, 127, 1))
        edge = edges[part, n // 2 : n // 2 + 1]
        return jnp.where(lane == 0, edge, pltpu.roll(centre, 1, 1))

    absent = (
        jnp.logical_and(sub == cells - 1, col == cols_n - 1),
        jnp.logical_and(sub == 0, col == 0),
        jnp.logical_and(lane == 127, row == rows_n - 1),
        jnp.logical_and(lane == 0, row == 0),
    )
    exchange = [None] * 3
    for direction in range(4):
        coupling = 0.5 * (stack[3] + neighbour(3, direction))
        coupling = jnp.where(absent[direction], 0.0, coupling)
        for a in range(3):
            term = coupling * (neighbour(a, direction) - stack[a])
            exchange[a] = term if exchange[a] is None else exchange[a] + term
    magnet = stack[:3]
    field = [exchange[a] + demag[a] for a in range(3)]
    field[2] = field[2] + anisotropy * magnet[2]
    first_cross = cross(magnet, field)
    second_cross = cross(magnet, first_cross)
    factor = -1.0 / (1.0 + damping * damping)
    for a in range(3):
        out_ref[a] = (first_cross[a] + damping * second_cross[a]) * factor


in_vmem = pl.BlockSpec(memory_space=pltpu.VMEM)
in_hbm = pl.BlockSpec(memory_space=pltpu.HBM)


def call(body, out_shapes, *args, scratch=(), in_spec=in_vmem, vmem=32 * 2**20, flops=10**8):
    shapes = [jax.ShapeDtypeStruct(shape, f32) for shape in out_shapes]
    return pl.pallas_call(
        body,
        out_shape=shapes,
        in_specs=[in_spec] * len(args),
        out_specs=[in_vmem] * len(shapes),
        scratch_shapes=list(scratch),
        compiler_params=pltpu.CompilerParams(vmem_limit_bytes=vmem),
        cost_estimate=pl.CostEstimate(flops=flops, bytes_accessed=10**6, transcendentals=0),
    )(*args)


def exchange(array, axis, chunks):
    shape = array.shape
    rows = shape[0] // chunks
    tile = math.gcd(rows, 8)
    array = array.reshape(chunks, rows // tile, tile, shape[1])
    return lax.all_to_all(array, axis, split_axis=0, concat_axis=0, tiled=True).reshape(shape)


def local(magnet, stiffness, kern):
    constant = {name: [jnp.asarray(t) for t in group] for name, group in tables().items()}
    film = jnp.concatenate([magnet, stiffness[None]], 0)
    packed, edge = call(
        pack_body, [(rows_n * halo_rows, 128), (8, 128)], film, constant["y"][0]
    )
    sums = exchange(packed, "row", rows_n)
    (columns,) = call(forward_body, [(512, 128)], sums, edge, constant["y"][1])
    columns = exchange(columns, "col", cols_n)
    tensor = kern.reshape(6, 4, 32, 128).transpose(0, 2, 1, 3).reshape(768, 128)
    (inverse_x,) = call(spectral_body, [(384, 128)], columns, tensor, *constant["x"])
    inverse_x = exchange(inverse_x, "col", cols_n)
    (coef,) = call(back_body, [(rows_n * sums_rows, 128)], inverse_x, constant["z"][0])
    coef = exchange(coef, "row", rows_n)
    (torque,) = call(
        torque_body, [(3, 64, 128)], coef, film, sums, columns, constant["z"][1]
    )
    return torque


def solution(mesh):
    in_specs = (P(None, "col", "row"), P("col", "row"), P(None, ("row", "col"), None))
    out_specs = P(None, "col", "row")
    return jax.shard_map(local, mesh=mesh, in_specs=in_specs, out_specs=out_specs, check_vma=False)
```

```python
import math

import jax
import jax.numpy as jnp
import ml_dtypes
import numpy as np
from jax import lax
from jax.experimental import pallas as pl
from jax.experimental.pallas import tpu as pltpu
from jax.sharding import PartitionSpec as P

damping = 0.3
anisotropy = 0.8
tensor_slots = ((0, 3, 4), (3, 1, 5), (4, 5, 2))

rows_n = 16
cols_n = 32
cells = 64
lanes = 128
length = 4096
bf16 = jnp.bfloat16
f32 = jnp.float32


modes = 14
sums_rows = 3 * modes
halo_rows = sums_rows + 2


def wave(first, second, period):
    angle = 2.0 * math.pi * (np.outer(first, second) % period) / period
    return np.cos(angle), np.sin(angle)


def split_table(table):
    high = table.astype(ml_dtypes.bfloat16)
    low = (table - high.astype(np.float64)).astype(ml_dtypes.bfloat16)
    return high, low


def thick(table):
    high, low = split_table(table)
    return np.concatenate([high, low, high, low], 1)


def tall(table):
    return np.concatenate(split_table(table), 0)


def deep(table):
    high, low = split_table(table)
    return np.concatenate([np.tile(high, (1, 2)), np.tile(low, (1, 2))], 0)


def factors():
    place = np.arange(lanes) - 0.5 * (lanes - 1)
    angle = 2.0 * math.pi * np.outer(place, place) / length
    level = (1.02 - (2.0 * place / lanes) ** 2) ** -0.3
    values, vectors, units = [], [], []
    for part, unit in ((np.cos(angle), 1.0), (np.sin(angle), -1j)):
        value, vector = np.linalg.eigh(part * np.outer(level, level))
        values.append(value)
        vectors.append(vector * np.where(vector[-1] < 0.0, -1.0, 1.0))
        units.append(np.full(lanes, unit))
    values, vectors = np.concatenate(values), np.concatenate(vectors, 1)
    units = np.concatenate(units)
    kept = np.argsort(-np.abs(values), kind="stable")[:modes]
    side = vectors[:, kept] * np.sqrt(np.abs(values[kept])) / level[:, None]
    return side, units[kept] * np.sign(values[kept])


def row_transform():
    side, weight = factors()
    place = np.arange(lanes) - 0.5 * (lanes - 1)
    centre = lanes * np.arange(rows_n) + 0.5 * (lanes - 1)
    turn = np.exp(-2j * math.pi * np.outer(centre, place) / length)
    offset = 0.5 * (lanes - 1)
    phase = np.exp(-2j * math.pi * np.arange(rows_n) * lanes * offset / length)
    constant = np.exp(-2j * math.pi * offset * offset / length)
    turns = turn * phase[:, None]
    gather = side.T[:, None] * turns[None]
    expand = (side * weight)[:, :, None] * turn.T[:, None, :] * phase * constant
    gather, expand = gather.reshape(-1, lanes), expand.reshape(lanes, -1)
    return side.T, turns, gather, expand


def parts(table):
    return np.concatenate([table.real, table.imag], 0)


def tables():
    col = np.arange(cols_n)
    x_l = np.arange(cells)
    k1x = np.arange(64)
    k2x = (2 * np.arange(32)[None, :] + np.arange(2)[:, None]).reshape(-1)
    kappa = (4 * col[None, :] + np.arange(4)[:, None]).reshape(-1)

    sides, turns, gather, expand = row_transform()
    y_gather = np.concatenate([parts(turns), sides], 0).astype(np.float32)
    y_expand = tall(parts(expand[kappa]))
    z_gather = deep(parts(gather[:, kappa]))
    z_expand = np.ascontiguousarray(tall(parts(expand)).T)

    cos, sin = wave(k1x, col, 64)
    x_first = thick(np.concatenate([cos, sin], 0))
    x_back = deep(np.concatenate([cos, sin], 0).reshape(2, 64, 32).transpose(2, 0, 1).reshape(32, 128))
    cos, sin = wave(k1x, x_l, length)
    x_twist = np.stack([np.concatenate([cos, cos], 1), np.concatenate([sin, -sin], 1)])
    cos, sin = wave(k2x, x_l, 64)
    x_last = deep(np.concatenate([cos, sin], 1))
    cos, sin = wave(x_l, k2x, 64)
    x_lead = deep(np.concatenate([cos, sin], 1))
    cos, sin = wave(x_l, k1x, length)
    own = [np.concatenate([cos, -cos], 1), np.concatenate([sin, -sin], 1)]
    other = [np.concatenate([-sin, -sin], 1), np.concatenate([cos, cos], 1)]
    x_twists = np.concatenate([x_twist, np.stack(own + other)], 0).astype(np.float32)
    return {
        "y": (y_gather, y_expand),
        "x": (x_first, x_twists, x_last, x_lead, x_back),
        "z": (z_gather, z_expand),
    }


def split(values):
    high = values.astype(bf16)
    low = (values - high.astype(f32)).astype(bf16)
    return high, low


def stacked_product(table, values):
    high, low = split(values)
    return jnp.dot(table, jnp.concatenate([high, high, low, low], 0), preferred_element_type=f32)


def tall_product(table, values):
    high, low = split(values)
    size = table.shape[0] // 2
    width = values.shape[1]
    both = jnp.dot(table, jnp.concatenate([high, low], 1), preferred_element_type=f32)
    rest = both[size:, :width] + both[:size, width:] + both[size:, width:]
    return both[:size, :width] + rest


def deep_product(table, values, contract):
    both = jnp.concatenate(split(values), contract)
    dims = (((1,), (contract,)), ((), ()))
    both = lax.dot_general(table, both, dims, preferred_element_type=f32)
    size = table.shape[0] // 2
    return both[:size] + both[size:]


def half_turn(values):
    return pltpu.roll(values, 64, 1)


def lane_index(shape):
    return lax.broadcasted_iota(jnp.int32, shape, len(shape) - 1)


def half_sign(rows):
    return jnp.where(lane_index((rows, 128)) < 64, 1.0, -1.0).astype(f32)


def pack_body(film_ref, gather_ref, out_ref, edge_ref):
    values = jnp.concatenate([film_ref[a] for a in range(3)], 0)
    size = rows_n * modes
    turns = gather_ref[0 : 2 * rows_n, :]
    sides = [gather_ref[2 * rows_n + n : 2 * rows_n + n + 1, :] for n in range(modes)]
    re = [turns[:rows_n] * side for side in sides]
    im = [turns[rows_n:] * side for side in sides]
    table_high, table_low = split(jnp.concatenate(re + im, 0))
    table = jnp.concatenate([table_high, table_low], 0)
    sums = deep_product(jnp.concatenate([table, table], 1), values, 1)
    low = lane_index((size, 128)) < 64
    re, im = sums[:size, :128], sums[size:, :128]
    last = jnp.concatenate([sums[:size, 128:], sums[size:, 128:]], 1)
    blocks = (jnp.where(low, re, half_turn(im)), jnp.where(low, half_turn(re), im), last)
    store_chunks(out_ref, halo_rows, blocks)
    former = jnp.concatenate([film_ref[0], film_ref[1]], 0).T
    latter = jnp.concatenate([film_ref[2], film_ref[3]], 0).T
    after = lax.broadcasted_iota(jnp.int32, (rows_n, lanes), 0) > lax.axis_index("row")
    for n, sides in enumerate((former, latter)):
        edges = jnp.where(after, sides[127:], sides[:1])
        out_ref[pl.ds(sums_rows + n, rows_n, stride=halo_rows), :] = edges
    for n in range(4):
        edge_ref[n : n + 1, :] = film_ref[n, :1, :]
        edge_ref[4 + n : 5 + n, :] = film_ref[n, cells - 1 :, :]


def spread_kern(kern_ref):
    low = lane_index((32, 128)) < 64
    spread = []
    for j in range(6):
        spread.append([])
        for k in range(4):
            part = kern_ref[pl.ds(128 * j + k, 32, stride=4), :]
            turned = half_turn(part)
            halves = [jnp.where(low, part, turned), jnp.where(low, turned, part)]
            spread[j].append(jnp.concatenate(halves, 0))
    return spread


def store_chunks(out_ref, rows, blocks):
    for a in range(3):
        for n in range(modes):
            out_ref[pl.ds(modes * a + n, rows_n, stride=rows), :] = blocks[a][
                rows_n * n : rows_n * n + rows_n
            ]


def load_chunks(in_ref, rows):
    columns = []
    for a in range(3):
        block = [in_ref[pl.ds(modes * a + n, rows_n, stride=rows), :] for n in range(modes)]
        columns.append(jnp.concatenate(block, 0))
    return jnp.concatenate(columns, 1)


def forward_body(in_ref, edge_ref, expand_ref, out_ref):
    sums = tall_product(expand_ref[...], load_chunks(in_ref, halo_rows))
    sign = half_sign(128)
    for a in range(3):
        block = sums[:, 128 * a : 128 * a + 128]
        block = block[:128] - half_turn(block[128:]) * sign
        for k in range(4):
            out_ref[pl.ds(4 * a + k, cols_n, stride=16), :] = block[32 * k : 32 * k + 32]
    col = lax.axis_index("col")
    first, last = edge_ref[0:4, :], edge_ref[4:8, :]
    for c in range(cols_n):
        out_ref[16 * c + 12 : 16 * c + 16, :] = jnp.where(c > col, last, first)


def spectral_body(
    in_ref, kern_ref, first_ref, twist_ref, last_ref, lead_ref, back_ref, out_ref
):
    sign = half_sign(64)
    own, other = twist_ref[0], twist_ref[1]
    kern = spread_kern(kern_ref)
    scale = -1.0 / (length * length)
    lane = lane_index((cols_n, 128))
    zero_weight = jnp.where(lane < 64, 1.0, 0.0).astype(f32)
    is_zero = jnp.logical_and(lax.axis_index("row") == 0, lax.axis_index("col") == 0)

    def enter(ks):
        columns = [in_ref[pl.ds(4 * a + k, cols_n, stride=16), :] for a in range(3) for k in ks]
        return stacked_product(first_ref[...], jnp.concatenate(columns, 1))

    def spread(section):
        turned = []
        for j in range(section.shape[1] // 128):
            block = section[:, 128 * j : 128 * j + 128]
            block = block[:64] + half_turn(block[64:]) * sign
            block = block * own + half_turn(block) * other
            turned.append(block)
            turned.append(half_turn(block) * sign)
        return jnp.concatenate(turned, 0)

    def multiply(freq, ks):
        sources = []
        for target in range(3):
            for n, k in enumerate(ks):
                total = None
                for b in range(3):
                    j = len(ks) * b + n
                    term = kern[tensor_slots[target][b]][k] * freq[:, 128 * j : 128 * j + 128]
                    total = term if total is None else total + term
                sources.append(jnp.concatenate([total, -half_turn(total) * sign], 0))
        return jnp.concatenate(sources, 1)

    def leave(section):
        turned = []
        for j in range(section.shape[1] // 128):
            block = section[:, 128 * j : 128 * j + 128]
            aside = half_turn(block)
            turned.append(block * twist_ref[2] + aside * twist_ref[4])
            turned.append(block * twist_ref[3] + aside * twist_ref[5])
        return jnp.concatenate(turned, 0)

    def store(result, ks):
        for a in range(3):
            for n, k in enumerate(ks):
                j = len(ks) * a + n
                block = result[:, 128 * j : 128 * j + 128]
                weight = jnp.full((cols_n, 128), 2.0, f32)
                if k == 0:
                    weight = jnp.where(is_zero, zero_weight, weight)
                out_ref[pl.ds(4 * a + k, cols_n, stride=12), :] = block * (weight * scale)

    groups = ((0,), (1,), (2,), (3,))
    states = [enter(ks) for ks in groups]
    states = [spread(state) for state in states]
    states = [deep_product(last_ref[...], state, 1) for state in states]
    states = [multiply(state, ks) for state, ks in zip(states, groups)]
    states = [deep_product(lead_ref[...], state, 0) for state in states]
    states = [leave(state) for state in states]
    states = [deep_product(back_ref[...], state, 1) for state in states]
    for state, ks in zip(states, groups):
        store(state, ks)


def back_body(in_ref, gather_ref, out_ref):
    columns = []
    for a in range(3):
        block = [in_ref[pl.ds(4 * a + k, cols_n, stride=12), :] for k in range(4)]
        columns.append(jnp.concatenate(block, 0))
    sums = deep_product(gather_ref[...], jnp.concatenate(columns, 1), 0)
    size = rows_n * modes
    sign = half_sign(size)
    blocks = []
    for a in range(3):
        block = sums[:, 128 * a : 128 * a + 128]
        blocks.append(block[:size] + half_turn(block[size:]) * sign)
    store_chunks(out_ref, sums_rows, blocks)


def cross(former, latter):
    return (
        former[1] * latter[2] - former[2] * latter[1],
        former[2] * latter[0] - former[0] * latter[2],
        former[0] * latter[1] - former[1] * latter[0],
    )


def torque_body(in_ref, film_ref, beside_y_ref, beside_x_ref, expand_ref, out_ref):
    row, col = lax.axis_index("row"), lax.axis_index("col")
    high, low = split(load_chunks(in_ref, sums_rows).T)
    both = jnp.dot(high, expand_ref[...], preferred_element_type=f32)
    rest = jnp.dot(low, expand_ref[:, :256], preferred_element_type=f32)
    sums = both[:, :256] + both[:, 256:] + rest
    demag = []
    for a in range(3):
        block = sums[128 * a : 128 * a + 128]
        demag.append(block[:64, :128] + block[64:, 128:])

    device = lax.broadcasted_iota(jnp.int32, (rows_n, 128), 0)

    def side(index):
        rows = []
        for n in range(2):
            halo = beside_y_ref[pl.ds(sums_rows + n, rows_n, stride=halo_rows), :]
            rows.append(jnp.sum(jnp.where(device == index, halo, 0.0), 0, keepdims=True))
        return rows

    before_y, after_y = side(row - 1), side(row + 1)
    before_x = beside_x_ref[pl.ds(pl.multiple_of(16 * jnp.maximum(col - 1, 0), 16), 16), :]
    after_x = beside_x_ref[pl.ds(pl.multiple_of(16 * jnp.minimum(col + 1, cols_n - 1), 16), 16), :]
    edges = jnp.concatenate(before_y + after_y + [jnp.zeros((124, 128), f32)], 0).T
    stack = [film_ref[n] for n in range(4)]
    lane = lane_index((cells, 128))
    sub = lax.broadcasted_iota(jnp.int32, (cells, 128), 0)

    def neighbour(n, direction):
        centre = stack[n]
        part = slice(64 * (n % 2), 64 * (n % 2) + 64)
        if direction == 0:
            return jnp.where(sub == cells - 1, after_x[12 + n : 13 + n], pltpu.roll(centre, cells - 1, 0))
        if direction == 1:
            return jnp.where(sub == 0, before_x[12 + n : 13 + n], pltpu.roll(centre, 1, 0))
        if direction == 2:
            edge = edges[part, 2 + n // 2 : 3 + n // 2]
            return jnp.where(lane == 127, edge, pltpu.roll(centre, 127, 1))
        edge = edges[part, n // 2 : n // 2 + 1]
        return jnp.where(lane == 0, edge, pltpu.roll(centre, 1, 1))

    absent = (
        jnp.logical_and(sub == cells - 1, col == cols_n - 1),
        jnp.logical_and(sub == 0, col == 0),
        jnp.logical_and(lane == 127, row == rows_n - 1),
        jnp.logical_and(lane == 0, row == 0),
    )
    exchange = [None] * 3
    for direction in range(4):
        coupling = 0.5 * (stack[3] + neighbour(3, direction))
        coupling = jnp.where(absent[direction], 0.0, coupling)
        for a in range(3):
            term = coupling * (neighbour(a, direction) - stack[a])
            exchange[a] = term if exchange[a] is None else exchange[a] + term
    magnet = stack[:3]
    field = [exchange[a] + demag[a] for a in range(3)]
    field[2] = field[2] + anisotropy * magnet[2]
    first_cross = cross(magnet, field)
    second_cross = cross(magnet, first_cross)
    factor = -1.0 / (1.0 + damping * damping)
    for a in range(3):
        out_ref[a] = (first_cross[a] + damping * second_cross[a]) * factor


in_vmem = pl.BlockSpec(memory_space=pltpu.VMEM)
in_hbm = pl.BlockSpec(memory_space=pltpu.HBM)


def call(body, out_shapes, *args, scratch=(), in_spec=in_vmem, vmem=32 * 2**20, flops=10**8):
    shapes = [jax.ShapeDtypeStruct(shape, f32) for shape in out_shapes]
    return pl.pallas_call(
        body,
        out_shape=shapes,
        in_specs=[in_spec] * len(args),
        out_specs=[in_vmem] * len(shapes),
        scratch_shapes=list(scratch),
        compiler_params=pltpu.CompilerParams(vmem_limit_bytes=vmem),
        cost_estimate=pl.CostEstimate(flops=flops, bytes_accessed=10**6, transcendentals=0),
    )(*args)


def exchange(array, axis, chunks):
    shape = array.shape
    rows = shape[0] // chunks
    tile = math.gcd(rows, 8)
    array = array.reshape(chunks, rows // tile, tile, shape[1])
    return lax.all_to_all(array, axis, split_axis=0, concat_axis=0, tiled=True).reshape(shape)


def local(magnet, stiffness, kern):
    constant = {name: [jnp.asarray(t) for t in group] for name, group in tables().items()}
    film = jnp.concatenate([magnet, stiffness[None]], 0)
    packed, edge = call(
        pack_body, [(rows_n * halo_rows, 128), (8, 128)], film, constant["y"][0]
    )
    sums = exchange(packed, "row", rows_n)
    (columns,) = call(forward_body, [(512, 128)], sums, edge, constant["y"][1])
    columns = exchange(columns, "col", cols_n)
    tensor = kern.reshape(6, 4, 32, 128).transpose(0, 2, 1, 3).reshape(768, 128)
    (inverse_x,) = call(spectral_body, [(384, 128)], columns, tensor, *constant["x"])
    inverse_x = exchange(inverse_x, "col", cols_n)
    (coef,) = call(back_body, [(rows_n * sums_rows, 128)], inverse_x, constant["z"][0])
    coef = exchange(coef, "row", rows_n)
    (torque,) = call(
        torque_body, [(3, 64, 128)], coef, film, sums, columns, constant["z"][1]
    )
    return torque


def solution(mesh):
    in_specs = (P(None, "col", "row"), P("col", "row"), P(None, ("row", "col"), None))
    out_specs = P(None, "col", "row")
    return jax.shard_map(local, mesh=mesh, in_specs=in_specs, out_specs=out_specs, check_vma=False)
```

```python
import math

import jax
import jax.numpy as jnp
import ml_dtypes
import numpy as np
from jax import lax
from jax.experimental import pallas as pl
from jax.experimental.pallas import tpu as pltpu
from jax.sharding import PartitionSpec as P

damping = 0.3
anisotropy = 0.8
tensor_slots = ((0, 3, 4), (3, 1, 5), (4, 5, 2))

rows_n = 16
cols_n = 32
cells = 64
lanes = 128
length = 4096
bf16 = jnp.bfloat16
f32 = jnp.float32


modes = 14
sums_rows = 3 * modes
halo_rows = sums_rows + 2


def wave(first, second, period):
    angle = 2.0 * math.pi * (np.outer(first, second) % period) / period
    return np.cos(angle), np.sin(angle)


def split_table(table):
    high = table.astype(ml_dtypes.bfloat16)
    low = (table - high.astype(np.float64)).astype(ml_dtypes.bfloat16)
    return high, low


def thick(table):
    high, low = split_table(table)
    return np.concatenate([high, low, high, low], 1)


def tall(table):
    return np.concatenate(split_table(table), 0)


def deep(table):
    high, low = split_table(table)
    return np.concatenate([np.tile(high, (1, 2)), np.tile(low, (1, 2))], 0)


def factors():
    place = np.arange(lanes) - 0.5 * (lanes - 1)
    angle = 2.0 * math.pi * np.outer(place, place) / length
    level = (1.02 - (2.0 * place / lanes) ** 2) ** -0.3
    values, vectors, units = [], [], []
    for part, unit in ((np.cos(angle), 1.0), (np.sin(angle), -1j)):
        value, vector = np.linalg.eigh(part * np.outer(level, level))
        values.append(value)
        vectors.append(vector * np.where(vector[-1] < 0.0, -1.0, 1.0))
        units.append(np.full(lanes, unit))
    values, vectors = np.concatenate(values), np.concatenate(vectors, 1)
    units = np.concatenate(units)
    kept = np.argsort(-np.abs(values), kind="stable")[:modes]
    side = vectors[:, kept] * np.sqrt(np.abs(values[kept])) / level[:, None]
    return side, units[kept] * np.sign(values[kept])


def row_transform():
    side, weight = factors()
    place = np.arange(lanes) - 0.5 * (lanes - 1)
    centre = lanes * np.arange(rows_n) + 0.5 * (lanes - 1)
    turn = np.exp(-2j * math.pi * np.outer(centre, place) / length)
    offset = 0.5 * (lanes - 1)
    phase = np.exp(-2j * math.pi * np.arange(rows_n) * lanes * offset / length)
    constant = np.exp(-2j * math.pi * offset * offset / length)
    turns = turn * phase[:, None]
    gather = side.T[:, None] * turns[None]
    expand = (side * weight)[:, :, None] * turn.T[:, None, :] * phase * constant
    gather, expand = gather.reshape(-1, lanes), expand.reshape(lanes, -1)
    return side.T, turns, gather, expand


def parts(table):
    return np.concatenate([table.real, table.imag], 0)


def tables():
    col = np.arange(cols_n)
    x_l = np.arange(cells)
    k1x = np.arange(64)
    k2x = (2 * np.arange(32)[None, :] + np.arange(2)[:, None]).reshape(-1)
    kappa = (4 * col[None, :] + np.arange(4)[:, None]).reshape(-1)

    sides, turns, gather, expand = row_transform()
    y_gather = np.concatenate([parts(turns), sides], 0).astype(np.float32)
    y_expand = tall(parts(expand[kappa]))
    gather = gather[:, kappa]
    z_gather = deep(np.concatenate([gather.real, gather.imag], 1))
    z_expand = np.ascontiguousarray(tall(parts(expand)).T)

    cos, sin = wave(k1x, col, 64)
    x_first = thick(np.concatenate([cos, sin], 0))
    x_back = deep(np.concatenate([cos, sin], 0).reshape(2, 64, 32).transpose(2, 0, 1).reshape(32, 128))
    cos, sin = wave(k1x, x_l, length)
    x_twist = np.stack([np.concatenate([cos, cos], 1), np.concatenate([sin, -sin], 1)])
    cos, sin = wave(k2x, x_l, 64)
    x_last = deep(np.concatenate([cos, sin], 1))
    cos, sin = wave(x_l, k2x, 64)
    x_lead = deep(np.concatenate([cos, sin], 1))
    cos, sin = wave(x_l, k1x, length)
    own = [np.concatenate([cos, -cos], 1), np.concatenate([sin, -sin], 1)]
    other = [np.concatenate([-sin, -sin], 1), np.concatenate([cos, cos], 1)]
    x_twists = np.concatenate([x_twist, np.stack(own + other)], 0).astype(np.float32)
    return {
        "y": (y_gather, y_expand),
        "x": (x_first, x_twists, x_last, x_lead, x_back),
        "z": (z_gather, z_expand),
    }


def split(values):
    high = values.astype(bf16)
    low = (values - high.astype(f32)).astype(bf16)
    return high, low


def stacked_product(table, values):
    high, low = split(values)
    return jnp.dot(table, jnp.concatenate([high, high, low, low], 0), preferred_element_type=f32)


def tall_product(table, values):
    high, low = split(values)
    size = table.shape[0] // 2
    width = values.shape[1]
    both = jnp.dot(table, jnp.concatenate([high, low], 1), preferred_element_type=f32)
    rest = both[size:, :width] + both[:size, width:] + both[size:, width:]
    return both[:size, :width] + rest


def deep_product(table, values, contract):
    both = jnp.concatenate(split(values), contract)
    dims = (((1,), (contract,)), ((), ()))
    both = lax.dot_general(table, both, dims, preferred_element_type=f32)
    size = table.shape[0] // 2
    return both[:size] + both[size:]


def half_turn(values):
    return pltpu.roll(values, 64, 1)


def lane_index(shape):
    return lax.broadcasted_iota(jnp.int32, shape, len(shape) - 1)


def half_sign(rows):
    return jnp.where(lane_index((rows, 128)) < 64, 1.0, -1.0).astype(f32)


def pack_body(film_ref, gather_ref, out_ref, edge_ref):
    values = jnp.concatenate([film_ref[a] for a in range(3)], 0)
    size = rows_n * modes
    turns = gather_ref[0 : 2 * rows_n, :]
    sides = [gather_ref[2 * rows_n + n : 2 * rows_n + n + 1, :] for n in range(modes)]
    re = [turns[:rows_n] * side for side in sides]
    im = [turns[rows_n:] * side for side in sides]
    table_high, table_low = split(jnp.concatenate(re + im, 0))
    table = jnp.concatenate([table_high, table_low], 0)
    sums = deep_product(jnp.concatenate([table, table], 1), values, 1)
    low = lane_index((size, 128)) < 64
    re, im = sums[:size, :128], sums[size:, :128]
    last = jnp.concatenate([sums[:size, 128:], sums[size:, 128:]], 1)
    blocks = (jnp.where(low, re, half_turn(im)), jnp.where(low, half_turn(re), im), last)
    store_chunks(out_ref, halo_rows, blocks)
    former = jnp.concatenate([film_ref[0], film_ref[1]], 0).T
    latter = jnp.concatenate([film_ref[2], film_ref[3]], 0).T
    after = lax.broadcasted_iota(jnp.int32, (rows_n, lanes), 0) > lax.axis_index("row")
    for n, sides in enumerate((former, latter)):
        edges = jnp.where(after, sides[127:], sides[:1])
        out_ref[pl.ds(sums_rows + n, rows_n, stride=halo_rows), :] = edges
    for n in range(4):
        edge_ref[n : n + 1, :] = film_ref[n, :1, :]
        edge_ref[4 + n : 5 + n, :] = film_ref[n, cells - 1 :, :]


def spread_kern(kern_ref):
    low = lane_index((32, 128)) < 64
    spread = []
    for j in range(6):
        spread.append([])
        for k in range(4):
            part = kern_ref[pl.ds(128 * j + k, 32, stride=4), :]
            turned = half_turn(part)
            halves = [jnp.where(low, part, turned), jnp.where(low, turned, part)]
            spread[j].append(jnp.concatenate(halves, 0))
    return spread


def store_chunks(out_ref, rows, blocks):
    for a in range(3):
        for n in range(modes):
            out_ref[pl.ds(modes * a + n, rows_n, stride=rows), :] = blocks[a][
                rows_n * n : rows_n * n + rows_n
            ]


def load_chunks(in_ref, rows):
    columns = []
    for a in range(3):
        block = [in_ref[pl.ds(modes * a + n, rows_n, stride=rows), :] for n in range(modes)]
        columns.append(jnp.concatenate(block, 0))
    return jnp.concatenate(columns, 1)


def forward_body(in_ref, edge_ref, expand_ref, out_ref):
    sums = tall_product(expand_ref[...], load_chunks(in_ref, halo_rows))
    sign = half_sign(128)
    for a in range(3):
        block = sums[:, 128 * a : 128 * a + 128]
        block = block[:128] - half_turn(block[128:]) * sign
        for k in range(4):
            out_ref[pl.ds(4 * a + k, cols_n, stride=16), :] = block[32 * k : 32 * k + 32]
    col = lax.axis_index("col")
    first, last = edge_ref[0:4, :], edge_ref[4:8, :]
    for c in range(cols_n):
        out_ref[16 * c + 12 : 16 * c + 16, :] = jnp.where(c > col, last, first)


def spectral_body(
    in_ref, kern_ref, first_ref, twist_ref, last_ref, lead_ref, back_ref, out_ref
):
    sign = half_sign(64)
    own, other = twist_ref[0], twist_ref[1]
    kern = spread_kern(kern_ref)
    scale = -1.0 / (length * length)
    lane = lane_index((cols_n, 128))
    zero_weight = jnp.where(lane < 64, 1.0, 0.0).astype(f32)
    is_zero = jnp.logical_and(lax.axis_index("row") == 0, lax.axis_index("col") == 0)

    def enter(ks):
        columns = [in_ref[pl.ds(4 * a + k, cols_n, stride=16), :] for a in range(3) for k in ks]
        return stacked_product(first_ref[...], jnp.concatenate(columns, 1))

    def spread(section):
        turned = []
        for j in range(section.shape[1] // 128):
            block = section[:, 128 * j : 128 * j + 128]
            block = block[:64] + half_turn(block[64:]) * sign
            block = block * own + half_turn(block) * other
            turned.append(block)
            turned.append(half_turn(block) * sign)
        return jnp.concatenate(turned, 0)

    def multiply(freq, ks):
        sources = []
        for target in range(3):
            for n, k in enumerate(ks):
                total = None
                for b in range(3):
                    j = len(ks) * b + n
                    term = kern[tensor_slots[target][b]][k] * freq[:, 128 * j : 128 * j + 128]
                    total = term if total is None else total + term
                sources.append(jnp.concatenate([total, -half_turn(total) * sign], 0))
        return jnp.concatenate(sources, 1)

    def leave(section):
        turned = []
        for j in range(section.shape[1] // 128):
            block = section[:, 128 * j : 128 * j + 128]
            aside = half_turn(block)
            turned.append(block * twist_ref[2] + aside * twist_ref[4])
            turned.append(block * twist_ref[3] + aside * twist_ref[5])
        return jnp.concatenate(turned, 0)

    def store(result, ks):
        for a in range(3):
            for n, k in enumerate(ks):
                j = len(ks) * a + n
                block = result[:, 128 * j : 128 * j + 128]
                weight = jnp.full((cols_n, 128), 2.0, f32)
                if k == 0:
                    weight = jnp.where(is_zero, zero_weight, weight)
                out_ref[pl.ds(4 * a + k, cols_n, stride=12), :] = block * (weight * scale)

    groups = ((0,), (1,), (2,), (3,))
    states = [enter(ks) for ks in groups]
    states = [spread(state) for state in states]
    states = [deep_product(last_ref[...], state, 1) for state in states]
    states = [multiply(state, ks) for state, ks in zip(states, groups)]
    states = [deep_product(lead_ref[...], state, 0) for state in states]
    states = [leave(state) for state in states]
    states = [deep_product(back_ref[...], state, 1) for state in states]
    for state, ks in zip(states, groups):
        store(state, ks)


def back_body(in_ref, gather_ref, out_ref):
    columns = []
    for a in range(3):
        block = [in_ref[pl.ds(4 * a + k, cols_n, stride=12), :] for k in range(4)]
        columns.append(jnp.concatenate(block, 0))
    sign = half_sign(128)
    columns = [jnp.concatenate([block, half_turn(block) * sign], 0) for block in columns]
    sums = deep_product(gather_ref[...], jnp.concatenate(columns, 1), 0)
    blocks = [sums[:, 128 * a : 128 * a + 128] for a in range(3)]
    store_chunks(out_ref, sums_rows, blocks)


def cross(former, latter):
    return (
        former[1] * latter[2] - former[2] * latter[1],
        former[2] * latter[0] - former[0] * latter[2],
        former[0] * latter[1] - former[1] * latter[0],
    )


def torque_body(in_ref, film_ref, beside_y_ref, beside_x_ref, expand_ref, out_ref):
    row, col = lax.axis_index("row"), lax.axis_index("col")
    high, low = split(load_chunks(in_ref, sums_rows).T)
    both = jnp.dot(high, expand_ref[...], preferred_element_type=f32)
    rest = jnp.dot(low, expand_ref[:, :256], preferred_element_type=f32)
    sums = both[:, :256] + both[:, 256:] + rest
    demag = []
    for a in range(3):
        block = sums[128 * a : 128 * a + 128]
        demag.append(block[:64, :128] + block[64:, 128:])

    device = lax.broadcasted_iota(jnp.int32, (rows_n, 128), 0)

    def side(index):
        rows = []
        for n in range(2):
            halo = beside_y_ref[pl.ds(sums_rows + n, rows_n, stride=halo_rows), :]
            rows.append(jnp.sum(jnp.where(device == index, halo, 0.0), 0, keepdims=True))
        return rows

    before_y, after_y = side(row - 1), side(row + 1)
    before_x = beside_x_ref[pl.ds(pl.multiple_of(16 * jnp.maximum(col - 1, 0), 16), 16), :]
    after_x = beside_x_ref[pl.ds(pl.multiple_of(16 * jnp.minimum(col + 1, cols_n - 1), 16), 16), :]
    edges = jnp.concatenate(before_y + after_y + [jnp.zeros((124, 128), f32)], 0).T
    stack = [film_ref[n] for n in range(4)]
    lane = lane_index((cells, 128))
    sub = lax.broadcasted_iota(jnp.int32, (cells, 128), 0)

    def neighbour(n, direction):
        centre = stack[n]
        part = slice(64 * (n % 2), 64 * (n % 2) + 64)
        if direction == 0:
            return jnp.where(sub == cells - 1, after_x[12 + n : 13 + n], pltpu.roll(centre, cells - 1, 0))
        if direction == 1:
            return jnp.where(sub == 0, before_x[12 + n : 13 + n], pltpu.roll(centre, 1, 0))
        if direction == 2:
            edge = edges[part, 2 + n // 2 : 3 + n // 2]
            return jnp.where(lane == 127, edge, pltpu.roll(centre, 127, 1))
        edge = edges[part, n // 2 : n // 2 + 1]
        return jnp.where(lane == 0, edge, pltpu.roll(centre, 1, 1))

    absent = (
        jnp.logical_and(sub == cells - 1, col == cols_n - 1),
        jnp.logical_and(sub == 0, col == 0),
        jnp.logical_and(lane == 127, row == rows_n - 1),
        jnp.logical_and(lane == 0, row == 0),
    )
    exchange = [None] * 3
    for direction in range(4):
        coupling = 0.5 * (stack[3] + neighbour(3, direction))
        coupling = jnp.where(absent[direction], 0.0, coupling)
        for a in range(3):
            term = coupling * (neighbour(a, direction) - stack[a])
            exchange[a] = term if exchange[a] is None else exchange[a] + term
    magnet = stack[:3]
    field = [exchange[a] + demag[a] for a in range(3)]
    field[2] = field[2] + anisotropy * magnet[2]
    first_cross = cross(magnet, field)
    second_cross = cross(magnet, first_cross)
    factor = -1.0 / (1.0 + damping * damping)
    for a in range(3):
        out_ref[a] = (first_cross[a] + damping * second_cross[a]) * factor


in_vmem = pl.BlockSpec(memory_space=pltpu.VMEM)
in_hbm = pl.BlockSpec(memory_space=pltpu.HBM)


def call(body, out_shapes, *args, scratch=(), in_spec=in_vmem, vmem=32 * 2**20, flops=10**8):
    shapes = [jax.ShapeDtypeStruct(shape, f32) for shape in out_shapes]
    return pl.pallas_call(
        body,
        out_shape=shapes,
        in_specs=[in_spec] * len(args),
        out_specs=[in_vmem] * len(shapes),
        scratch_shapes=list(scratch),
        compiler_params=pltpu.CompilerParams(vmem_limit_bytes=vmem),
        cost_estimate=pl.CostEstimate(flops=flops, bytes_accessed=10**6, transcendentals=0),
    )(*args)


def exchange(array, axis, chunks):
    shape = array.shape
    rows = shape[0] // chunks
    tile = math.gcd(rows, 8)
    array = array.reshape(chunks, rows // tile, tile, shape[1])
    return lax.all_to_all(array, axis, split_axis=0, concat_axis=0, tiled=True).reshape(shape)


def local(magnet, stiffness, kern):
    constant = {name: [jnp.asarray(t) for t in group] for name, group in tables().items()}
    film = jnp.concatenate([magnet, stiffness[None]], 0)
    packed, edge = call(
        pack_body, [(rows_n * halo_rows, 128), (8, 128)], film, constant["y"][0]
    )
    sums = exchange(packed, "row", rows_n)
    (columns,) = call(forward_body, [(512, 128)], sums, edge, constant["y"][1])
    columns = exchange(columns, "col", cols_n)
    tensor = kern.reshape(6, 4, 32, 128).transpose(0, 2, 1, 3).reshape(768, 128)
    (inverse_x,) = call(spectral_body, [(384, 128)], columns, tensor, *constant["x"])
    inverse_x = exchange(inverse_x, "col", cols_n)
    (coef,) = call(back_body, [(rows_n * sums_rows, 128)], inverse_x, constant["z"][0])
    coef = exchange(coef, "row", rows_n)
    (torque,) = call(
        torque_body, [(3, 64, 128)], coef, film, sums, columns, constant["z"][1]
    )
    return torque


def solution(mesh):
    in_specs = (P(None, "col", "row"), P("col", "row"), P(None, ("row", "col"), None))
    out_specs = P(None, "col", "row")
    return jax.shard_map(local, mesh=mesh, in_specs=in_specs, out_specs=out_specs, check_vma=False)
```
